512 devices in a mesh: gx: 64 (over y, z_hi, x), gy: 8 (over z_lo, core).
Axes of the slice: x: 4, y: 8, z: 8 (z_hi: 2, z_lo: 4; z = z_hi * 4 + z_lo), core: 2. Of those that a mesh axis runs over, the one named last changes fastest.
Arguments:
- populations: float32 [19, 128, 16, 2048], P(None, 'gx', None, 'gy'), may hold values from 0 to 1
- mass: float32 [128, 16, 2048], P('gx', None, 'gy'), may hold values from 0.05 to 0.95
- flags: int32 [2, 128, 16, 2048], P(None, 'gx', None, 'gy'), may hold values from 0 to 3
- relax: float32 [128, 16, 2048], P('gx', None, 'gy'), may hold values from 0.6 to 1.9
Outputs:
- populations_out: float32 [19, 128, 16, 2048], P(None, 'gx', None, 'gy')
- mass_out: float32 [128, 16, 2048], P('gx', None, 'gy')
The draws below stay inside these ranges and needn't reach their ends.
Inputs may be any that keep to these rules, and one draw needn't show every extreme that they name: `flags`: 0 gas, 1 interface, 2 liquid, 3 wall.
All inputs are finite; a program needn't handle non-finite values.
Results may differ from the reference program's by a relative error of at most 0.0003.
Values sent between devices are 32-bit elements; how exact they have to be, the bound alone decides.
A program may use at most 64 MiB of HBM per device.

```python
import math
import jax
import jax.numpy as jnp
import numpy as np
from jax import lax

NZ = 16
STEPS = 2
NX = 128
NY = 2048


draw_velocity = np.array([(0, 0, 0), (1, 0, 0), (-1, 0, 0), (0, 1, 0), (0, -1, 0), (0, 0, 1), (0, 0, -1), (1, 1, 0), (-1, -1, 0), (1, -1, 0), (-1, 1, 0), (1, 0, 1), (-1, 0, -1), (1, 0, -1), (-1, 0, 1), (0, 1, 1), (0, -1, -1), (0, 1, -1), (0, -1, 1)], np.float32)


draw_weight = np.array([1.0 / 3.0] + [1.0 / 18.0] * 6 + [1.0 / 36.0] * 12, np.float32)


def draw_populations(key, part):
    key = jax.random.fold_in(key, 1)
    key_rho, key_mom, key_noise = jax.random.split(key, 3)
    density = 1.0 + 0.1 * jax.random.truncated_normal(key_rho, -3.0, 3.0, (NX, NZ, NY), jnp.float32)
    noise = 0.15 * jax.random.truncated_normal(key_noise, -3.0, 3.0, (19, NX, NZ, NY), jnp.float32)
    momentum = 0.03 * jax.random.truncated_normal(key_mom, -3.0, 3.0, (3, NX, NZ, NY), jnp.float32)
    velocity = jnp.asarray(draw_velocity)
    projected = velocity[:, 0, None, None, None] * momentum[0] + velocity[:, 1, None, None, None] * momentum[1] + velocity[:, 2, None, None, None] * momentum[2]
    square = momentum[0] * momentum[0] + momentum[1] * momentum[1] + momentum[2] * momentum[2]
    weights = jnp.asarray(draw_weight)[:, None, None, None]
    base = weights * (density + 3.0 * projected + 4.5 * projected * projected - 1.5 * square)
    return (base * (1.0 + noise)).astype(jnp.float32)


def set_ends(entries, key, low, high):
    extent = entries.shape
    spot = [jax.random.randint(jax.random.fold_in(key, axis), (), 0, extent[axis]) for axis in range(len(extent))]
    entries = entries.at[tuple(spot)].set(low)
    longest = extent.index(max(extent))
    spot[longest] = (spot[longest] + 1) % extent[longest]
    return entries.at[tuple(spot)].set(high)


def levels(rng, dims, pieces, smallest, top_value):
    level, own = 1.0, jax.random.fold_in(rng, 6)
    for position, blocks in pieces:
        heights = jnp.exp(jax.random.uniform(jax.random.fold_in(own, position), (blocks,), jnp.float32, smallest / len(pieces), top_value / len(pieces)))
        level = level * jnp.repeat(heights, dims[position] // blocks).reshape([-1 if axis == position else 1 for axis in range(len(dims))])
    return level


def setup_inputs(seed: int = 0) -> dict:
    key_list = jax.random.split(jax.random.key(seed), 5)
    populations = draw_populations(jax.random.fold_in(key_list[4], 71), 0)
    mass = jnp.clip(0.05 + 0.9 * jax.random.uniform(key_list[1], (NX, NZ, NY), jnp.float32) ** levels(key_list[1], (NX, NZ, NY), ((0, 64), (2, 8)), -0.2, 0.2), 0.05, 0.95)
    flags = set_ends(jax.random.randint(key_list[2], (STEPS, NX, NZ, NY), 0, 4), jax.random.fold_in(key_list[2], 1), 0, 3).astype(jnp.int32)
    relax = jnp.clip(jnp.exp(math.log(1.9) - 1.1526795 * jax.random.uniform(key_list[3], (NX, NZ, NY), jnp.float32) ** levels(key_list[3], (NX, NZ, NY), ((0, 64), (2, 8)), -0.2, 0.2)), 0.6, 1.9)
    return {"populations": populations, "mass": mass, "flags": flags, "relax": relax}


lattice_list = [(0, 0, 0), (1, 0, 0), (-1, 0, 0), (0, 1, 0), (0, -1, 0), (0, 0, 1), (0, 0, -1),
                (1, 1, 0), (-1, -1, 0), (1, -1, 0), (-1, 1, 0), (1, 0, 1), (-1, 0, -1), (1, 0, -1),
                (-1, 0, 1), (0, 1, 1), (0, -1, -1), (0, 1, -1), (0, -1, 1)]
opposite_index = [0, 2, 1, 4, 3, 6, 5, 8, 7, 10, 9, 12, 11, 14, 13, 16, 15, 18, 17]
lattice_weight = np.array([1.0 / 3.0] + [1.0 / 18.0] * 6 + [1.0 / 36.0] * 12, np.float32)
lattice_vel = np.array(lattice_list, np.float32)
pair_table = np.stack([lattice_vel[:, 0] ** 2, lattice_vel[:, 1] ** 2, lattice_vel[:, 2] ** 2,
                       2 * lattice_vel[:, 0] * lattice_vel[:, 1], 2 * lattice_vel[:, 0] * lattice_vel[:, 2],
                       2 * lattice_vel[:, 1] * lattice_vel[:, 2]], 1).astype(np.float32)
surface_sigma = 0.02
highest = lax.Precision.HIGHEST


def advance(extended, mass, kinds, relax):
    width_x = extended.shape[1] - 2
    depth = extended.shape[2]
    width_y = extended.shape[3] - 2
    padded = jnp.pad(extended, ((0, 0), (0, 0), (1, 1), (0, 0)))
    edge_plane = jnp.zeros(padded.shape[1:], jnp.float32).at[:, 0].set(-1.0).at[:, -1].set(-1.0)
    padded = padded.at[19].add(edge_plane)
    pops = extended[:19, 1:-1, :, 1:-1]
    source_pop = []
    source_code = []
    for index in range(19):
        shift_x, shift_y, shift_z = lattice_list[index]
        source_pop.append(padded[index, 1 - shift_x:1 - shift_x + width_x, 1 - shift_z:1 - shift_z + depth, 1 - shift_y:1 - shift_y + width_y])
        source_code.append(padded[19, 1 - shift_x:1 - shift_x + width_x, 1 - shift_z:1 - shift_z + depth, 1 - shift_y:1 - shift_y + width_y])
    source_pop = jnp.stack(source_pop)
    source_code = jnp.stack(source_code)
    reverse = jnp.stack([pops[other] for other in opposite_index])
    weights = jnp.asarray(lattice_weight)[:, None, None, None]
    velocity = jnp.asarray(lattice_vel)
    is_face = kinds == 1
    is_liquid = kinds == 2
    is_fluid = is_face | is_liquid
    momentum_old = jnp.tensordot(velocity.T, pops, axes=1, precision=highest)
    own_frac = jnp.where(is_liquid, 1.0, jnp.where(is_face, mass, 0.0))
    near_frac = jnp.where(source_code == 1.0, 1.0, jnp.where(source_code > 1.5, source_code - 2.0, 0.0))
    laplace = jnp.sum(near_frac[1:7], 0) - 6.0 * own_frac
    gas_density = 1.0 - 3.0 * surface_sigma * laplace
    proj_old = jnp.tensordot(velocity, momentum_old, axes=1, precision=highest)
    square_old = jnp.sum(momentum_old * momentum_old, 0)
    rebuilt = 2.0 * weights * (gas_density + 4.5 * proj_old * proj_old - 1.5 * square_old) - reverse
    incoming = jnp.where(source_code == -1.0, reverse, jnp.where(source_code == 0.0, rebuilt, source_pop))
    share = jnp.where(source_code == 1.0, 1.0, jnp.where(source_code > 1.5, 0.5 * (mass + (source_code - 2.0)), 0.0))
    moved_mass = jnp.sum((share * (source_pop - reverse))[1:], 0)
    density = jnp.sum(incoming, 0)
    mass_new = jnp.where(is_face, mass + moved_mass, jnp.where(is_liquid, density, 0.0))
    momentum = jnp.tensordot(velocity.T, incoming, axes=1, precision=highest)
    projected = jnp.tensordot(velocity, momentum, axes=1, precision=highest)
    square = jnp.sum(momentum * momentum, 0)
    equilibrium = weights * (density + 3.0 * projected + 4.5 * projected * projected - 1.5 * square)
    stress = jnp.tensordot(jnp.asarray(pair_table).T, incoming - equilibrium, axes=1, precision=highest)
    trace_part = stress[0] + stress[1] + stress[2]
    contraction = jnp.tensordot(jnp.asarray(pair_table), stress, axes=1, precision=highest) - trace_part / 3.0
    collided = equilibrium + (1.0 - relax) * 4.5 * weights * contraction
    pops_new = jnp.where(is_fluid, collided, weights * jnp.ones_like(collided))
    return pops_new, mass_new


def cell_code(mass, kinds):
    return jnp.where(kinds == 3, -1.0, jnp.where(kinds == 0, 0.0, jnp.where(kinds == 2, 1.0, 2.0 + mass))).astype(jnp.float32)


def reference(populations, mass, flags, relax):
    pops = populations
    fill = mass
    for step in range(STEPS):
        kinds = flags[step]
        stacked = jnp.concatenate([pops, cell_code(fill, kinds)[None]], 0)
        extended = jnp.pad(stacked, ((0, 0), (1, 1), (0, 0), (1, 1)), mode="wrap")
        pops, fill = advance(extended, fill, kinds, relax)
    return pops, fill
```

```python
import jax
import jax.numpy as jnp
from jax import lax
from jax.experimental import pallas as pl
from jax.experimental.pallas import tpu as pltpu
from jax.sharding import PartitionSpec as P

MESH = pl.DeviceIdType.MESH

VEL = [
    (0, 0, 0),
    (1, 0, 0),
    (-1, 0, 0),
    (0, 1, 0),
    (0, -1, 0),
    (0, 0, 1),
    (0, 0, -1),
    (1, 1, 0),
    (-1, -1, 0),
    (1, -1, 0),
    (-1, 1, 0),
    (1, 0, 1),
    (-1, 0, -1),
    (1, 0, -1),
    (-1, 0, 1),
    (0, 1, 1),
    (0, -1, -1),
    (0, 1, -1),
    (0, -1, 1),
]
INDEX = {c: q for q, c in enumerate(VEL)}
OPP = [INDEX[(-a, -b, -c)] for a, b, c in VEL]
W0, W1, W2 = 1.0 / 3.0, 1.0 / 18.0, 1.0 / 36.0
WEIGHT = [W0] + [W1] * 6 + [W2] * 12
SIGMA = 0.02
OFFS = [(0, 0), (1, 0), (-1, 0), (0, 1), (0, -1)]
LANES = 128


def side_dirs(cx):
    return [INDEX[(cx, b, c)] for b, c in OFFS]


def y_columns(cy):
    cols = []
    for plane in (0, 1):
        for cz in (0, 1, -1):
            cols.append((INDEX[(0, cy, cz)], plane))
        cols.append((INDEX[(1 - 2 * plane, cy, 0)], plane))
        cols.append((None, plane))
    return cols


def frac_of(e):
    return jnp.where(e == 1.0, 1.0, jnp.where(e > 1.5, e - 2.0, 0.0))


def code_of(kind, mass):
    return jnp.where(kind == 3, -1.0, jnp.where(kind == 0, 0.0, jnp.where(kind == 2, 1.0, 2.0 + mass)))


def half(h):
    return slice(h * LANES, (h + 1) * LANES)


def shift_y(halves, cy, column):
    lane = lax.broadcasted_iota(jnp.int32, halves[0].shape, 1)
    if cy == 1:
        moved = [pltpu.roll(a, 1, 1) for a in halves]
        edge = lane == 0
        return [jnp.where(edge, column, moved[0]), jnp.where(edge, moved[0], moved[1])]
    moved = [pltpu.roll(a, LANES - 1, 1) for a in halves]
    edge = lane == LANES - 1
    return [jnp.where(edge, moved[1], moved[0]), jnp.where(edge, column, moved[1])]


def shift_z(halves, cz):
    depth = halves[0].shape[0]
    return [pltpu.roll(a, cz % depth, 0) for a in halves]


def wall_z(halves, cz):
    row = lax.broadcasted_iota(jnp.int32, halves[0].shape, 0)
    outside = row == (0 if cz == 1 else halves[0].shape[0] - 1)
    return [jnp.where(outside, -1.0, a) for a in shift_z(halves, cz)]


def spread(tile, k):
    return jnp.broadcast_to(tile[:, k : k + 1], tile.shape)


def pack(columns):
    lane = lax.broadcasted_iota(jnp.int32, (columns[0].shape[0], LANES), 1)
    tile = jnp.zeros(lane.shape, jnp.float32)
    for k, column in enumerate(columns):
        tile = jnp.where(lane == k, jnp.broadcast_to(column, lane.shape), tile)
    return tile


def kernel(
    pops_in,
    mass_in,
    flags_in,
    relax_in,
    pops_out,
    mass_out,
    pops,
    mass,
    flags,
    relax,
    code,
    src,
    near,
    far,
    part,
    sx,
    rx,
    sc,
    rc,
    sy,
    ry,
    sk,
    rk,
    load_sem,
    sx_sem,
    rx_sem,
    sc_sem,
    rc_sem,
    sy_sem,
    ry_sem,
    sk_sem,
    rk_sem,
):
    nx, ny = lax.axis_size("gx"), lax.axis_size("gy")
    gx, gy = lax.axis_index("gx"), lax.axis_index("gy")
    left, right = lax.rem(gx + nx - 1, nx), lax.rem(gx + 1, nx)
    down, up = lax.rem(gy + ny - 1, ny), lax.rem(gy + 1, ny)
    side_id = [(left, gy), (right, gy)]
    y_id = [(gx, down), (gx, up)]
    corner_id = [[(left, down), (left, up)], [(right, down), (right, up)]]

    loads = [
        pltpu.make_async_copy(mass_in, mass.at[0], load_sem.at[0]),
        pltpu.make_async_copy(flags_in, flags, load_sem.at[1]),
        pltpu.make_async_copy(pops_in, pops.at[0], load_sem.at[2]),
        pltpu.make_async_copy(relax_in, relax, load_sem.at[3]),
    ]
    for load in loads:
        load.start()
    barrier = pltpu.get_barrier_semaphore()
    for other in side_id + y_id + corner_id[0] + corner_id[1]:
        pl.semaphore_signal(barrier, inc=1, device_id=other, device_id_type=MESH)

    def send_code(t, d):
        return pltpu.make_async_remote_copy(
            sc.at[t, d], rc.at[t, 1 - d], sc_sem.at[t, d], rc_sem.at[t, 1 - d], device_id=side_id[d], device_id_type=MESH
        )

    def send_pops(t, d, h):
        return pltpu.make_async_remote_copy(
            sx.at[t, d, h],
            rx.at[t, 1 - d, h],
            sx_sem.at[t, d, h],
            rx_sem.at[t, 1 - d, h],
            device_id=side_id[d],
            device_id_type=MESH,
        )

    def send_y(t, u):
        return pltpu.make_async_remote_copy(
            sy.at[t, u], ry.at[t, 1 - u], sy_sem.at[t, u], ry_sem.at[t, 1 - u], device_id=y_id[u], device_id_type=MESH
        )

    def send_corner(t, d, u):
        return pltpu.make_async_remote_copy(
            sk.at[t, d, u],
            rk.at[t, 1 - d, 1 - u],
            sk_sem.at[t, d, u],
            rk_sem.at[t, 1 - d, 1 - u],
            device_id=corner_id[d][u],
            device_id_type=MESH,
        )

    def plane_of(t, q, p):
        return [pops[t, q, p, :, half(h)] for h in (0, 1)]

    def rim(t, q, p, u):
        at = 0 if u == 0 else 2 * LANES - 1
        if q is None:
            return code[t, p, :, at : at + 1]
        return pops[t, q, p, :, at : at + 1]

    def fill_y(t):
        for u in (0, 1):
            sy[t, u] = pack([rim(t, q, p, u) for q, p in y_columns(2 * u - 1)])

    def fill_corner(t, d):
        for u in (0, 1):
            q = INDEX[(2 * d - 1, 2 * u - 1, 0)]
            sk[t, d, u] = pack([rim(t, q, d, u), rim(t, None, d, u)])

    loads[0].wait()
    loads[1].wait()
    for p in (0, 1):
        code[0, p] = code_of(flags[0, p], mass[0, p])
        sc[0, p] = code[0, p]
    loads[2].wait()
    for d in (0, 1):
        fill_corner(0, d)
        for k, q in enumerate(side_dirs(2 * d - 1)):
            cy, cz = OFFS[k]
            halves = plane_of(0, q, d)
            if cy:
                halves = shift_y(halves, cy, halves[0])
            if cz:
                halves = shift_z(halves, cz)
            for h in (0, 1):
                sx[0, d, h, k] = halves[h]
    fill_y(0)
    loads[3].wait()

    pl.semaphore_wait(barrier, 8)
    for d in (0, 1):
        send_code(0, d).start()
    for h in (0, 1):
        for d in (0, 1):
            send_pops(0, d, h).start()
    for d in (0, 1):
        for u in (0, 1):
            send_corner(0, d, u).start()
    for u in (0, 1):
        send_y(0, u).start()

    def stream(t):
        cols = [ry[t, 0], ry[t, 1]]
        place = [{c: k for k, c in enumerate(y_columns(cy))} for cy in (1, -1)]

        def column(q, p, cy):
            u = 0 if cy == 1 else 1
            return spread(cols[u], place[u][(q, p)])

        for p in (0, 1):
            own = [code[t, p, :, half(h)] for h in (0, 1)]
            table = {(0, 0): own}
            for cy in (1, -1):
                table[(cy, 0)] = shift_y(own, cy, column(None, p, cy))
            for cy in (0, 1, -1):
                for cz in (1, -1):
                    table[(cy, cz)] = wall_z(table[(cy, 0)], cz)
            for (cy, cz), halves in table.items():
                for h in (0, 1):
                    near[p, cy + 1, cz + 1, :, half(h)] = halves[h]
            for q, (cx, cy, cz) in enumerate(VEL):
                if q == 0 or not 0 <= p + cx <= 1:
                    continue
                halves = plane_of(t, q, p)
                if cy:
                    halves = shift_y(halves, cy, column(q, p, cy))
                if cz:
                    halves = shift_z(halves, cz)
                for h in (0, 1):
                    src[p + cx, q, :, half(h)] = halves[h]

    def far_codes(t, d):
        own = [rc[t, d, :, half(h)] for h in (0, 1)]
        for k, (cy, cz) in enumerate(OFFS):
            halves = own
            if cy:
                halves = shift_y(own, cy, spread(rk[t, d, 0 if cy == 1 else 1], 1))
            if cz:
                halves = wall_z(own, cz)
            for h in (0, 1):
                far[d, k, :, half(h)] = halves[h]

    def far_sources(t, d, h):
        if t == 0:
            out = [rx[t, d, h, k] for k in range(5)]
            lane = lax.broadcasted_iota(jnp.int32, out[0].shape, 1)
            k, edge, u = (1, lane == 0, 0) if h == 0 else (2, lane == LANES - 1, 1)
            out[k] = jnp.where(edge, spread(rk[t, d, u], 0), out[k])
            return out
        out = []
        for k, (cy, cz) in enumerate(OFFS):
            halves = [rx[t, d, 0, k], rx[t, d, 1, k]]
            if cy:
                halves = shift_y(halves, cy, spread(rk[t, d, 0 if cy == 1 else 1], 0))
            if cz:
                halves = shift_z(halves, cz)
            out.append(halves[h])
        return out

    def arrive(e, s, r, rebuilt, m):
        g = jnp.where(e == -1.0, r, jnp.where(e == 0.0, rebuilt - r, s))
        a = jnp.where(e == 1.0, 1.0, jnp.where(e > 1.5, 0.5 * (m + (e - 2.0)), 0.0))
        return g, a * (s - r)

    def side_moments(cx, g):
        total = (g[0] + g[1]) + (g[2] + (g[3] + g[4]))
        dy, dz, sy2, sz2 = g[1] - g[2], g[3] - g[4], g[1] + g[2], g[3] + g[4]
        if cx == 1:
            return [total, total, dy, dz, total, sy2, sz2, dy, dz]
        return [total, -total, dy, dz, total, sy2, sz2, -dy, -dz]

    def interior(t, p, h):
        ys = half(h)
        kind, m = flags[t, p, :, ys], mass[t, p, :, ys]
        f = [pops[t, q, p, :, ys] for q in range(19)]
        j0 = []
        for axis in range(3):
            plus = [f[q] for q in range(19) if VEL[q][axis] == 1]
            minus = [f[q] for q in range(19) if VEL[q][axis] == -1]
            j0.append(sum(a - b for a, b in zip(plus, minus)))
        own = jnp.where(kind == 2, 1.0, jnp.where(kind == 1, m, 0.0))
        x_far = far[p, 0, :, ys]
        x_near = near[1 - p, 1, 1, :, ys]
        around = frac_of(x_far) + frac_of(x_near)
        for cy, cz in OFFS[1:]:
            around = around + frac_of(near[p, cy + 1, cz + 1, :, ys])
        gas = 1.0 - 3.0 * SIGMA * (around - 6.0 * own)
        lift = 2.0 * gas - 3.0 * (j0[0] * j0[0] + j0[1] * j0[1] + j0[2] * j0[2])

        def rebuilt(q):
            along = [c * j for c, j in zip(VEL[q], j0) if c]
            proj = None
            for c, j in zip(VEL[q], j0):
                if c:
                    term = j if c == 1 else -j
                    proj = term if proj is None else proj + term
            return WEIGHT[q] * (lift + 9.0 * (proj * proj) if along else lift)

        dm = jnp.zeros_like(m)
        g = {}
        e0 = near[p, 1, 1, :, ys]
        g[0] = jnp.where(e0 == 0.0, rebuilt(0) - f[0], f[0])
        for q, (cx, cy, cz) in enumerate(VEL):
            if q == 0 or not 0 <= p - cx <= 1:
                continue
            e = near[p - cx, cy + 1, cz + 1, :, ys]
            g[q], moved = arrive(e, src[p, q, :, ys], f[OPP[q]], rebuilt(q), m)
            dm = dm + moved
        cx = 1 if p == 1 else -1
        total, jx, jy, jz, pxx, pyy, pzz, pxy, pxz = side_moments(cx, [g[q] for q in side_dirs(cx)])
        pp, mm, pm, mp = (g[INDEX[(0, b, c)]] for b, c in ((1, 1), (-1, -1), (1, -1), (-1, 1)))
        diag, anti = pp + mm, pm + mp
        yy, zz = g[3] + g[4], g[5] + g[6]
        rho = total + g[0] + yy + zz + (diag + anti)
        jy = jy + (g[3] - g[4]) + (pp - mm) + (pm - mp)
        jz = jz + (g[5] - g[6]) + (pp - mm) - (pm - mp)
        pyy = pyy + yy + (diag + anti)
        pzz = pzz + zz + (diag + anti)
        pyz = diag - anti
        for k, value in enumerate((rho, jx, jy, jz, pxx, pyy, pzz, pxy, pxz, pyz, dm, lift, *j0)):
            part[p, k, :, ys] = value

    def finish(t, p, h):
        ys = half(h)
        cx = 1 if p == 0 else -1
        kind, m = flags[t, p, :, ys], mass[t, p, :, ys]
        rho, jx, jy, jz, pxx, pyy, pzz, pxy, pxz, pyz, dm, lift, ax, ay, az = (part[p, k, :, ys] for k in range(15))
        sources = far_sources(t, p, h)
        g = []
        for k, q in enumerate(side_dirs(cx)):
            cy, cz = OFFS[k]
            proj = ax if cx == 1 else -ax
            if cy:
                proj = proj + (ay if cy == 1 else -ay)
            if cz:
                proj = proj + (az if cz == 1 else -az)
            rebuilt = WEIGHT[q] * (lift + 9.0 * (proj * proj))
            value, moved = arrive(far[p, k, :, ys], sources[k], pops[t, OPP[q], p, :, ys], rebuilt, m)
            g.append(value)
            dm = dm + moved
        more = side_moments(cx, g)
        rho, jx, jy, jz, pxx, pyy, pzz, pxy, pxz = (
            a + b for a, b in zip((rho, jx, jy, jz, pxx, pyy, pzz, pxy, pxz), more)
        )
        is_face, is_liquid = kind == 1, kind == 2
        mass_new = jnp.where(is_face, m + dm, jnp.where(is_liquid, rho, 0.0))
        fluid = is_face | is_liquid
        third = rho * (1.0 / 3.0)
        xx, yy, zz = jx * jx, jy * jy, jz * jz
        strength = (1.0 - relax[p, :, ys]) * 4.5
        qxx, qyy, qzz = pxx - third - xx, pyy - third - yy, pzz - third - zz
        mean = (qxx + qyy + qzz) * (1.0 / 3.0)
        qxx, qyy, qzz, mean = strength * qxx, strength * qyy, strength * qzz, strength * mean
        four = 4.0 * strength
        qxy, qxz, qyz = four * (pxy - jx * jy), four * (pxz - jx * jz), four * (pyz - jy * jz)
        base = rho - 1.5 * (xx + yy + zz) - mean
        new = {0: W0 * base}

        def couple(q, proj, stress):
            w = WEIGHT[q]
            even = w * (base + 4.5 * (proj * proj) + stress)
            odd = (3.0 * w) * proj
            new[q], new[OPP[q]] = even + odd, even - odd

        couple(1, jx, qxx)
        couple(3, jy, qyy)
        couple(5, jz, qzz)
        couple(INDEX[(1, 1, 0)], jx + jy, qxx + qyy + qxy)
        couple(INDEX[(1, -1, 0)], jx - jy, qxx + qyy - qxy)
        couple(INDEX[(1, 0, 1)], jx + jz, qxx + qzz + qxz)
        couple(INDEX[(1, 0, -1)], jx - jz, qxx + qzz - qxz)
        couple(INDEX[(0, 1, 1)], jy + jz, qyy + qzz + qyz)
        couple(INDEX[(0, 1, -1)], jy - jz, qyy + qzz - qyz)
        new = [jnp.where(fluid, new[q], WEIGHT[q]) for q in range(19)]
        if t == 1:
            mass_out[p, :, ys] = mass_new
            for q in range(19):
                pops_out[q, p, :, ys] = new[q]
            return
        for k, q in enumerate(side_dirs(2 * p - 1)):
            sx[1, p, h, k] = new[q]
        code_new = code_of(flags[1, p, :, ys], mass_new)
        sc[1, p, :, ys] = code_new
        code[1, p, :, ys] = code_new
        mass[1, p, :, ys] = mass_new
        for q in range(19):
            pops[1, q, p, :, ys] = new[q]

    for t in (0, 1):
        for u in (0, 1):
            send_y(t, u).wait_recv()
        stream(t)
        for d in (0, 1):
            send_code(t, 1 - d).wait_recv()
            for u in (0, 1):
                send_corner(t, 1 - d, u).wait_recv()
            far_codes(t, d)
        for p in (0, 1):
            for h in (0, 1):
                interior(t, p, h)
        for p in (0, 1):
            if t == 1:
                for h in (0, 1):
                    send_pops(t, 1 - p, h).wait_recv()
            for h in (0, 1):
                if t == 0:
                    send_pops(t, 1 - p, h).wait_recv()
                finish(t, p, h)
                if t == 0:
                    if h == 1:
                        send_code(1, p).start()
                    send_pops(1, p, h).start()
            if t == 0:
                fill_corner(1, p)
                for u in (0, 1):
                    send_corner(1, p, u).start()
        if t == 0:
            fill_y(1)
            for u in (0, 1):
                send_y(1, u).start()

    for t in (0, 1):
        for d in (0, 1):
            send_code(t, d).wait_send()
            for h in (0, 1):
                send_pops(t, d, h).wait_send()
                send_corner(t, d, h).wait_send()
            send_y(t, d).wait_send()


def on_device(populations, mass, flags, relax):
    _, planes, depth, width = populations.shape
    tile, plane = (depth, LANES), (depth, width)
    f32 = jnp.float32
    vmem, dma = pltpu.VMEM, pltpu.SemaphoreType.DMA
    hbm = pl.BlockSpec(memory_space=pltpu.HBM)
    here = pl.BlockSpec(memory_space=pltpu.VMEM)
    return pl.pallas_call(
        kernel,
        out_shape=(
            jax.ShapeDtypeStruct(populations.shape, f32),
            jax.ShapeDtypeStruct(mass.shape, f32),
        ),
        in_specs=[hbm] * 4,
        out_specs=(here, here),
        scratch_shapes=[
            vmem((2, 19, planes, *plane), f32),
            vmem((2, planes, *plane), f32),
            vmem((2, planes, *plane), jnp.int32),
            vmem((planes, *plane), f32),
            vmem((2, planes, *plane), f32),
            vmem((planes, 19, *plane), f32),
            vmem((planes, 3, 3, *plane), f32),
            vmem((2, 5, *plane), f32),
            vmem((planes, 15, *plane), f32),
            vmem((2, 2, 2, 5, *tile), f32),
            vmem((2, 2, 2, 5, *tile), f32),
            vmem((2, 2, *plane), f32),
            vmem((2, 2, *plane), f32),
            vmem((2, 2, *tile), f32),
            vmem((2, 2, *tile), f32),
            vmem((2, 2, 2, *tile), f32),
            vmem((2, 2, 2, *tile), f32),
            dma((4,)),
            dma((2, 2, 2)),
            dma((2, 2, 2)),
            dma((2, 2)),
            dma((2, 2)),
            dma((2, 2)),
            dma((2, 2)),
            dma((2, 2, 2)),
            dma((2, 2, 2)),
        ],
        compiler_params=pltpu.CompilerParams(
            collective_id=0, has_side_effects=True, vmem_limit_bytes=32 * 1024 * 1024
        ),
        name="lattice_steps",
    )(populations, mass, flags, relax)


def solution(mesh):
    return jax.shard_map(
        on_device,
        mesh=mesh,
        in_specs=(
            P(None, "gx", None, "gy"),
            P("gx", None, "gy"),
            P(None, "gx", None, "gy"),
            P("gx", None, "gy"),
        ),
        out_specs=(P(None, "gx", None, "gy"), P("gx", None, "gy")),
        check_vma=False,
    )
```

```python
import jax
import jax.numpy as jnp
from jax import lax
from jax.experimental import pallas as pl
from jax.experimental.pallas import tpu as pltpu
from jax.sharding import PartitionSpec as P

MESH = pl.DeviceIdType.MESH

VEL = [
    (0, 0, 0),
    (1, 0, 0),
    (-1, 0, 0),
    (0, 1, 0),
    (0, -1, 0),
    (0, 0, 1),
    (0, 0, -1),
    (1, 1, 0),
    (-1, -1, 0),
    (1, -1, 0),
    (-1, 1, 0),
    (1, 0, 1),
    (-1, 0, -1),
    (1, 0, -1),
    (-1, 0, 1),
    (0, 1, 1),
    (0, -1, -1),
    (0, 1, -1),
    (0, -1, 1),
]
INDEX = {c: q for q, c in enumerate(VEL)}
OPP = [INDEX[(-a, -b, -c)] for a, b, c in VEL]
W0, W1, W2 = 1.0 / 3.0, 1.0 / 18.0, 1.0 / 36.0
WEIGHT = [W0] + [W1] * 6 + [W2] * 12
SIGMA = 0.02
OFFS = [(0, 0), (1, 0), (-1, 0), (0, 1), (0, -1)]
LANES = 128


def side_dirs(cx):
    return [INDEX[(cx, b, c)] for b, c in OFFS]


def y_columns(cy):
    cols = []
    for plane in (0, 1):
        for cz in (0, 1, -1):
            cols.append((INDEX[(0, cy, cz)], plane))
        cols.append((INDEX[(1 - 2 * plane, cy, 0)], plane))
        cols.append((None, plane))
    return cols


def frac_of(e):
    return jnp.where(e == 1.0, 1.0, jnp.where(e > 1.5, e - 2.0, 0.0))


def code_of(kind, mass):
    return jnp.where(kind == 3, -1.0, jnp.where(kind == 0, 0.0, jnp.where(kind == 2, 1.0, 2.0 + mass)))


def half(h):
    return slice(h * LANES, (h + 1) * LANES)


def shift_y(halves, cy, column):
    lane = lax.broadcasted_iota(jnp.int32, halves[0].shape, 1)
    if cy == 1:
        moved = [pltpu.roll(a, 1, 1) for a in halves]
        edge = lane == 0
        return [jnp.where(edge, column, moved[0]), jnp.where(edge, moved[0], moved[1])]
    moved = [pltpu.roll(a, LANES - 1, 1) for a in halves]
    edge = lane == LANES - 1
    return [jnp.where(edge, moved[1], moved[0]), jnp.where(edge, column, moved[1])]


def shift_z(halves, cz):
    depth = halves[0].shape[0]
    return [pltpu.roll(a, cz % depth, 0) for a in halves]


def wall_z(halves, cz):
    row = lax.broadcasted_iota(jnp.int32, halves[0].shape, 0)
    outside = row == (0 if cz == 1 else halves[0].shape[0] - 1)
    return [jnp.where(outside, -1.0, a) for a in shift_z(halves, cz)]


def spread(tile, k):
    return jnp.broadcast_to(tile[:, k : k + 1], tile.shape)


def pack(columns):
    lane = lax.broadcasted_iota(jnp.int32, (columns[0].shape[0], LANES), 1)
    tile = jnp.zeros(lane.shape, jnp.float32)
    for k, column in enumerate(columns):
        tile = jnp.where(lane == k, jnp.broadcast_to(column, lane.shape), tile)
    return tile


def kernel(
    pops_in,
    mass_in,
    flags_in,
    relax_in,
    pops_out,
    mass_out,
    pops,
    mass,
    flags,
    relax,
    code,
    src,
    near,
    far,
    part,
    sx,
    rx,
    sc,
    rc,
    sy,
    ry,
    sk,
    rk,
    load_sem,
    sx_sem,
    rx_sem,
    sc_sem,
    rc_sem,
    sy_sem,
    ry_sem,
    sk_sem,
    rk_sem,
):
    nx, ny = lax.axis_size("gx"), lax.axis_size("gy")
    gx, gy = lax.axis_index("gx"), lax.axis_index("gy")
    left, right = lax.rem(gx + nx - 1, nx), lax.rem(gx + 1, nx)
    down, up = lax.rem(gy + ny - 1, ny), lax.rem(gy + 1, ny)
    side_id = [(left, gy), (right, gy)]
    y_id = [(gx, down), (gx, up)]
    corner_id = [[(left, down), (left, up)], [(right, down), (right, up)]]

    barrier = pltpu.get_barrier_semaphore()
    for other in side_id + y_id + corner_id[0] + corner_id[1]:
        pl.semaphore_signal(barrier, inc=1, device_id=other, device_id_type=MESH)
    loads = [
        pltpu.make_async_copy(mass_in, mass.at[0], load_sem.at[0]),
        pltpu.make_async_copy(flags_in, flags, load_sem.at[1]),
        pltpu.make_async_copy(pops_in, pops.at[0], load_sem.at[2]),
        pltpu.make_async_copy(relax_in, relax, load_sem.at[3]),
    ]
    for load in loads:
        load.start()

    def send_code(t, d):
        return pltpu.make_async_remote_copy(
            sc.at[t, d], rc.at[t, 1 - d], sc_sem.at[t, d], rc_sem.at[t, 1 - d], device_id=side_id[d], device_id_type=MESH
        )

    def send_pops(t, d, h):
        return pltpu.make_async_remote_copy(
            sx.at[t, d, h],
            rx.at[t, 1 - d, h],
            sx_sem.at[t, d, h],
            rx_sem.at[t, 1 - d, h],
            device_id=side_id[d],
            device_id_type=MESH,
        )

    def send_y(t, u):
        return pltpu.make_async_remote_copy(
            sy.at[t, u], ry.at[t, 1 - u], sy_sem.at[t, u], ry_sem.at[t, 1 - u], device_id=y_id[u], device_id_type=MESH
        )

    def send_corner(t, d, u):
        return pltpu.make_async_remote_copy(
            sk.at[t, d, u],
            rk.at[t, 1 - d, 1 - u],
            sk_sem.at[t, d, u],
            rk_sem.at[t, 1 - d, 1 - u],
            device_id=corner_id[d][u],
            device_id_type=MESH,
        )

    def plane_of(t, q, p):
        return [pops[t, q, p, :, half(h)] for h in (0, 1)]

    def rim(t, q, p, u):
        at = 0 if u == 0 else 2 * LANES - 1
        if q is None:
            return code[t, p, :, at : at + 1]
        return pops[t, q, p, :, at : at + 1]

    def fill_y(t):
        for u in (0, 1):
            sy[t, u] = pack([rim(t, q, p, u) for q, p in y_columns(2 * u - 1)])

    def fill_corner(t, d):
        for u in (0, 1):
            q = INDEX[(2 * d - 1, 2 * u - 1, 0)]
            sk[t, d, u] = pack([rim(t, q, d, u), rim(t, None, d, u)])

    loads[0].wait()
    loads[1].wait()
    for p in (0, 1):
        code[0, p] = code_of(flags[0, p], mass[0, p])
        sc[0, p] = code[0, p]
    loads[2].wait()
    for d in (0, 1):
        fill_corner(0, d)
        for k, q in enumerate(side_dirs(2 * d - 1)):
            cy, cz = OFFS[k]
            halves = plane_of(0, q, d)
            if cy:
                halves = shift_y(halves, cy, halves[0])
            if cz:
                halves = shift_z(halves, cz)
            for h in (0, 1):
                sx[0, d, h, k] = halves[h]
    fill_y(0)
    loads[3].wait()

    pl.semaphore_wait(barrier, 8)
    for d in (0, 1):
        send_code(0, d).start()
    for h in (0, 1):
        for d in (0, 1):
            send_pops(0, d, h).start()
    for d in (0, 1):
        for u in (0, 1):
            send_corner(0, d, u).start()
    for u in (0, 1):
        send_y(0, u).start()

    def stream(t):
        cols = [ry[t, 0], ry[t, 1]]
        place = [{c: k for k, c in enumerate(y_columns(cy))} for cy in (1, -1)]

        def column(q, p, cy):
            u = 0 if cy == 1 else 1
            return spread(cols[u], place[u][(q, p)])

        for p in (0, 1):
            own = [code[t, p, :, half(h)] for h in (0, 1)]
            table = {(0, 0): own}
            for cy in (1, -1):
                table[(cy, 0)] = shift_y(own, cy, column(None, p, cy))
            for cy in (0, 1, -1):
                for cz in (1, -1):
                    table[(cy, cz)] = wall_z(table[(cy, 0)], cz)
            for (cy, cz), halves in table.items():
                for h in (0, 1):
                    near[p, cy + 1, cz + 1, :, half(h)] = halves[h]
            for q, (cx, cy, cz) in enumerate(VEL):
                if q == 0 or not 0 <= p + cx <= 1:
                    continue
                halves = plane_of(t, q, p)
                if cy:
                    halves = shift_y(halves, cy, column(q, p, cy))
                if cz:
                    halves = shift_z(halves, cz)
                for h in (0, 1):
                    src[p + cx, q, :, half(h)] = halves[h]

    def far_codes(t, d):
        own = [rc[t, d, :, half(h)] for h in (0, 1)]
        for k, (cy, cz) in enumerate(OFFS):
            halves = own
            if cy:
                halves = shift_y(own, cy, spread(rk[t, d, 0 if cy == 1 else 1], 1))
            if cz:
                halves = wall_z(own, cz)
            for h in (0, 1):
                far[d, k, :, half(h)] = halves[h]

    def far_sources(t, d, h):
        if t == 0:
            out = [rx[t, d, h, k] for k in range(5)]
            lane = lax.broadcasted_iota(jnp.int32, out[0].shape, 1)
            k, edge, u = (1, lane == 0, 0) if h == 0 else (2, lane == LANES - 1, 1)
            out[k] = jnp.where(edge, spread(rk[t, d, u], 0), out[k])
            return out
        out = []
        for k, (cy, cz) in enumerate(OFFS):
            halves = [rx[t, d, 0, k], rx[t, d, 1, k]]
            if cy:
                halves = shift_y(halves, cy, spread(rk[t, d, 0 if cy == 1 else 1], 0))
            if cz:
                halves = shift_z(halves, cz)
            out.append(halves[h])
        return out

    def arrive(e, s, r, rebuilt, m):
        g = jnp.where(e == -1.0, r, jnp.where(e == 0.0, rebuilt - r, s))
        a = jnp.where(e == 1.0, 1.0, jnp.where(e > 1.5, 0.5 * (m + (e - 2.0)), 0.0))
        return g, a * (s - r)

    def side_moments(cx, g):
        total = (g[0] + g[1]) + (g[2] + (g[3] + g[4]))
        dy, dz, sy2, sz2 = g[1] - g[2], g[3] - g[4], g[1] + g[2], g[3] + g[4]
        if cx == 1:
            return [total, total, dy, dz, total, sy2, sz2, dy, dz]
        return [total, -total, dy, dz, total, sy2, sz2, -dy, -dz]

    def interior(t, p, h):
        ys = half(h)
        kind, m = flags[t, p, :, ys], mass[t, p, :, ys]
        f = [pops[t, q, p, :, ys] for q in range(19)]
        j0 = []
        for axis in range(3):
            plus = [f[q] for q in range(19) if VEL[q][axis] == 1]
            minus = [f[q] for q in range(19) if VEL[q][axis] == -1]
            j0.append(sum(a - b for a, b in zip(plus, minus)))
        own = jnp.where(kind == 2, 1.0, jnp.where(kind == 1, m, 0.0))
        x_far = far[p, 0, :, ys]
        x_near = near[1 - p, 1, 1, :, ys]
        around = frac_of(x_far) + frac_of(x_near)
        for cy, cz in OFFS[1:]:
            around = around + frac_of(near[p, cy + 1, cz + 1, :, ys])
        gas = 1.0 - 3.0 * SIGMA * (around - 6.0 * own)
        lift = 2.0 * gas - 3.0 * (j0[0] * j0[0] + j0[1] * j0[1] + j0[2] * j0[2])

        def rebuilt(q):
            along = [c * j for c, j in zip(VEL[q], j0) if c]
            proj = None
            for c, j in zip(VEL[q], j0):
                if c:
                    term = j if c == 1 else -j
                    proj = term if proj is None else proj + term
            return WEIGHT[q] * (lift + 9.0 * (proj * proj) if along else lift)

        dm = jnp.zeros_like(m)
        g = {}
        e0 = near[p, 1, 1, :, ys]
        g[0] = jnp.where(e0 == 0.0, rebuilt(0) - f[0], f[0])
        for q, (cx, cy, cz) in enumerate(VEL):
            if q == 0 or not 0 <= p - cx <= 1:
                continue
            e = near[p - cx, cy + 1, cz + 1, :, ys]
            g[q], moved = arrive(e, src[p, q, :, ys], f[OPP[q]], rebuilt(q), m)
            dm = dm + moved
        cx = 1 if p == 1 else -1
        total, jx, jy, jz, pxx, pyy, pzz, pxy, pxz = side_moments(cx, [g[q] for q in side_dirs(cx)])
        pp, mm, pm, mp = (g[INDEX[(0, b, c)]] for b, c in ((1, 1), (-1, -1), (1, -1), (-1, 1)))
        diag, anti = pp + mm, pm + mp
        yy, zz = g[3] + g[4], g[5] + g[6]
        rho = total + g[0] + yy + zz + (diag + anti)
        jy = jy + (g[3] - g[4]) + (pp - mm) + (pm - mp)
        jz = jz + (g[5] - g[6]) + (pp - mm) - (pm - mp)
        pyy = pyy + yy + (diag + anti)
        pzz = pzz + zz + (diag + anti)
        pyz = diag - anti
        for k, value in enumerate((rho, jx, jy, jz, pxx, pyy, pzz, pxy, pxz, pyz, dm, lift, *j0)):
            part[p, k, :, ys] = value

    def finish(t, p, h):
        ys = half(h)
        cx = 1 if p == 0 else -1
        kind, m = flags[t, p, :, ys], mass[t, p, :, ys]
        rho, jx, jy, jz, pxx, pyy, pzz, pxy, pxz, pyz, dm, lift, ax, ay, az = (part[p, k, :, ys] for k in range(15))
        sources = far_sources(t, p, h)
        g = []
        for k, q in enumerate(side_dirs(cx)):
            cy, cz = OFFS[k]
            proj = ax if cx == 1 else -ax
            if cy:
                proj = proj + (ay if cy == 1 else -ay)
            if cz:
                proj = proj + (az if cz == 1 else -az)
            rebuilt = WEIGHT[q] * (lift + 9.0 * (proj * proj))
            value, moved = arrive(far[p, k, :, ys], sources[k], pops[t, OPP[q], p, :, ys], rebuilt, m)
            g.append(value)
            dm = dm + moved
        more = side_moments(cx, g)
        rho, jx, jy, jz, pxx, pyy, pzz, pxy, pxz = (
            a + b for a, b in zip((rho, jx, jy, jz, pxx, pyy, pzz, pxy, pxz), more)
        )
        is_face, is_liquid = kind == 1, kind == 2
        mass_new = jnp.where(is_face, m + dm, jnp.where(is_liquid, rho, 0.0))
        fluid = is_face | is_liquid
        third = rho * (1.0 / 3.0)
        xx, yy, zz = jx * jx, jy * jy, jz * jz
        strength = (1.0 - relax[p, :, ys]) * 4.5
        qxx, qyy, qzz = pxx - third - xx, pyy - third - yy, pzz - third - zz
        mean = (qxx + qyy + qzz) * (1.0 / 3.0)
        qxx, qyy, qzz, mean = strength * qxx, strength * qyy, strength * qzz, strength * mean
        four = 4.0 * strength
        qxy, qxz, qyz = four * (pxy - jx * jy), four * (pxz - jx * jz), four * (pyz - jy * jz)
        base = rho - 1.5 * (xx + yy + zz) - mean
        new = {0: W0 * base}

        def couple(q, proj, stress):
            w = WEIGHT[q]
            even = w * (base + 4.5 * (proj * proj) + stress)
            odd = (3.0 * w) * proj
            new[q], new[OPP[q]] = even + odd, even - odd

        couple(1, jx, qxx)
        couple(3, jy, qyy)
        couple(5, jz, qzz)
        couple(INDEX[(1, 1, 0)], jx + jy, qxx + qyy + qxy)
        couple(INDEX[(1, -1, 0)], jx - jy, qxx + qyy - qxy)
        couple(INDEX[(1, 0, 1)], jx + jz, qxx + qzz + qxz)
        couple(INDEX[(1, 0, -1)], jx - jz, qxx + qzz - qxz)
        couple(INDEX[(0, 1, 1)], jy + jz, qyy + qzz + qyz)
        couple(INDEX[(0, 1, -1)], jy - jz, qyy + qzz - qyz)
        new = [jnp.where(fluid, new[q], WEIGHT[q]) for q in range(19)]
        if t == 1:
            mass_out[p, :, ys] = mass_new
            for q in range(19):
                pops_out[q, p, :, ys] = new[q]
            return
        for k, q in enumerate(side_dirs(2 * p - 1)):
            sx[1, p, h, k] = new[q]
        code_new = code_of(flags[1, p, :, ys], mass_new)
        sc[1, p, :, ys] = code_new
        code[1, p, :, ys] = code_new
        mass[1, p, :, ys] = mass_new
        for q in range(19):
            pops[1, q, p, :, ys] = new[q]

    for t in (0, 1):
        for u in (0, 1):
            send_y(t, u).wait_recv()
        stream(t)
        for d in (0, 1):
            send_code(t, 1 - d).wait_recv()
            for u in (0, 1):
                send_corner(t, 1 - d, u).wait_recv()
            far_codes(t, d)
        for p in (0, 1):
            for h in (0, 1):
                interior(t, p, h)
        for p in (0, 1):
            if t == 1:
                for h in (0, 1):
                    send_pops(t, 1 - p, h).wait_recv()
            for h in (0, 1):
                if t == 0:
                    send_pops(t, 1 - p, h).wait_recv()
                finish(t, p, h)
                if t == 0:
                    if h == 1:
                        send_code(1, p).start()
                    send_pops(1, p, h).start()
            if t == 0:
                fill_corner(1, p)
                for u in (0, 1):
                    send_corner(1, p, u).start()
        if t == 0:
            fill_y(1)
            for u in (0, 1):
                send_y(1, u).start()

    for t in (0, 1):
        for d in (0, 1):
            send_code(t, d).wait_send()
            for h in (0, 1):
                send_pops(t, d, h).wait_send()
                send_corner(t, d, h).wait_send()
            send_y(t, d).wait_send()


def write_back(pops, mass, pops_out, mass_out, sem):
    copies = [
        pltpu.make_async_copy(pops, pops_out, sem.at[0]),
        pltpu.make_async_copy(mass, mass_out, sem.at[1]),
    ]
    for copy in copies:
        copy.start()
    for copy in copies:
        copy.wait()


def on_device(populations, mass, flags, relax):
    _, planes, depth, width = populations.shape
    tile, plane = (depth, LANES), (depth, width)
    f32 = jnp.float32
    vmem, dma = pltpu.VMEM, pltpu.SemaphoreType.DMA
    state_shape = (
        jax.ShapeDtypeStruct(populations.shape, f32),
        jax.ShapeDtypeStruct(mass.shape, f32),
    )
    hbm = pl.BlockSpec(memory_space=pltpu.HBM)
    here = pl.BlockSpec(memory_space=pltpu.VMEM)
    args = [pltpu.with_memory_space_constraint(a, pltpu.HBM) for a in (populations, mass, flags, relax)]
    state = pl.pallas_call(
        kernel,
        out_shape=state_shape,
        in_specs=[hbm] * 4,
        out_specs=(here, here),
        scratch_shapes=[
            vmem((2, 19, planes, *plane), f32),
            vmem((2, planes, *plane), f32),
            vmem((2, planes, *plane), jnp.int32),
            vmem((planes, *plane), f32),
            vmem((2, planes, *plane), f32),
            vmem((planes, 19, *plane), f32),
            vmem((planes, 3, 3, *plane), f32),
            vmem((2, 5, *plane), f32),
            vmem((planes, 15, *plane), f32),
            vmem((2, 2, 2, 5, *tile), f32),
            vmem((2, 2, 2, 5, *tile), f32),
            vmem((2, 2, *plane), f32),
            vmem((2, 2, *plane), f32),
            vmem((2, 2, *tile), f32),
            vmem((2, 2, *tile), f32),
            vmem((2, 2, 2, *tile), f32),
            vmem((2, 2, 2, *tile), f32),
            dma((4,)),
            dma((2, 2, 2)),
            dma((2, 2, 2)),
            dma((2, 2)),
            dma((2, 2)),
            dma((2, 2)),
            dma((2, 2)),
            dma((2, 2, 2)),
            dma((2, 2, 2)),
        ],
        compiler_params=pltpu.CompilerParams(
            collective_id=0, has_side_effects=True, vmem_limit_bytes=32 * 1024 * 1024
        ),
        name="lattice_steps",
    )(*args)
    anywhere = pl.BlockSpec(memory_space=pl.ANY)
    return pl.pallas_call(
        write_back,
        out_shape=state_shape,
        in_specs=[here] * 2,
        out_specs=(anywhere,) * 2,
        scratch_shapes=[dma((2,))],
        name="write_back",
    )(*(pltpu.with_memory_space_constraint(a, pltpu.VMEM) for a in state))


def solution(mesh):
    return jax.shard_map(
        on_device,
        mesh=mesh,
        in_specs=(
            P(None, "gx", None, "gy"),
            P("gx", None, "gy"),
            P(None, "gx", None, "gy"),
            P("gx", None, "gy"),
        ),
        out_specs=(P(None, "gx", None, "gy"), P("gx", None, "gy")),
        check_vma=False,
    )
```

```python
import jax
import jax.numpy as jnp
from jax import lax
from jax.experimental import pallas as pl
from jax.experimental.pallas import tpu as pltpu
from jax.sharding import PartitionSpec as P

MESH = pl.DeviceIdType.MESH

VEL = [
    (0, 0, 0),
    (1, 0, 0),
    (-1, 0, 0),
    (0, 1, 0),
    (0, -1, 0),
    (0, 0, 1),
    (0, 0, -1),
    (1, 1, 0),
    (-1, -1, 0),
    (1, -1, 0),
    (-1, 1, 0),
    (1, 0, 1),
    (-1, 0, -1),
    (1, 0, -1),
    (-1, 0, 1),
    (0, 1, 1),
    (0, -1, -1),
    (0, 1, -1),
    (0, -1, 1),
]
INDEX = {c: q for q, c in enumerate(VEL)}
OPP = [INDEX[(-a, -b, -c)] for a, b, c in VEL]
W0, W1, W2 = 1.0 / 3.0, 1.0 / 18.0, 1.0 / 36.0
WEIGHT = [W0] + [W1] * 6 + [W2] * 12
SIGMA = 0.02
OFFS = [(0, 0), (1, 0), (-1, 0), (0, 1), (0, -1)]
IN_PLANE = [(1, 0), (-1, 0), (0, 1), (0, -1), (1, 1), (-1, -1), (1, -1), (-1, 1)]
LANES = 128
ROWS = 8


OPP_OFFS = [0, 2, 1, 4, 3]
CHUNKS = [(zh, h) for h in (0, 1) for zh in (0, 1)]


def side_dirs(cx):
    return [INDEX[(cx, b, c)] for b, c in OFFS]


def y_columns(cy):
    cols = []
    for plane in (0, 1):
        for cz in (0, 1, -1):
            cols.append((INDEX[(0, cy, cz)], plane))
        cols.append((INDEX[(1 - 2 * plane, cy, 0)], plane))
        cols.append((None, plane))
    return cols


def frac_of(e):
    return jnp.where(e == 1.0, 1.0, jnp.where(e > 1.5, e - 2.0, 0.0))


def code_of(kind, mass):
    return jnp.where(kind == 3, -1.0, jnp.where(kind == 0, 0.0, jnp.where(kind == 2, 1.0, 2.0 + mass)))


def half(h):
    return slice(h * LANES, (h + 1) * LANES)


def shift_y(halves, cy, column):
    lane = lax.broadcasted_iota(jnp.int32, halves[0].shape, 1)
    if cy == 1:
        moved = [pltpu.roll(a, 1, 1) for a in halves]
        edge = lane == 0
        return [jnp.where(edge, column, moved[0]), jnp.where(edge, moved[0], moved[1])]
    moved = [pltpu.roll(a, LANES - 1, 1) for a in halves]
    edge = lane == LANES - 1
    return [jnp.where(edge, moved[1], moved[0]), jnp.where(edge, column, moved[1])]


def shift_z(halves, cz):
    depth = halves[0].shape[0]
    return [pltpu.roll(a, cz % depth, 0) for a in halves]


def wall_z(halves, cz):
    row = lax.broadcasted_iota(jnp.int32, halves[0].shape, 0)
    outside = row == (0 if cz == 1 else halves[0].shape[0] - 1)
    return [jnp.where(outside, -1.0, a) for a in shift_z(halves, cz)]


def rows(z):
    return slice(z * ROWS, (z + 1) * ROWS)


def spread(tile, k):
    low, high = tile[:, 2 * k : 2 * k + 1], tile[:, 2 * k + 1 : 2 * k + 2]
    return jnp.concatenate([jnp.broadcast_to(low, tile.shape), jnp.broadcast_to(high, tile.shape)], axis=0)


def pack(columns):
    lane = lax.broadcasted_iota(jnp.int32, (ROWS, LANES), 1)
    tile = jnp.zeros(lane.shape, jnp.float32)
    for k, column in enumerate(columns):
        for z in (0, 1):
            tile = jnp.where(lane == 2 * k + z, jnp.broadcast_to(column[rows(z)], lane.shape), tile)
    return tile


def kernel(
    pops_in,
    mass_in,
    flags_in,
    relax_in,
    pops_out,
    mass_out,
    pops,
    mass,
    flags,
    relax,
    code,
    inner,
    cross,
    near,
    far,
    part,
    sx,
    rx,
    sc,
    rc,
    sy,
    ry,
    sk,
    rk,
    load_sem,
    sx_sem,
    rx_sem,
    sc_sem,
    rc_sem,
    sy_sem,
    ry_sem,
    sk_sem,
    rk_sem,
):
    nx, ny = lax.axis_size("gx"), lax.axis_size("gy")
    gx, gy = lax.axis_index("gx"), lax.axis_index("gy")
    ys = [lax.rem(gy + ny - 1, ny), gy, lax.rem(gy + 1, ny)]
    sides = [lax.rem(gx, 2), lax.rem(gx + 1, 2)]

    def device(d, u):
        return (lax.rem(gx + 2 * d - 1 + nx, nx), ys[u + 1])

    barrier = pltpu.get_barrier_semaphore()
    for d in sides:
        for u in (0, -1, 1):
            pl.semaphore_signal(barrier, inc=1, device_id=device(d, u), device_id_type=MESH)
    for u in (-1, 1):
        pl.semaphore_signal(barrier, inc=1, device_id=(gx, ys[u + 1]), device_id_type=MESH)
    loads = [
        pltpu.make_async_copy(mass_in, mass.at[0], load_sem.at[0]),
        pltpu.make_async_copy(flags_in, flags, load_sem.at[1]),
        pltpu.make_async_copy(pops_in, pops.at[0], load_sem.at[2]),
        pltpu.make_async_copy(relax_in, relax, load_sem.at[3]),
    ]
    for load in loads:
        load.start()

    def x_code(d, at):
        return pltpu.make_async_remote_copy(
            sc.at[d], rc.at[at], sc_sem.at[d], rc_sem.at[at], device_id=device(d, 0), device_id_type=MESH
        )

    def x_chunk(t, d, c, at):
        count = pl.ds(0, 5 + t)
        return pltpu.make_async_remote_copy(
            sx.at[t, d, c, count],
            rx.at[t, at, c, count],
            sx_sem.at[t, d, c],
            rx_sem.at[t, at, c],
            device_id=device(d, 0),
            device_id_type=MESH,
        )

    def x_corner(t, d, u, at):
        return pltpu.make_async_remote_copy(
            sk.at[t, d, u],
            rk.at[t, at[0], at[1]],
            sk_sem.at[t, d, u],
            rk_sem.at[t, at[0], at[1]],
            device_id=device(d, 2 * u - 1),
            device_id_type=MESH,
        )

    def y_tile(t, u, at):
        return pltpu.make_async_remote_copy(
            sy.at[t, u], ry.at[t, at], sy_sem.at[t, u], ry_sem.at[t, at], device_id=(gx, ys[2 * u]), device_id_type=MESH
        )

    def pick(pair, p):
        return pair[0] + p * (pair[1] - pair[0])

    plus, minus = side_dirs(1), side_dirs(-1)
    inward = list(zip(plus, minus))
    outward = list(zip(minus, plus))

    def rim_of(t, q, p, u):
        at = 0 if u == 0 else 2 * LANES - 1
        if q is None:
            return code[t, p, :, at : at + 1]
        return pops[t, q, p, :, at : at + 1]

    def fill_y(t):
        for u in (0, 1):
            sy[t, u] = pack([rim_of(t, q, p, u) for q, p in y_columns(2 * u - 1)])

    def fill_corner(t, p):
        for u in (0, 1):
            q = pick(outward[2 - u], p)
            sk[t, p, u] = pack([rim_of(t, q, p, u), rim_of(t, None, p, u)])

    loads[0].wait()
    loads[1].wait()
    for p in (0, 1):
        code[0, p] = code_of(flags[0, p], mass[0, p])
        sc[p] = code[0, p]
    loads[2].wait()
    for p in (0, 1):
        fill_corner(0, p)
        for k, (cy, cz) in enumerate(OFFS):
            halves = [pops[0, outward[k][p], p, :, half(h)] for h in (0, 1)]
            if cy:
                halves = shift_y(halves, cy, halves[0])
            if cz:
                halves = shift_z(halves, cz)
            for c, (z, h) in enumerate(CHUNKS):
                sx[0, p, c, k] = halves[h][rows(z)]
    fill_y(0)
    loads[3].wait()

    pl.semaphore_wait(barrier, 8)
    for i, d in enumerate(sides):
        for u in (0, 1):
            x_corner(0, d, u, (1 - d, 1 - u)).start()
        x_code(d, 1 - d).start()
        for c in range(4):
            x_chunk(0, d, c, 1 - d).start()
        if i == 0:
            for u in (0, 1):
                y_tile(0, u, 1 - u).start()

    def stream(t):
        place = [{c: k for k, c in enumerate(y_columns(cy))} for cy in (1, -1)]

        def column(q, p, cy):
            u = 0 if cy == 1 else 1
            return spread(ry[t, u], place[u][(q, p)])

        def moved(q, p, cy, cz):
            halves = [pops[t, q, p, :, half(h)] for h in (0, 1)]
            if cy:
                halves = shift_y(halves, cy, column(q, p, cy))
            if cz:
                halves = shift_z(halves, cz)
            return halves

        for p in (0, 1):
            own = [code[t, p, :, half(h)] for h in (0, 1)]
            table = {(0, 0): own}
            for cy in (1, -1):
                table[(cy, 0)] = shift_y(own, cy, column(None, p, cy))
            for cy in (0, 1, -1):
                for cz in (1, -1):
                    table[(cy, cz)] = wall_z(table[(cy, 0)], cz)
            for (cy, cz), halves in table.items():
                for h in (0, 1):
                    near[p, cy + 1, cz + 1, :, half(h)] = halves[h]
            for k, (cy, cz) in enumerate(IN_PLANE):
                halves = moved(INDEX[(0, cy, cz)], p, cy, cz)
                for h in (0, 1):
                    inner[p, k, :, half(h)] = halves[h]
            for k, (cy, cz) in enumerate(OFFS):
                halves = moved(outward[k][p], 1 - p, cy, cz)
                for h in (0, 1):
                    cross[p, k, :, half(h)] = halves[h]

    def plane_code(t, p):
        if t == 0:
            return [rc[p, :, half(h)] for h in (0, 1)]
        return [jnp.concatenate([rx[1, p, 2 * h, 5], rx[1, p, 2 * h + 1, 5]], axis=0) for h in (0, 1)]

    def far_codes(t, p):
        own = plane_code(t, p)
        for k, (cy, cz) in enumerate(OFFS):
            halves = own
            if cy:
                halves = shift_y(own, cy, spread(rk[t, p, 0 if cy == 1 else 1], 1))
            if cz:
                halves = wall_z(own, cz)
            for h in (0, 1):
                far[p, k, :, half(h)] = halves[h]

    def arrive(e, s, r, rebuilt, m):
        g = jnp.where(e == -1.0, r, jnp.where(e == 0.0, rebuilt - r, s))
        a = jnp.where(e == 1.0, 1.0, jnp.where(e > 1.5, 0.5 * (m + (e - 2.0)), 0.0))
        return g, a * (s - r)

    def side_moments(g):
        total = (g[0] + g[1]) + (g[2] + (g[3] + g[4]))
        return [total, g[1] - g[2], g[3] - g[4], g[1] + g[2], g[3] + g[4]]

    def interior(t, p, h, x_far):
        lanes = half(h)
        kind, m = flags[t, p, :, lanes], mass[t, p, :, lanes]
        rest = pops[t, 0, p, :, lanes]
        flat = [pops[t, INDEX[(0, cy, cz)], p, :, lanes] for cy, cz in IN_PLANE]
        fin = [pops[t, pick(inward[k], p), p, :, lanes] for k in range(5)]
        fout = [pops[t, pick(outward[k], p), p, :, lanes] for k in range(5)]
        tin, yin, zin, _, _ = side_moments(fin)
        tout, yout, zout, _, _ = side_moments(fout)
        pp, mm, pm, mp = flat[4:]
        ax = tin - tout
        ay = (yin + yout) + (flat[0] - flat[1]) + (pp - mm) + (pm - mp)
        az = (zin + zout) + (flat[2] - flat[3]) + (pp - mm) - (pm - mp)
        own = jnp.where(kind == 2, 1.0, jnp.where(kind == 1, m, 0.0))
        around = frac_of(x_far) + frac_of(near[1 - p, 1, 1, :, lanes])
        for cy, cz in OFFS[1:]:
            around = around + frac_of(near[p, cy + 1, cz + 1, :, lanes])
        gas = 1.0 - 3.0 * SIGMA * (around - 6.0 * own)
        lift = 2.0 * gas - 3.0 * (ax * ax + ay * ay + az * az)

        dm = jnp.zeros_like(m)
        e0 = near[p, 1, 1, :, lanes]
        g0 = jnp.where(e0 == 0.0, W0 * lift - rest, rest)
        g = []
        for k, (cy, cz) in enumerate(IN_PLANE):
            proj = sum(c * j for c, j in ((cy, ay), (cz, az)) if c)
            w = W2 if cy and cz else W1
            value, moved = arrive(
                near[p, cy + 1, cz + 1, :, lanes],
                inner[p, k, :, lanes],
                flat[k ^ 1],
                w * (lift + 9.0 * (proj * proj)),
                m,
            )
            g.append(value)
            dm = dm + moved
        out = []
        for k, (cy, cz) in enumerate(OFFS):
            proj = -ax + sum(c * j for c, j in ((cy, ay), (cz, az)) if c)
            w = W2 if cy or cz else W1
            value, moved = arrive(
                near[1 - p, cy + 1, cz + 1, :, lanes],
                cross[p, k, :, lanes],
                fin[OPP_OFFS[k]],
                w * (lift + 9.0 * (proj * proj)),
                m,
            )
            out.append(value)
            dm = dm + moved
        total, dy, dz, yy2, zz2 = side_moments(out)
        pp, mm, pm, mp = g[4:]
        diag, anti = pp + mm, pm + mp
        yy, zz = g[0] + g[1], g[2] + g[3]
        rho = total + g0 + yy + zz + (diag + anti)
        jy = dy + (g[0] - g[1]) + (pp - mm) + (pm - mp)
        jz = dz + (g[2] - g[3]) + (pp - mm) - (pm - mp)
        pyy = yy2 + yy + (diag + anti)
        pzz = zz2 + zz + (diag + anti)
        kept = (rho, total, jy, jz, pyy, pzz, dy, dz, diag - anti, dm, lift, ax, ay, az)
        for k, value in enumerate(kept):
            part[p, k, :, lanes] = value

    def finish(t, p, z, lanes, sources):
        kind, m = flags[t, p, z, lanes], mass[t, p, z, lanes]
        rho, tout, jy, jz, pyy, pzz, dyout, dzout, pyz, dm, lift, ax, ay, az = (
            part[p, k, z, lanes] for k in range(14)
        )
        g = []
        for k, (cy, cz) in enumerate(OFFS):
            proj = ax + sum(c * j for c, j in ((cy, ay), (cz, az)) if c)
            w = W2 if cy or cz else W1
            value, moved = arrive(
                far[p, k, z, lanes],
                sources[k],
                pops[t, pick(outward[OPP_OFFS[k]], p), p, z, lanes],
                w * (lift + 9.0 * (proj * proj)),
                m,
            )
            g.append(value)
            dm = dm + moved
        total, dy, dz, yy2, zz2 = side_moments(g)
        rho, jx, pxx = rho + total, total - tout, total + tout
        jy, jz, pyy, pzz = jy + dy, jz + dz, pyy + yy2, pzz + zz2
        pxy, pxz = dy - dyout, dz - dzout
        is_face, is_liquid = kind == 1, kind == 2
        mass_new = jnp.where(is_face, m + dm, jnp.where(is_liquid, rho, 0.0))
        fluid = is_face | is_liquid
        third = rho * (1.0 / 3.0)
        xx, yy, zz = jx * jx, jy * jy, jz * jz
        strength = (1.0 - relax[p, z, lanes]) * 4.5
        qxx, qyy, qzz = pxx - third - xx, pyy - third - yy, pzz - third - zz
        mean = (qxx + qyy + qzz) * (1.0 / 3.0)
        qxx, qyy, qzz, mean = strength * qxx, strength * qyy, strength * qzz, strength * mean
        four = 4.0 * strength
        qxy, qxz, qyz = four * (pxy - jx * jy), four * (pxz - jx * jz), four * (pyz - jy * jz)
        base = rho - 1.5 * (xx + yy + zz) - mean

        def couple(w, proj, stress):
            even = w * (base + 4.5 * (proj * proj) + stress)
            odd = (3.0 * w) * proj
            return jnp.where(fluid, even + odd, w), jnp.where(fluid, even - odd, w)

        new_in, new_out = [None] * 5, [None] * 5
        new_in[0], new_out[0] = couple(W1, jx, qxx)
        new_in[1], new_out[2] = couple(W2, jx + jy, qxx + qyy + qxy)
        new_in[2], new_out[1] = couple(W2, jx - jy, qxx + qyy - qxy)
        new_in[3], new_out[4] = couple(W2, jx + jz, qxx + qzz + qxz)
        new_in[4], new_out[3] = couple(W2, jx - jz, qxx + qzz - qxz)
        flat = [
            *couple(W1, jy, qyy),
            *couple(W1, jz, qzz),
            *couple(W2, jy + jz, qyy + qzz + qyz),
            *couple(W2, jy - jz, qyy + qzz - qyz),
        ]
        new = [(0, jnp.where(fluid, W0 * base, W0))]
        new += [(INDEX[(0, cy, cz)], flat[k]) for k, (cy, cz) in enumerate(IN_PLANE)]
        new += [(pick(inward[k], p), new_in[k]) for k in range(5)]
        new += [(pick(outward[k], p), new_out[k]) for k in range(5)]
        return mass_new, new, new_out

    def close(t, p):
        for u in (0, 1):
            x_corner(t, p, u, (p, u)).wait_recv()
        if t == 0:
            x_code(p, p).wait_recv()
            far_codes(0, p)
            for h in (0, 1):
                interior(0, p, h, far[p, 0, :, half(h)])
            for c, (z, h) in enumerate(CHUNKS):
                x_chunk(0, p, c, p).wait_recv()
                sources = [rx[0, p, c, k] for k in range(5)]
                lane = lax.broadcasted_iota(jnp.int32, sources[0].shape, 1)
                k, edge, u = (1, lane == 0, 0) if h == 0 else (2, lane == LANES - 1, 1)
                column = jnp.broadcast_to(rk[0, p, u][:, z : z + 1], lane.shape)
                sources[k] = jnp.where(edge, column, sources[k])
                z, lanes = rows(z), half(h)
                mass_new, new, new_out = finish(0, p, z, lanes, sources)
                code_new = code_of(flags[1, p, z, lanes], mass_new)
                for k in range(5):
                    sx[1, p, c, k] = new_out[k]
                sx[1, p, c, 5] = code_new
                x_chunk(1, p, c, 1 - p).start()
                code[1, p, z, lanes] = code_new
                mass[1, p, z, lanes] = mass_new
                for q, value in new:
                    pops[1, q, p, z, lanes] = value
            fill_corner(1, p)
            for u in (0, 1):
                x_corner(1, p, u, (1 - p, 1 - u)).start()
            return
        for h in (0, 1):
            for z in (0, 1):
                x_chunk(1, p, 2 * h + z, p).wait_recv()
            interior(1, p, h, jnp.concatenate([rx[1, p, 2 * h, 5], rx[1, p, 2 * h + 1, 5]], axis=0))
        far_codes(1, p)
        beyond = []
        for k, (cy, cz) in enumerate(OFFS):
            halves = [jnp.concatenate([rx[1, p, 2 * h, k], rx[1, p, 2 * h + 1, k]], axis=0) for h in (0, 1)]
            if cy:
                halves = shift_y(halves, cy, spread(rk[1, p, 0 if cy == 1 else 1], 0))
            if cz:
                halves = shift_z(halves, cz)
            beyond.append(halves)
        for h in (0, 1):
            lanes = half(h)
            mass_new, new, _ = finish(1, p, slice(None), lanes, [halves[h] for halves in beyond])
            mass_out[p, :, lanes] = mass_new
            for q, value in new:
                pops_out[q, p, :, lanes] = value

    for t in (0, 1):
        for u in (0, 1):
            y_tile(t, u, u).wait_recv()
        stream(t)

        @pl.loop(0, 2)
        def _(i, t=t):
            close(t, lax.rem(gx + 1 + i, 2))

        if t == 0:
            fill_y(1)
            for u in (0, 1):
                y_tile(1, u, 1 - u).start()

    for d in (0, 1):
        x_code(d, 1 - d).wait_send()
        for t in (0, 1):
            for c in range(4):
                x_chunk(t, d, c, 1 - d).wait_send()
            for u in (0, 1):
                x_corner(t, d, u, (1 - d, 1 - u)).wait_send()
            y_tile(t, d, 1 - d).wait_send()


def write_back(pops, mass, pops_out, mass_out, sem):
    copies = [
        pltpu.make_async_copy(pops, pops_out, sem.at[0]),
        pltpu.make_async_copy(mass, mass_out, sem.at[1]),
    ]
    for copy in copies:
        copy.start()
    for copy in copies:
        copy.wait()


def on_device(populations, mass, flags, relax):
    _, planes, depth, width = populations.shape
    tile, plane = (ROWS, LANES), (depth, width)
    f32 = jnp.float32
    vmem, dma = pltpu.VMEM, pltpu.SemaphoreType.DMA
    state_shape = (
        jax.ShapeDtypeStruct(populations.shape, f32),
        jax.ShapeDtypeStruct(mass.shape, f32),
    )
    hbm = pl.BlockSpec(memory_space=pltpu.HBM)
    here = pl.BlockSpec(memory_space=pltpu.VMEM)
    args = [pltpu.with_memory_space_constraint(a, pltpu.HBM) for a in (populations, mass, flags, relax)]
    state = pl.pallas_call(
        kernel,
        out_shape=state_shape,
        in_specs=[hbm] * 4,
        out_specs=(here, here),
        scratch_shapes=[
            vmem((2, 19, planes, *plane), f32),
            vmem((2, planes, *plane), f32),
            vmem((2, planes, *plane), jnp.int32),
            vmem((planes, *plane), f32),
            vmem((2, planes, *plane), f32),
            vmem((planes, 8, *plane), f32),
            vmem((planes, 5, *plane), f32),
            vmem((planes, 3, 3, *plane), f32),
            vmem((2, 5, *plane), f32),
            vmem((planes, 14, *plane), f32),
            vmem((2, 2, 4, 6, *tile), f32),
            vmem((2, 2, 4, 6, *tile), f32),
            vmem((2, *plane), f32),
            vmem((2, *plane), f32),
            vmem((2, 2, *tile), f32),
            vmem((2, 2, *tile), f32),
            vmem((2, 2, 2, *tile), f32),
            vmem((2, 2, 2, *tile), f32),
            dma((4,)),
            dma((2, 2, 4)),
            dma((2, 2, 4)),
            dma((2,)),
            dma((2,)),
            dma((2, 2)),
            dma((2, 2)),
            dma((2, 2, 2)),
            dma((2, 2, 2)),
        ],
        compiler_params=pltpu.CompilerParams(
            collective_id=0, has_side_effects=True, vmem_limit_bytes=32 * 1024 * 1024
        ),
        name="lattice_steps",
    )(*args)
    anywhere = pl.BlockSpec(memory_space=pl.ANY)
    return pl.pallas_call(
        write_back,
        out_shape=state_shape,
        in_specs=[here] * 2,
        out_specs=(anywhere,) * 2,
        scratch_shapes=[dma((2,))],
        name="write_back",
    )(*(pltpu.with_memory_space_constraint(a, pltpu.VMEM) for a in state))


def solution(mesh):
    return jax.shard_map(
        on_device,
        mesh=mesh,
        in_specs=(
            P(None, "gx", None, "gy"),
            P("gx", None, "gy"),
            P(None, "gx", None, "gy"),
            P("gx", None, "gy"),
        ),
        out_specs=(P(None, "gx", None, "gy"), P("gx", None, "gy")),
        check_vma=False,
    )
```

```python
import jax
import jax.numpy as jnp
from jax import lax
from jax.experimental import pallas as pl
from jax.experimental.pallas import tpu as pltpu
from jax.sharding import PartitionSpec as P

MESH = pl.DeviceIdType.MESH

VEL = [
    (0, 0, 0),
    (1, 0, 0),
    (-1, 0, 0),
    (0, 1, 0),
    (0, -1, 0),
    (0, 0, 1),
    (0, 0, -1),
    (1, 1, 0),
    (-1, -1, 0),
    (1, -1, 0),
    (-1, 1, 0),
    (1, 0, 1),
    (-1, 0, -1),
    (1, 0, -1),
    (-1, 0, 1),
    (0, 1, 1),
    (0, -1, -1),
    (0, 1, -1),
    (0, -1, 1),
]
INDEX = {c: q for q, c in enumerate(VEL)}
OPP = [INDEX[(-a, -b, -c)] for a, b, c in VEL]
W0, W1, W2 = 1.0 / 3.0, 1.0 / 18.0, 1.0 / 36.0
WEIGHT = [W0] + [W1] * 6 + [W2] * 12
SIGMA = 0.02
OFFS = [(0, 0), (1, 0), (-1, 0), (0, 1), (0, -1)]
IN_PLANE = [(1, 0), (-1, 0), (0, 1), (0, -1), (1, 1), (-1, -1), (1, -1), (-1, 1)]
LANES = 128
ROWS = 8


OPP_OFFS = [0, 2, 1, 4, 3]
CHUNKS = [(zh, h) for h in (0, 1) for zh in (0, 1)]


def side_dirs(cx):
    return [INDEX[(cx, b, c)] for b, c in OFFS]


def y_columns(cy):
    cols = []
    for plane in (0, 1):
        for cz in (0, 1, -1):
            cols.append((INDEX[(0, cy, cz)], plane))
        cols.append((INDEX[(1 - 2 * plane, cy, 0)], plane))
        cols.append((None, plane))
    return cols


def frac_of(e):
    return jnp.where(e == 1.0, 1.0, jnp.where(e > 1.5, e - 2.0, 0.0))


def code_of(kind, mass):
    return jnp.where(kind == 3, -1.0, jnp.where(kind == 0, 0.0, jnp.where(kind == 2, 1.0, 2.0 + mass)))


def half(h):
    return slice(h * LANES, (h + 1) * LANES)


def shift_y(halves, cy, column):
    lane = lax.broadcasted_iota(jnp.int32, halves[0].shape, 1)
    if cy == 1:
        moved = [pltpu.roll(a, 1, 1) for a in halves]
        edge = lane == 0
        return [jnp.where(edge, column, moved[0]), jnp.where(edge, moved[0], moved[1])]
    moved = [pltpu.roll(a, LANES - 1, 1) for a in halves]
    edge = lane == LANES - 1
    return [jnp.where(edge, moved[1], moved[0]), jnp.where(edge, column, moved[1])]


def shift_z(halves, cz):
    depth = halves[0].shape[0]
    return [pltpu.roll(a, cz % depth, 0) for a in halves]


def wall_z(halves, cz):
    row = lax.broadcasted_iota(jnp.int32, halves[0].shape, 0)
    outside = row == (0 if cz == 1 else halves[0].shape[0] - 1)
    return [jnp.where(outside, -1.0, a) for a in shift_z(halves, cz)]


def rows(z):
    return slice(z * ROWS, (z + 1) * ROWS)


def spread(tile, k):
    low, high = tile[:, 2 * k : 2 * k + 1], tile[:, 2 * k + 1 : 2 * k + 2]
    return jnp.concatenate([jnp.broadcast_to(low, tile.shape), jnp.broadcast_to(high, tile.shape)], axis=0)


def pack(columns):
    lane = lax.broadcasted_iota(jnp.int32, (ROWS, LANES), 1)
    tile = jnp.zeros(lane.shape, jnp.float32)
    for k, column in enumerate(columns):
        for z in (0, 1):
            tile = jnp.where(lane == 2 * k + z, jnp.broadcast_to(column[rows(z)], lane.shape), tile)
    return tile


def kernel(
    pops_in,
    mass_in,
    flags_in,
    relax_in,
    pops_out,
    mass_out,
    pops,
    mass,
    flags,
    relax,
    code,
    inner,
    cross,
    near,
    far,
    part,
    sx,
    rx,
    sc,
    rc,
    sy,
    ry,
    sk,
    rk,
    held_x,
    held_c,
    held_k,
    load_sem,
    sx_sem,
    rx_sem,
    sc_sem,
    rc_sem,
    sy_sem,
    ry_sem,
    sk_sem,
    rk_sem,
    held_x_sem,
    held_c_sem,
    held_k_sem,
    on_sem,
    go_sem,
):
    nx, ny = lax.axis_size("gx"), lax.axis_size("gy")
    gx, gy = lax.axis_index("gx"), lax.axis_index("gy")
    ys = [lax.rem(gy + ny - 1, ny), gy, lax.rem(gy + 1, ny)]
    parity = lax.rem(gx, 2)
    sides = [parity, 1 - parity]
    place = lax.rem(gx, 8)
    early = (place == 0) | (place == 3)
    late = (place == 4) | (place == 7)

    def peer(dx, u):
        return (lax.rem(gx + dx + nx, nx), ys[u + 1])

    def device(d, u):
        return peer(2 * d - 1, u)

    relay, relayed, beyond_relay = 2 * parity - 5, 3 + 2 * parity, 4

    barrier = pltpu.get_barrier_semaphore()

    def greet(*devices):
        for other in devices:
            pl.semaphore_signal(barrier, inc=1, device_id=other, device_id_type=MESH)

    @pl.when(jnp.logical_not(late))
    def _():
        greet(*[device(sides[0], u) for u in (0, -1, 1)])

    @pl.when(early)
    def _():
        greet(peer(beyond_relay, 0), *[peer(relayed, u) for u in (0, -1, 1)])

    greet(*[device(sides[1], u) for u in (0, -1, 1)], peer(0, -1), peer(0, 1))
    loads = [
        pltpu.make_async_copy(mass_in, mass.at[0], load_sem.at[0]),
        pltpu.make_async_copy(flags_in, flags, load_sem.at[1]),
        pltpu.make_async_copy(pops_in, pops.at[0], load_sem.at[2]),
        pltpu.make_async_copy(relax_in, relax, load_sem.at[3]),
    ]
    for load in loads:
        load.start()

    def x_code(d, at):
        return pltpu.make_async_remote_copy(
            sc.at[d], rc.at[at], sc_sem.at[d], rc_sem.at[at], device_id=device(d, 0), device_id_type=MESH
        )

    def x_chunk(t, d, c, at):
        count = pl.ds(0, 5 + t)
        return pltpu.make_async_remote_copy(
            sx.at[t, d, c, count],
            rx.at[t, at, c, count],
            sx_sem.at[t, d, c],
            rx_sem.at[t, at, c],
            device_id=device(d, 0),
            device_id_type=MESH,
        )

    def x_corner(t, d, u, at):
        return pltpu.make_async_remote_copy(
            sk.at[t, d, u],
            rk.at[t, at[0], at[1]],
            sk_sem.at[t, d, u],
            rk_sem.at[t, at[0], at[1]],
            device_id=device(d, 2 * u - 1),
            device_id_type=MESH,
        )

    def y_tile(t, u, at):
        return pltpu.make_async_remote_copy(
            sy.at[t, u], ry.at[t, at], sy_sem.at[t, u], ry_sem.at[t, at], device_id=(gx, ys[2 * u]), device_id_type=MESH
        )

    def to_relay(src, dst, send, recv, u=0):
        return pltpu.make_async_remote_copy(
            src, dst, send, recv, device_id=peer(relay, u), device_id_type=MESH
        )

    def to_relay_corner(u):
        d = parity
        return to_relay(sk.at[0, d, u], held_k.at[1 - u], sk_sem.at[0, d, u], held_k_sem.at[1 - u], 2 * u - 1)

    def to_relay_code():
        return to_relay(sc.at[parity], held_c, sc_sem.at[parity], held_c_sem.at[0])

    def to_relay_chunk(c):
        d, count = parity, pl.ds(0, 5)
        return to_relay(sx.at[0, d, c, count], held_x.at[c], sx_sem.at[0, d, c], held_x_sem.at[c])

    def arrivals():
        return [to_relay_corner(1), to_relay_corner(0), to_relay_code()] + [to_relay_chunk(c) for c in range(4)]

    def onward(i):
        d, count = parity, pl.ds(0, 5)
        parts = [(held_k.at[u], rk.at[0, d, u], rk_sem.at[0, d, u]) for u in (0, 1)]
        parts.append((held_c, rc.at[d], rc_sem.at[d]))
        parts += [(held_x.at[c], rx.at[0, d, c, count], rx_sem.at[0, d, c]) for c in range(4)]
        src, dst, recv = parts[i]
        return pltpu.make_async_remote_copy(
            src, dst, on_sem.at[i], recv, device_id=peer(beyond_relay, 0), device_id_type=MESH
        )

    def pick(pair, p):
        return pair[0] + p * (pair[1] - pair[0])

    plus, minus = side_dirs(1), side_dirs(-1)
    inward = list(zip(plus, minus))
    outward = list(zip(minus, plus))

    def rim_of(t, q, p, u):
        at = 0 if u == 0 else 2 * LANES - 1
        if q is None:
            return code[t, p, :, at : at + 1]
        return pops[t, q, p, :, at : at + 1]

    def fill_y(t):
        for u in (0, 1):
            sy[t, u] = pack([rim_of(t, q, p, u) for q, p in y_columns(2 * u - 1)])

    def fill_corner(t, p):
        for u in (0, 1):
            q = pick(outward[2 - u], p)
            sk[t, p, u] = pack([rim_of(t, q, p, u), rim_of(t, None, p, u)])

    loads[0].wait()
    loads[1].wait()
    for p in (0, 1):
        code[0, p] = code_of(flags[0, p], mass[0, p])
        sc[p] = code[0, p]
    loads[2].wait()
    for p in (0, 1):
        fill_corner(0, p)
        for k, (cy, cz) in enumerate(OFFS):
            halves = [pops[0, outward[k][p], p, :, half(h)] for h in (0, 1)]
            if cy:
                halves = shift_y(halves, cy, halves[0])
            if cz:
                halves = shift_z(halves, cz)
            for c, (z, h) in enumerate(CHUNKS):
                sx[0, p, c, k] = halves[h][rows(z)]
    fill_y(0)
    loads[3].wait()

    pl.semaphore_wait(barrier, 8 + late.astype(jnp.int32))

    @pl.when(late)
    def _():
        pl.semaphore_signal(go_sem, inc=1, device_id=peer(-beyond_relay, 0), device_id_type=MESH)

    def open_side(d):
        for u in (0, 1):
            x_corner(0, d, u, (1 - d, 1 - u)).start()
        x_code(d, 1 - d).start()
        for c in range(4):
            x_chunk(0, d, c, 1 - d).start()

    @pl.when(early)
    def _():
        for u in (0, 1):
            to_relay_corner(u).start()
        to_relay_code().start()
        for c in range(4):
            to_relay_chunk(c).start()

    @pl.when(jnp.logical_not(early))
    def _():
        open_side(sides[0])

    for u in (0, 1):
        y_tile(0, u, 1 - u).start()
    open_side(sides[1])

    def stream(t):
        place = [{c: k for k, c in enumerate(y_columns(cy))} for cy in (1, -1)]

        def column(q, p, cy):
            u = 0 if cy == 1 else 1
            return spread(ry[t, u], place[u][(q, p)])

        def moved(q, p, cy, cz):
            halves = [pops[t, q, p, :, half(h)] for h in (0, 1)]
            if cy:
                halves = shift_y(halves, cy, column(q, p, cy))
            if cz:
                halves = shift_z(halves, cz)
            return halves

        for p in (0, 1):
            own = [code[t, p, :, half(h)] for h in (0, 1)]
            table = {(0, 0): own}
            for cy in (1, -1):
                table[(cy, 0)] = shift_y(own, cy, column(None, p, cy))
            for cy in (0, 1, -1):
                for cz in (1, -1):
                    table[(cy, cz)] = wall_z(table[(cy, 0)], cz)
            for (cy, cz), halves in table.items():
                for h in (0, 1):
                    near[p, cy + 1, cz + 1, :, half(h)] = halves[h]
            for k, (cy, cz) in enumerate(IN_PLANE):
                halves = moved(INDEX[(0, cy, cz)], p, cy, cz)
                for h in (0, 1):
                    inner[p, k, :, half(h)] = halves[h]
            for k, (cy, cz) in enumerate(OFFS):
                halves = moved(outward[k][p], 1 - p, cy, cz)
                for h in (0, 1):
                    cross[p, k, :, half(h)] = halves[h]

    def plane_code(t, p):
        if t == 0:
            return [rc[p, :, half(h)] for h in (0, 1)]
        return [jnp.concatenate([rx[1, p, 2 * h, 5], rx[1, p, 2 * h + 1, 5]], axis=0) for h in (0, 1)]

    def far_codes(t, p):
        own = plane_code(t, p)
        for k, (cy, cz) in enumerate(OFFS):
            halves = own
            if cy:
                halves = shift_y(own, cy, spread(rk[t, p, 0 if cy == 1 else 1], 1))
            if cz:
                halves = wall_z(own, cz)
            for h in (0, 1):
                far[p, k, :, half(h)] = halves[h]

    def arrive(e, s, r, rebuilt, m):
        g = jnp.where(e == -1.0, r, jnp.where(e == 0.0, rebuilt - r, s))
        a = jnp.where(e == 1.0, 1.0, jnp.where(e > 1.5, 0.5 * (m + (e - 2.0)), 0.0))
        return g, a * (s - r)

    def side_moments(g):
        total = (g[0] + g[1]) + (g[2] + (g[3] + g[4]))
        return [total, g[1] - g[2], g[3] - g[4], g[1] + g[2], g[3] + g[4]]

    def interior(t, p, h, x_far):
        lanes = half(h)
        kind, m = flags[t, p, :, lanes], mass[t, p, :, lanes]
        rest = pops[t, 0, p, :, lanes]
        flat = [pops[t, INDEX[(0, cy, cz)], p, :, lanes] for cy, cz in IN_PLANE]
        fin = [pops[t, pick(inward[k], p), p, :, lanes] for k in range(5)]
        fout = [pops[t, pick(outward[k], p), p, :, lanes] for k in range(5)]
        tin, yin, zin, _, _ = side_moments(fin)
        tout, yout, zout, _, _ = side_moments(fout)
        pp, mm, pm, mp = flat[4:]
        ax = tin - tout
        ay = (yin + yout) + (flat[0] - flat[1]) + (pp - mm) + (pm - mp)
        az = (zin + zout) + (flat[2] - flat[3]) + (pp - mm) - (pm - mp)
        own = jnp.where(kind == 2, 1.0, jnp.where(kind == 1, m, 0.0))
        around = frac_of(x_far) + frac_of(near[1 - p, 1, 1, :, lanes])
        for cy, cz in OFFS[1:]:
            around = around + frac_of(near[p, cy + 1, cz + 1, :, lanes])
        gas = 1.0 - 3.0 * SIGMA * (around - 6.0 * own)
        lift = 2.0 * gas - 3.0 * (ax * ax + ay * ay + az * az)

        dm = jnp.zeros_like(m)
        e0 = near[p, 1, 1, :, lanes]
        g0 = jnp.where(e0 == 0.0, W0 * lift - rest, rest)
        g = []
        for k, (cy, cz) in enumerate(IN_PLANE):
            proj = sum(c * j for c, j in ((cy, ay), (cz, az)) if c)
            w = W2 if cy and cz else W1
            value, moved = arrive(
                near[p, cy + 1, cz + 1, :, lanes],
                inner[p, k, :, lanes],
                flat[k ^ 1],
                w * (lift + 9.0 * (proj * proj)),
                m,
            )
            g.append(value)
            dm = dm + moved
        out = []
        for k, (cy, cz) in enumerate(OFFS):
            proj = -ax + sum(c * j for c, j in ((cy, ay), (cz, az)) if c)
            w = W2 if cy or cz else W1
            value, moved = arrive(
                near[1 - p, cy + 1, cz + 1, :, lanes],
                cross[p, k, :, lanes],
                fin[OPP_OFFS[k]],
                w * (lift + 9.0 * (proj * proj)),
                m,
            )
            out.append(value)
            dm = dm + moved
        total, dy, dz, yy2, zz2 = side_moments(out)
        pp, mm, pm, mp = g[4:]
        diag, anti = pp + mm, pm + mp
        yy, zz = g[0] + g[1], g[2] + g[3]
        rho = total + g0 + yy + zz + (diag + anti)
        jy = dy + (g[0] - g[1]) + (pp - mm) + (pm - mp)
        jz = dz + (g[2] - g[3]) + (pp - mm) - (pm - mp)
        pyy = yy2 + yy + (diag + anti)
        pzz = zz2 + zz + (diag + anti)
        kept = (rho, total, jy, jz, pyy, pzz, dy, dz, diag - anti, dm, lift, ax, ay, az)
        for k, value in enumerate(kept):
            part[p, k, :, lanes] = value

    def finish(t, p, z, lanes, sources):
        kind, m = flags[t, p, z, lanes], mass[t, p, z, lanes]
        rho, tout, jy, jz, pyy, pzz, dyout, dzout, pyz, dm, lift, ax, ay, az = (
            part[p, k, z, lanes] for k in range(14)
        )
        g = []
        for k, (cy, cz) in enumerate(OFFS):
            proj = ax + sum(c * j for c, j in ((cy, ay), (cz, az)) if c)
            w = W2 if cy or cz else W1
            value, moved = arrive(
                far[p, k, z, lanes],
                sources[k],
                pops[t, pick(outward[OPP_OFFS[k]], p), p, z, lanes],
                w * (lift + 9.0 * (proj * proj)),
                m,
            )
            g.append(value)
            dm = dm + moved
        total, dy, dz, yy2, zz2 = side_moments(g)
        rho, jx, pxx = rho + total, total - tout, total + tout
        jy, jz, pyy, pzz = jy + dy, jz + dz, pyy + yy2, pzz + zz2
        pxy, pxz = dy - dyout, dz - dzout
        is_face, is_liquid = kind == 1, kind == 2
        mass_new = jnp.where(is_face, m + dm, jnp.where(is_liquid, rho, 0.0))
        fluid = is_face | is_liquid
        third = rho * (1.0 / 3.0)
        xx, yy, zz = jx * jx, jy * jy, jz * jz
        strength = (1.0 - relax[p, z, lanes]) * 4.5
        qxx, qyy, qzz = pxx - third - xx, pyy - third - yy, pzz - third - zz
        mean = (qxx + qyy + qzz) * (1.0 / 3.0)
        qxx, qyy, qzz, mean = strength * qxx, strength * qyy, strength * qzz, strength * mean
        four = 4.0 * strength
        qxy, qxz, qyz = four * (pxy - jx * jy), four * (pxz - jx * jz), four * (pyz - jy * jz)
        base = rho - 1.5 * (xx + yy + zz) - mean

        def couple(w, proj, stress):
            even = w * (base + 4.5 * (proj * proj) + stress)
            odd = (3.0 * w) * proj
            return jnp.where(fluid, even + odd, w), jnp.where(fluid, even - odd, w)

        new_in, new_out = [None] * 5, [None] * 5
        new_in[0], new_out[0] = couple(W1, jx, qxx)
        new_in[1], new_out[2] = couple(W2, jx + jy, qxx + qyy + qxy)
        new_in[2], new_out[1] = couple(W2, jx - jy, qxx + qyy - qxy)
        new_in[3], new_out[4] = couple(W2, jx + jz, qxx + qzz + qxz)
        new_in[4], new_out[3] = couple(W2, jx - jz, qxx + qzz - qxz)
        flat = [
            *couple(W1, jy, qyy),
            *couple(W1, jz, qzz),
            *couple(W2, jy + jz, qyy + qzz + qyz),
            *couple(W2, jy - jz, qyy + qzz - qyz),
        ]
        new = [(0, jnp.where(fluid, W0 * base, W0))]
        new += [(INDEX[(0, cy, cz)], flat[k]) for k, (cy, cz) in enumerate(IN_PLANE)]
        new += [(pick(inward[k], p), new_in[k]) for k in range(5)]
        new += [(pick(outward[k], p), new_out[k]) for k in range(5)]
        return mass_new, new, new_out

    def close(t, p):
        for u in (0, 1):
            x_corner(t, p, u, (p, u)).wait_recv()
        if t == 0:
            x_code(p, p).wait_recv()
            far_codes(0, p)
            for h in (0, 1):
                interior(0, p, h, far[p, 0, :, half(h)])
            for c, (z, h) in enumerate(CHUNKS):
                x_chunk(0, p, c, p).wait_recv()
                sources = [rx[0, p, c, k] for k in range(5)]
                lane = lax.broadcasted_iota(jnp.int32, sources[0].shape, 1)
                k, edge, u = (1, lane == 0, 0) if h == 0 else (2, lane == LANES - 1, 1)
                column = jnp.broadcast_to(rk[0, p, u][:, z : z + 1], lane.shape)
                sources[k] = jnp.where(edge, column, sources[k])
                z, lanes = rows(z), half(h)
                mass_new, new, new_out = finish(0, p, z, lanes, sources)
                code_new = code_of(flags[1, p, z, lanes], mass_new)
                for k in range(5):
                    sx[1, p, c, k] = new_out[k]
                sx[1, p, c, 5] = code_new
                x_chunk(1, p, c, 1 - p).start()
                code[1, p, z, lanes] = code_new
                mass[1, p, z, lanes] = mass_new
                for q, value in new:
                    pops[1, q, p, z, lanes] = value
            fill_corner(1, p)
            for u in (0, 1):
                x_corner(1, p, u, (1 - p, 1 - u)).start()
            return
        for h in (0, 1):
            for z in (0, 1):
                x_chunk(1, p, 2 * h + z, p).wait_recv()
            interior(1, p, h, jnp.concatenate([rx[1, p, 2 * h, 5], rx[1, p, 2 * h + 1, 5]], axis=0))
        far_codes(1, p)
        beyond = []
        for k, (cy, cz) in enumerate(OFFS):
            halves = [jnp.concatenate([rx[1, p, 2 * h, k], rx[1, p, 2 * h + 1, k]], axis=0) for h in (0, 1)]
            if cy:
                halves = shift_y(halves, cy, spread(rk[1, p, 0 if cy == 1 else 1], 0))
            if cz:
                halves = shift_z(halves, cz)
            beyond.append(halves)
        for h in (0, 1):
            lanes = half(h)
            mass_new, new, _ = finish(1, p, slice(None), lanes, [halves[h] for halves in beyond])
            mass_out[p, :, lanes] = mass_new
            for q, value in new:
                pops_out[q, p, :, lanes] = value

    for t in (0, 1):
        for u in (0, 1):
            y_tile(t, u, u).wait_recv()
        stream(t)

        if t == 0:

            @pl.when(early)
            def _():
                pl.semaphore_wait(go_sem, 1)
                for i, arrival in enumerate(arrivals()):
                    arrival.wait_recv()
                    onward(i).start()

        @pl.loop(0, 2)
        def _(i, t=t):
            close(t, lax.rem(gx + 1 + i, 2))

        if t == 0:
            fill_y(1)
            for u in (0, 1):
                y_tile(1, u, 1 - u).start()

    @pl.when(early)
    def _():
        for i in range(7):
            onward(i).wait_send()

    for d in (0, 1):
        x_code(d, 1 - d).wait_send()
        for t in (0, 1):
            for c in range(4):
                x_chunk(t, d, c, 1 - d).wait_send()
            for u in (0, 1):
                x_corner(t, d, u, (1 - d, 1 - u)).wait_send()
            y_tile(t, d, 1 - d).wait_send()


def write_back(pops, mass, pops_out, mass_out, sem):
    copies = [
        pltpu.make_async_copy(pops, pops_out, sem.at[0]),
        pltpu.make_async_copy(mass, mass_out, sem.at[1]),
    ]
    for copy in copies:
        copy.start()
    for copy in copies:
        copy.wait()


def on_device(populations, mass, flags, relax):
    _, planes, depth, width = populations.shape
    tile, plane = (ROWS, LANES), (depth, width)
    f32 = jnp.float32
    vmem, dma = pltpu.VMEM, pltpu.SemaphoreType.DMA
    state_shape = (
        jax.ShapeDtypeStruct(populations.shape, f32),
        jax.ShapeDtypeStruct(mass.shape, f32),
    )
    hbm = pl.BlockSpec(memory_space=pltpu.HBM)
    here = pl.BlockSpec(memory_space=pltpu.VMEM)
    args = [pltpu.with_memory_space_constraint(a, pltpu.HBM) for a in (populations, mass, flags, relax)]
    state = pl.pallas_call(
        kernel,
        out_shape=state_shape,
        in_specs=[hbm] * 4,
        out_specs=(here, here),
        scratch_shapes=[
            vmem((2, 19, planes, *plane), f32),
            vmem((2, planes, *plane), f32),
            vmem((2, planes, *plane), jnp.int32),
            vmem((planes, *plane), f32),
            vmem((2, planes, *plane), f32),
            vmem((planes, 8, *plane), f32),
            vmem((planes, 5, *plane), f32),
            vmem((planes, 3, 3, *plane), f32),
            vmem((2, 5, *plane), f32),
            vmem((planes, 14, *plane), f32),
            vmem((2, 2, 4, 6, *tile), f32),
            vmem((2, 2, 4, 6, *tile), f32),
            vmem((2, *plane), f32),
            vmem((2, *plane), f32),
            vmem((2, 2, *tile), f32),
            vmem((2, 2, *tile), f32),
            vmem((2, 2, 2, *tile), f32),
            vmem((2, 2, 2, *tile), f32),
            vmem((4, 5, *tile), f32),
            vmem(plane, f32),
            vmem((2, *tile), f32),
            dma((4,)),
            dma((2, 2, 4)),
            dma((2, 2, 4)),
            dma((2,)),
            dma((2,)),
            dma((2, 2)),
            dma((2, 2)),
            dma((2, 2, 2)),
            dma((2, 2, 2)),
            dma((4,)),
            dma((1,)),
            dma((2,)),
            dma((7,)),
            pltpu.SemaphoreType.REGULAR,
        ],
        compiler_params=pltpu.CompilerParams(
            collective_id=0, has_side_effects=True, vmem_limit_bytes=32 * 1024 * 1024
        ),
        name="lattice_steps",
    )(*args)
    anywhere = pl.BlockSpec(memory_space=pl.ANY)
    return pl.pallas_call(
        write_back,
        out_shape=state_shape,
        in_specs=[here] * 2,
        out_specs=(anywhere,) * 2,
        scratch_shapes=[dma((2,))],
        name="write_back",
    )(*(pltpu.with_memory_space_constraint(a, pltpu.VMEM) for a in state))


def solution(mesh):
    return jax.shard_map(
        on_device,
        mesh=mesh,
        in_specs=(
            P(None, "gx", None, "gy"),
            P("gx", None, "gy"),
            P(None, "gx", None, "gy"),
            P("gx", None, "gy"),
        ),
        out_specs=(P(None, "gx", None, "gy"), P("gx", None, "gy")),
        check_vma=False,
    )
```

```python
import jax
import jax.numpy as jnp
from jax import lax
from jax.experimental import pallas as pl
from jax.experimental.pallas import tpu as pltpu
from jax.sharding import PartitionSpec as P

MESH = pl.DeviceIdType.MESH

VEL = [
    (0, 0, 0),
    (1, 0, 0),
    (-1, 0, 0),
    (0, 1, 0),
    (0, -1, 0),
    (0, 0, 1),
    (0, 0, -1),
    (1, 1, 0),
    (-1, -1, 0),
    (1, -1, 0),
    (-1, 1, 0),
    (1, 0, 1),
    (-1, 0, -1),
    (1, 0, -1),
    (-1, 0, 1),
    (0, 1, 1),
    (0, -1, -1),
    (0, 1, -1),
    (0, -1, 1),
]
INDEX = {c: q for q, c in enumerate(VEL)}
OPP = [INDEX[(-a, -b, -c)] for a, b, c in VEL]
W0, W1, W2 = 1.0 / 3.0, 1.0 / 18.0, 1.0 / 36.0
WEIGHT = [W0] + [W1] * 6 + [W2] * 12
SIGMA = 0.02
OFFS = [(0, 0), (1, 0), (-1, 0), (0, 1), (0, -1)]
IN_PLANE = [(1, 0), (-1, 0), (0, 1), (0, -1), (1, 1), (-1, -1), (1, -1), (-1, 1)]
LANES = 128
ROWS = 8


OPP_OFFS = [0, 2, 1, 4, 3]
CHUNKS = [(zh, h) for h in (0, 1) for zh in (0, 1)]


def side_dirs(cx):
    return [INDEX[(cx, b, c)] for b, c in OFFS]


def y_columns(cy):
    cols = []
    for plane in (0, 1):
        for cz in (0, 1, -1):
            cols.append((INDEX[(0, cy, cz)], plane))
        cols.append((INDEX[(1 - 2 * plane, cy, 0)], plane))
        cols.append((None, plane))
    return cols


def frac_of(e):
    return jnp.where(e == 1.0, 1.0, jnp.where(e > 1.5, e - 2.0, 0.0))


def code_of(kind, mass):
    return jnp.where(kind == 3, -1.0, jnp.where(kind == 0, 0.0, jnp.where(kind == 2, 1.0, 2.0 + mass)))


def half(h):
    return slice(h * LANES, (h + 1) * LANES)


def shift_y(halves, cy, column):
    lane = lax.broadcasted_iota(jnp.int32, halves[0].shape, 1)
    if cy == 1:
        moved = [pltpu.roll(a, 1, 1) for a in halves]
        edge = lane == 0
        return [jnp.where(edge, column, moved[0]), jnp.where(edge, moved[0], moved[1])]
    moved = [pltpu.roll(a, LANES - 1, 1) for a in halves]
    edge = lane == LANES - 1
    return [jnp.where(edge, moved[1], moved[0]), jnp.where(edge, column, moved[1])]


def shift_z(halves, cz):
    depth = halves[0].shape[0]
    return [pltpu.roll(a, cz % depth, 0) for a in halves]


def wall_z(halves, cz):
    row = lax.broadcasted_iota(jnp.int32, halves[0].shape, 0)
    outside = row == (0 if cz == 1 else halves[0].shape[0] - 1)
    return [jnp.where(outside, -1.0, a) for a in shift_z(halves, cz)]


def rows(z):
    return slice(z * ROWS, (z + 1) * ROWS)


def spread(tile, k):
    low, high = tile[:, 2 * k : 2 * k + 1], tile[:, 2 * k + 1 : 2 * k + 2]
    return jnp.concatenate([jnp.broadcast_to(low, tile.shape), jnp.broadcast_to(high, tile.shape)], axis=0)


def pack(columns):
    lane = lax.broadcasted_iota(jnp.int32, (ROWS, LANES), 1)
    tile = jnp.zeros(lane.shape, jnp.float32)
    for k, column in enumerate(columns):
        for z in (0, 1):
            tile = jnp.where(lane == 2 * k + z, jnp.broadcast_to(column[rows(z)], lane.shape), tile)
    return tile


def kernel(
    pops_in,
    mass_in,
    flags_in,
    relax_in,
    pops_out,
    mass_out,
    pops,
    mass,
    flags,
    relax,
    code,
    inner,
    cross,
    near,
    far,
    part,
    sx,
    rx,
    sc,
    rc,
    sy,
    ry,
    sk,
    rk,
    held_x,
    held_c,
    held_k,
    load_sem,
    sx_sem,
    rx_sem,
    sc_sem,
    rc_sem,
    sy_sem,
    ry_sem,
    sk_sem,
    rk_sem,
    held_x_sem,
    held_c_sem,
    held_k_sem,
    on_sem,
    go_sem,
):
    nx, ny = lax.axis_size("gx"), lax.axis_size("gy")
    gx, gy = lax.axis_index("gx"), lax.axis_index("gy")
    ys = [lax.rem(gy + ny - 1, ny), gy, lax.rem(gy + 1, ny)]
    parity = lax.rem(gx, 2)
    sides = [parity, 1 - parity]
    place = lax.rem(gx, 8)
    early = (place == 0) | (place == 3)
    late = (place == 4) | (place == 7)

    def peer(dx, u):
        return (lax.rem(gx + dx + nx, nx), ys[u + 1])

    def device(d, u):
        return peer(2 * d - 1, u)

    relay, relayed, beyond_relay = 2 * parity - 5, 3 + 2 * parity, 4

    odd, last = lax.rem(gy, 2) == 1, gy == ny - 1
    answers_up = late & odd & jnp.logical_not(last)
    answers_down = late & (odd | (gy == 0))
    barrier = pltpu.get_barrier_semaphore()

    def greet(when, *devices):
        @pl.when(when)
        def _():
            for other in devices:
                pl.semaphore_signal(barrier, inc=1, device_id=other, device_id_type=MESH)

    greet(jnp.logical_not(late), *[device(sides[0], u) for u in (0, -1, 1)])
    greet(early, peer(beyond_relay, 0), *[peer(relayed, u) for u in (0, -1, 1)])
    greet(jnp.logical_not(late) | answers_down, peer(0, -1))
    greet(jnp.logical_not(late) | answers_up, peer(0, 1))
    greet((place != 5) & (place != 6), *[device(sides[1], u) for u in (0, -1, 1)])
    loads = [
        pltpu.make_async_copy(mass_in, mass.at[0], load_sem.at[0]),
        pltpu.make_async_copy(flags_in, flags, load_sem.at[1]),
        pltpu.make_async_copy(pops_in, pops.at[0], load_sem.at[2]),
        pltpu.make_async_copy(relax_in, relax, load_sem.at[3]),
    ]
    for load in loads:
        load.start()

    def x_code(d, at):
        return pltpu.make_async_remote_copy(
            sc.at[d], rc.at[at], sc_sem.at[d], rc_sem.at[at], device_id=device(d, 0), device_id_type=MESH
        )

    def x_chunk(t, d, c, at):
        count = pl.ds(0, 5 + t)
        return pltpu.make_async_remote_copy(
            sx.at[t, d, c, count],
            rx.at[t, at, c, count],
            sx_sem.at[t, d, c],
            rx_sem.at[t, at, c],
            device_id=device(d, 0),
            device_id_type=MESH,
        )

    def x_corner(t, d, u, at):
        return pltpu.make_async_remote_copy(
            sk.at[t, d, u],
            rk.at[t, at[0], at[1]],
            sk_sem.at[t, d, u],
            rk_sem.at[t, at[0], at[1]],
            device_id=device(d, 2 * u - 1),
            device_id_type=MESH,
        )

    def y_tile(t, u, at):
        return pltpu.make_async_remote_copy(
            sy.at[t, u], ry.at[t, at], sy_sem.at[t, u], ry_sem.at[t, at], device_id=(gx, ys[2 * u]), device_id_type=MESH
        )

    def to_relay(src, dst, send, recv, u=0):
        return pltpu.make_async_remote_copy(
            src, dst, send, recv, device_id=peer(relay, u), device_id_type=MESH
        )

    def to_relay_corner(u):
        d = parity
        return to_relay(sk.at[0, d, u], held_k.at[1 - u], sk_sem.at[0, d, u], held_k_sem.at[1 - u], 2 * u - 1)

    def to_relay_code():
        return to_relay(sc.at[parity], held_c, sc_sem.at[parity], held_c_sem.at[0])

    def to_relay_chunk(c):
        d, count = parity, pl.ds(0, 5)
        return to_relay(sx.at[0, d, c, count], held_x.at[c], sx_sem.at[0, d, c], held_x_sem.at[c])

    def arrivals():
        return [to_relay_corner(1), to_relay_corner(0), to_relay_code()] + [to_relay_chunk(c) for c in range(4)]

    def onward(i):
        d, count = parity, pl.ds(0, 5)
        parts = [(held_k.at[u], rk.at[0, d, u], rk_sem.at[0, d, u]) for u in (0, 1)]
        parts.append((held_c, rc.at[d], rc_sem.at[d]))
        parts += [(held_x.at[c], rx.at[0, d, c, count], rx_sem.at[0, d, c]) for c in range(4)]
        src, dst, recv = parts[i]
        return pltpu.make_async_remote_copy(
            src, dst, on_sem.at[i], recv, device_id=peer(beyond_relay, 0), device_id_type=MESH
        )

    def pick(pair, p):
        return pair[0] + p * (pair[1] - pair[0])

    plus, minus = side_dirs(1), side_dirs(-1)
    inward = list(zip(plus, minus))
    outward = list(zip(minus, plus))

    def rim_of(t, q, p, u):
        at = 0 if u == 0 else 2 * LANES - 1
        if q is None:
            return code[t, p, :, at : at + 1]
        return pops[t, q, p, :, at : at + 1]

    def fill_y(t):
        for u in (0, 1):
            sy[t, u] = pack([rim_of(t, q, p, u) for q, p in y_columns(2 * u - 1)])

    def fill_corner(t, p, u):
        q = pick(outward[2 - u], p)
        sk[t, p, u] = pack([rim_of(t, q, p, u), rim_of(t, None, p, u)])

    loads[0].wait()
    loads[1].wait()
    for p in (0, 1):
        code[0, p] = code_of(flags[0, p], mass[0, p])
        sc[p] = code[0, p]
    loads[2].wait()
    for p in (0, 1):
        for u in (0, 1):
            fill_corner(0, p, u)
        for k, (cy, cz) in enumerate(OFFS):
            halves = [pops[0, outward[k][p], p, :, half(h)] for h in (0, 1)]
            if cy:
                halves = shift_y(halves, cy, halves[0])
            if cz:
                halves = shift_z(halves, cz)
            for c, (z, h) in enumerate(CHUNKS):
                sx[0, p, c, k] = halves[h][rows(z)]
    fill_y(0)
    loads[3].wait()

    fewer = 2 * late.astype(jnp.int32) + answers_up.astype(jnp.int32) + answers_down.astype(jnp.int32)
    pl.semaphore_wait(barrier, 8 - fewer)

    @pl.when(late)
    def _():
        pl.semaphore_signal(go_sem, inc=1, device_id=peer(-beyond_relay, 0), device_id_type=MESH)

    def open_side(d):
        for u in (0, 1):
            x_corner(0, d, u, (1 - d, 1 - u)).start()
        x_code(d, 1 - d).start()
        for c in range(4):
            x_chunk(0, d, c, 1 - d).start()

    @pl.when(early)
    def _():
        for u in (0, 1):
            to_relay_corner(u).start()
        to_relay_code().start()
        for c in range(4):
            to_relay_chunk(c).start()

    @pl.when(jnp.logical_not(early))
    def _():
        open_side(sides[0])

    for u, answers in enumerate((answers_down, answers_up)):

        @pl.when(jnp.logical_not(answers))
        def _(u=u):
            y_tile(0, u, 1 - u).start()

    @pl.when(jnp.logical_not(late))
    def _():
        open_side(sides[1])

    def stream(t):
        place = [{c: k for k, c in enumerate(y_columns(cy))} for cy in (1, -1)]

        def column(q, p, cy):
            u = 0 if cy == 1 else 1
            return spread(ry[t, u], place[u][(q, p)])

        def moved(q, p, cy, cz):
            halves = [pops[t, q, p, :, half(h)] for h in (0, 1)]
            if cy:
                halves = shift_y(halves, cy, column(q, p, cy))
            if cz:
                halves = shift_z(halves, cz)
            return halves

        for p in (0, 1):
            own = [code[t, p, :, half(h)] for h in (0, 1)]
            table = {(0, 0): own}
            for cy in (1, -1):
                table[(cy, 0)] = shift_y(own, cy, column(None, p, cy))
            for cy in (0, 1, -1):
                for cz in (1, -1):
                    table[(cy, cz)] = wall_z(table[(cy, 0)], cz)
            for (cy, cz), halves in table.items():
                for h in (0, 1):
                    near[p, cy + 1, cz + 1, :, half(h)] = halves[h]
            for k, (cy, cz) in enumerate(IN_PLANE):
                halves = moved(INDEX[(0, cy, cz)], p, cy, cz)
                for h in (0, 1):
                    inner[p, k, :, half(h)] = halves[h]
            for k, (cy, cz) in enumerate(OFFS):
                halves = moved(outward[k][p], 1 - p, cy, cz)
                for h in (0, 1):
                    cross[p, k, :, half(h)] = halves[h]

    def plane_code(t, p):
        if t == 0:
            return [rc[p, :, half(h)] for h in (0, 1)]
        return [jnp.concatenate([rx[1, p, 2 * h, 5], rx[1, p, 2 * h + 1, 5]], axis=0) for h in (0, 1)]

    def far_codes(t, p):
        own = plane_code(t, p)
        for k, (cy, cz) in enumerate(OFFS):
            halves = own
            if cy:
                halves = shift_y(own, cy, spread(rk[t, p, 0 if cy == 1 else 1], 1))
            if cz:
                halves = wall_z(own, cz)
            for h in (0, 1):
                far[p, k, :, half(h)] = halves[h]

    def arrive(e, s, r, rebuilt, m):
        g = jnp.where(e == -1.0, r, jnp.where(e == 0.0, rebuilt - r, s))
        a = jnp.where(e == 1.0, 1.0, jnp.where(e > 1.5, 0.5 * (m + (e - 2.0)), 0.0))
        return g, a * (s - r)

    def side_moments(g):
        total = (g[0] + g[1]) + (g[2] + (g[3] + g[4]))
        return [total, g[1] - g[2], g[3] - g[4], g[1] + g[2], g[3] + g[4]]

    def interior(t, p, h, x_far):
        lanes = half(h)
        kind, m = flags[t, p, :, lanes], mass[t, p, :, lanes]
        rest = pops[t, 0, p, :, lanes]
        flat = [pops[t, INDEX[(0, cy, cz)], p, :, lanes] for cy, cz in IN_PLANE]
        fin = [pops[t, pick(inward[k], p), p, :, lanes] for k in range(5)]
        fout = [pops[t, pick(outward[k], p), p, :, lanes] for k in range(5)]
        tin, yin, zin, _, _ = side_moments(fin)
        tout, yout, zout, _, _ = side_moments(fout)
        pp, mm, pm, mp = flat[4:]
        ax = tin - tout
        ay = (yin + yout) + (flat[0] - flat[1]) + (pp - mm) + (pm - mp)
        az = (zin + zout) + (flat[2] - flat[3]) + (pp - mm) - (pm - mp)
        own = jnp.where(kind == 2, 1.0, jnp.where(kind == 1, m, 0.0))
        around = frac_of(x_far) + frac_of(near[1 - p, 1, 1, :, lanes])
        for cy, cz in OFFS[1:]:
            around = around + frac_of(near[p, cy + 1, cz + 1, :, lanes])
        gas = 1.0 - 3.0 * SIGMA * (around - 6.0 * own)
        lift = 2.0 * gas - 3.0 * (ax * ax + ay * ay + az * az)

        dm = jnp.zeros_like(m)
        e0 = near[p, 1, 1, :, lanes]
        g0 = jnp.where(e0 == 0.0, W0 * lift - rest, rest)
        g = []
        for k, (cy, cz) in enumerate(IN_PLANE):
            proj = sum(c * j for c, j in ((cy, ay), (cz, az)) if c)
            w = W2 if cy and cz else W1
            value, moved = arrive(
                near[p, cy + 1, cz + 1, :, lanes],
                inner[p, k, :, lanes],
                flat[k ^ 1],
                w * (lift + 9.0 * (proj * proj)),
                m,
            )
            g.append(value)
            dm = dm + moved
        out = []
        for k, (cy, cz) in enumerate(OFFS):
            proj = -ax + sum(c * j for c, j in ((cy, ay), (cz, az)) if c)
            w = W2 if cy or cz else W1
            value, moved = arrive(
                near[1 - p, cy + 1, cz + 1, :, lanes],
                cross[p, k, :, lanes],
                fin[OPP_OFFS[k]],
                w * (lift + 9.0 * (proj * proj)),
                m,
            )
            out.append(value)
            dm = dm + moved
        total, dy, dz, yy2, zz2 = side_moments(out)
        pp, mm, pm, mp = g[4:]
        diag, anti = pp + mm, pm + mp
        yy, zz = g[0] + g[1], g[2] + g[3]
        rho = total + g0 + yy + zz + (diag + anti)
        jy = dy + (g[0] - g[1]) + (pp - mm) + (pm - mp)
        jz = dz + (g[2] - g[3]) + (pp - mm) - (pm - mp)
        pyy = yy2 + yy + (diag + anti)
        pzz = zz2 + zz + (diag + anti)
        kept = (rho, total, jy, jz, pyy, pzz, dy, dz, diag - anti, dm, lift, ax, ay, az)
        for k, value in enumerate(kept):
            part[p, k, :, lanes] = value

    def finish(t, p, z, lanes, sources):
        kind, m = flags[t, p, z, lanes], mass[t, p, z, lanes]
        rho, tout, jy, jz, pyy, pzz, dyout, dzout, pyz, dm, lift, ax, ay, az = (
            part[p, k, z, lanes] for k in range(14)
        )
        g = []
        for k, (cy, cz) in enumerate(OFFS):
            proj = ax + sum(c * j for c, j in ((cy, ay), (cz, az)) if c)
            w = W2 if cy or cz else W1
            value, moved = arrive(
                far[p, k, z, lanes],
                sources[k],
                pops[t, pick(outward[OPP_OFFS[k]], p), p, z, lanes],
                w * (lift + 9.0 * (proj * proj)),
                m,
            )
            g.append(value)
            dm = dm + moved
        total, dy, dz, yy2, zz2 = side_moments(g)
        rho, jx, pxx = rho + total, total - tout, total + tout
        jy, jz, pyy, pzz = jy + dy, jz + dz, pyy + yy2, pzz + zz2
        pxy, pxz = dy - dyout, dz - dzout
        is_face, is_liquid = kind == 1, kind == 2
        mass_new = jnp.where(is_face, m + dm, jnp.where(is_liquid, rho, 0.0))
        fluid = is_face | is_liquid
        third = rho * (1.0 / 3.0)
        xx, yy, zz = jx * jx, jy * jy, jz * jz
        strength = (1.0 - relax[p, z, lanes]) * 4.5
        qxx, qyy, qzz = pxx - third - xx, pyy - third - yy, pzz - third - zz
        mean = (qxx + qyy + qzz) * (1.0 / 3.0)
        qxx, qyy, qzz, mean = strength * qxx, strength * qyy, strength * qzz, strength * mean
        four = 4.0 * strength
        qxy, qxz, qyz = four * (pxy - jx * jy), four * (pxz - jx * jz), four * (pyz - jy * jz)
        base = rho - 1.5 * (xx + yy + zz) - mean

        def couple(w, proj, stress):
            even = w * (base + 4.5 * (proj * proj) + stress)
            odd = (3.0 * w) * proj
            return jnp.where(fluid, even + odd, w), jnp.where(fluid, even - odd, w)

        new_in, new_out = [None] * 5, [None] * 5
        new_in[0], new_out[0] = couple(W1, jx, qxx)
        new_in[1], new_out[2] = couple(W2, jx + jy, qxx + qyy + qxy)
        new_in[2], new_out[1] = couple(W2, jx - jy, qxx + qyy - qxy)
        new_in[3], new_out[4] = couple(W2, jx + jz, qxx + qzz + qxz)
        new_in[4], new_out[3] = couple(W2, jx - jz, qxx + qzz - qxz)
        flat = [
            *couple(W1, jy, qyy),
            *couple(W1, jz, qzz),
            *couple(W2, jy + jz, qyy + qzz + qyz),
            *couple(W2, jy - jz, qyy + qzz - qyz),
        ]
        new = [(0, jnp.where(fluid, W0 * base, W0))]
        new += [(INDEX[(0, cy, cz)], flat[k]) for k, (cy, cz) in enumerate(IN_PLANE)]
        new += [(pick(inward[k], p), new_in[k]) for k in range(5)]
        new += [(pick(outward[k], p), new_out[k]) for k in range(5)]
        return mass_new, new, new_out

    def close(t, p):
        for u in (0, 1):
            x_corner(t, p, u, (p, u)).wait_recv()
        if t == 0:
            x_code(p, p).wait_recv()

            @pl.when(late & (p == sides[1]))
            def _():
                open_side(p)

            far_codes(0, p)
            for h in (0, 1):
                interior(0, p, h, far[p, 0, :, half(h)])
            for c, (z, h) in enumerate(CHUNKS):
                x_chunk(0, p, c, p).wait_recv()
                sources = [rx[0, p, c, k] for k in range(5)]
                lane = lax.broadcasted_iota(jnp.int32, sources[0].shape, 1)
                k, edge, u = (1, lane == 0, 0) if h == 0 else (2, lane == LANES - 1, 1)
                column = jnp.broadcast_to(rk[0, p, u][:, z : z + 1], lane.shape)
                sources[k] = jnp.where(edge, column, sources[k])
                z, lanes = rows(z), half(h)
                mass_new, new, new_out = finish(0, p, z, lanes, sources)
                code_new = code_of(flags[1, p, z, lanes], mass_new)
                for k in range(5):
                    sx[1, p, c, k] = new_out[k]
                sx[1, p, c, 5] = code_new
                code[1, p, z, lanes] = code_new
                for q, value in new:
                    pops[1, q, p, z, lanes] = value
                if c % 2 == 1:
                    fill_corner(1, p, h)
                    x_corner(1, p, h, (1 - p, 1 - h)).start()
                x_chunk(1, p, c, 1 - p).start()
                mass[1, p, z, lanes] = mass_new
            return
        for h in (0, 1):
            for z in (0, 1):
                x_chunk(1, p, 2 * h + z, p).wait_recv()
            interior(1, p, h, jnp.concatenate([rx[1, p, 2 * h, 5], rx[1, p, 2 * h + 1, 5]], axis=0))
        far_codes(1, p)
        beyond = []
        for k, (cy, cz) in enumerate(OFFS):
            halves = [jnp.concatenate([rx[1, p, 2 * h, k], rx[1, p, 2 * h + 1, k]], axis=0) for h in (0, 1)]
            if cy:
                halves = shift_y(halves, cy, spread(rk[1, p, 0 if cy == 1 else 1], 0))
            if cz:
                halves = shift_z(halves, cz)
            beyond.append(halves)
        for h in (0, 1):
            lanes = half(h)
            mass_new, new, _ = finish(1, p, slice(None), lanes, [halves[h] for halves in beyond])
            mass_out[p, :, lanes] = mass_new
            for q, value in new:
                pops_out[q, p, :, lanes] = value

    for t in (0, 1):
        for u in (0, 1):
            y_tile(t, u, u).wait_recv()
        if t == 0:

            for u, answers in enumerate((answers_down, answers_up)):

                @pl.when(answers)
                def _(u=u):
                    y_tile(0, u, 1 - u).start()

        stream(t)

        if t == 0:

            @pl.when(early)
            def _():
                pl.semaphore_wait(go_sem, 1)
                for i, arrival in enumerate(arrivals()):
                    arrival.wait_recv()
                    onward(i).start()

        @pl.loop(0, 2)
        def _(i, t=t):
            close(t, lax.rem(gx + 1 + i, 2))

        if t == 0:
            fill_y(1)
            for u in (0, 1):
                y_tile(1, u, 1 - u).start()

    @pl.when(early)
    def _():
        for i in range(7):
            onward(i).wait_send()

    for d in (0, 1):
        x_code(d, 1 - d).wait_send()
        for t in (0, 1):
            for c in range(4):
                x_chunk(t, d, c, 1 - d).wait_send()
            for u in (0, 1):
                x_corner(t, d, u, (1 - d, 1 - u)).wait_send()
            y_tile(t, d, 1 - d).wait_send()


def write_back(pops, mass, pops_out, mass_out, sem):
    copies = [
        pltpu.make_async_copy(pops, pops_out, sem.at[0]),
        pltpu.make_async_copy(mass, mass_out, sem.at[1]),
    ]
    for copy in copies:
        copy.start()
    for copy in copies:
        copy.wait()


def on_device(populations, mass, flags, relax):
    _, planes, depth, width = populations.shape
    tile, plane = (ROWS, LANES), (depth, width)
    f32 = jnp.float32
    vmem, dma = pltpu.VMEM, pltpu.SemaphoreType.DMA
    state_shape = (
        jax.ShapeDtypeStruct(populations.shape, f32),
        jax.ShapeDtypeStruct(mass.shape, f32),
    )
    hbm = pl.BlockSpec(memory_space=pltpu.HBM)
    here = pl.BlockSpec(memory_space=pltpu.VMEM)
    args = [pltpu.with_memory_space_constraint(a, pltpu.HBM) for a in (populations, mass, flags, relax)]
    state = pl.pallas_call(
        kernel,
        out_shape=state_shape,
        in_specs=[hbm] * 4,
        out_specs=(here, here),
        scratch_shapes=[
            vmem((2, 19, planes, *plane), f32),
            vmem((2, planes, *plane), f32),
            vmem((2, planes, *plane), jnp.int32),
            vmem((planes, *plane), f32),
            vmem((2, planes, *plane), f32),
            vmem((planes, 8, *plane), f32),
            vmem((planes, 5, *plane), f32),
            vmem((planes, 3, 3, *plane), f32),
            vmem((2, 5, *plane), f32),
            vmem((planes, 14, *plane), f32),
            vmem((2, 2, 4, 6, *tile), f32),
            vmem((2, 2, 4, 6, *tile), f32),
            vmem((2, *plane), f32),
            vmem((2, *plane), f32),
            vmem((2, 2, *tile), f32),
            vmem((2, 2, *tile), f32),
            vmem((2, 2, 2, *tile), f32),
            vmem((2, 2, 2, *tile), f32),
            vmem((4, 5, *tile), f32),
            vmem(plane, f32),
            vmem((2, *tile), f32),
            dma((4,)),
            dma((2, 2, 4)),
            dma((2, 2, 4)),
            dma((2,)),
            dma((2,)),
            dma((2, 2)),
            dma((2, 2)),
            dma((2, 2, 2)),
            dma((2, 2, 2)),
            dma((4,)),
            dma((1,)),
            dma((2,)),
            dma((7,)),
            pltpu.SemaphoreType.REGULAR,
        ],
        compiler_params=pltpu.CompilerParams(
            collective_id=0, has_side_effects=True, vmem_limit_bytes=32 * 1024 * 1024
        ),
        name="lattice_steps",
    )(*args)
    anywhere = pl.BlockSpec(memory_space=pl.ANY)
    return pl.pallas_call(
        write_back,
        out_shape=state_shape,
        in_specs=[here] * 2,
        out_specs=(anywhere,) * 2,
        scratch_shapes=[dma((2,))],
        name="write_back",
    )(*(pltpu.with_memory_space_constraint(a, pltpu.VMEM) for a in state))


def solution(mesh):
    return jax.shard_map(
        on_device,
        mesh=mesh,
        in_specs=(
            P(None, "gx", None, "gy"),
            P("gx", None, "gy"),
            P(None, "gx", None, "gy"),
            P("gx", None, "gy"),
        ),
        out_specs=(P(None, "gx", None, "gy"), P("gx", None, "gy")),
        check_vma=False,
    )
```

```python
import jax
import jax.numpy as jnp
from jax import lax
from jax.experimental import pallas as pl
from jax.experimental.pallas import tpu as pltpu
from jax.sharding import PartitionSpec as P

MESH = pl.DeviceIdType.MESH

VEL = [
    (0, 0, 0),
    (1, 0, 0),
    (-1, 0, 0),
    (0, 1, 0),
    (0, -1, 0),
    (0, 0, 1),
    (0, 0, -1),
    (1, 1, 0),
    (-1, -1, 0),
    (1, -1, 0),
    (-1, 1, 0),
    (1, 0, 1),
    (-1, 0, -1),
    (1, 0, -1),
    (-1, 0, 1),
    (0, 1, 1),
    (0, -1, -1),
    (0, 1, -1),
    (0, -1, 1),
]
INDEX = {c: q for q, c in enumerate(VEL)}
OPP = [INDEX[(-a, -b, -c)] for a, b, c in VEL]
W0, W1, W2 = 1.0 / 3.0, 1.0 / 18.0, 1.0 / 36.0
WEIGHT = [W0] + [W1] * 6 + [W2] * 12
SIGMA = 0.02
OFFS = [(0, 0), (1, 0), (-1, 0), (0, 1), (0, -1)]
IN_PLANE = [(1, 0), (-1, 0), (0, 1), (0, -1), (1, 1), (-1, -1), (1, -1), (-1, 1)]
LANES = 128
ROWS = 8


OPP_OFFS = [0, 2, 1, 4, 3]
CHUNKS = [(zh, h) for h in (0, 1) for zh in (0, 1)]


def side_dirs(cx):
    return [INDEX[(cx, b, c)] for b, c in OFFS]


def y_columns(cy):
    cols = []
    for plane in (0, 1):
        for cz in (0, 1, -1):
            cols.append((INDEX[(0, cy, cz)], plane))
        cols.append((INDEX[(1 - 2 * plane, cy, 0)], plane))
        cols.append((None, plane))
    return cols


def frac_of(e):
    return jnp.where(e == 1.0, 1.0, jnp.where(e > 1.5, e - 2.0, 0.0))


def code_of(kind, mass):
    return jnp.where(kind == 3, -1.0, jnp.where(kind == 0, 0.0, jnp.where(kind == 2, 1.0, 2.0 + mass)))


def half(h):
    return slice(h * LANES, (h + 1) * LANES)


def shift_y(halves, cy, column):
    lane = lax.broadcasted_iota(jnp.int32, halves[0].shape, 1)
    if cy == 1:
        moved = [pltpu.roll(a, 1, 1) for a in halves]
        edge = lane == 0
        return [jnp.where(edge, column, moved[0]), jnp.where(edge, moved[0], moved[1])]
    moved = [pltpu.roll(a, LANES - 1, 1) for a in halves]
    edge = lane == LANES - 1
    return [jnp.where(edge, moved[1], moved[0]), jnp.where(edge, column, moved[1])]


def shift_z(halves, cz):
    depth = halves[0].shape[0]
    return [pltpu.roll(a, cz % depth, 0) for a in halves]


def wall_z(halves, cz):
    row = lax.broadcasted_iota(jnp.int32, halves[0].shape, 0)
    outside = row == (0 if cz == 1 else halves[0].shape[0] - 1)
    return [jnp.where(outside, -1.0, a) for a in shift_z(halves, cz)]


def rows(z):
    return slice(z * ROWS, (z + 1) * ROWS)


def spread(tile, k):
    low, high = tile[:, 2 * k : 2 * k + 1], tile[:, 2 * k + 1 : 2 * k + 2]
    return jnp.concatenate([jnp.broadcast_to(low, tile.shape), jnp.broadcast_to(high, tile.shape)], axis=0)


def pack(columns):
    lane = lax.broadcasted_iota(jnp.int32, (ROWS, LANES), 1)
    tile = jnp.zeros(lane.shape, jnp.float32)
    for k, column in enumerate(columns):
        for z in (0, 1):
            tile = jnp.where(lane == 2 * k + z, jnp.broadcast_to(column[rows(z)], lane.shape), tile)
    return tile


def kernel(
    pops_in,
    mass_in,
    flags_in,
    relax_in,
    pops_out,
    mass_out,
    pops,
    mass,
    flags,
    relax,
    code,
    inner,
    cross,
    near,
    far,
    part,
    sx,
    rx,
    sc,
    rc,
    sy,
    ry,
    sk,
    rk,
    held_x,
    held_c,
    held_k,
    load_sem,
    sx_sem,
    rx_sem,
    sc_sem,
    rc_sem,
    sy_sem,
    ry_sem,
    sk_sem,
    rk_sem,
    held_x_sem,
    held_c_sem,
    held_k_sem,
    on_sem,
    go_sem,
):
    nx, ny = lax.axis_size("gx"), lax.axis_size("gy")
    gx, gy = lax.axis_index("gx"), lax.axis_index("gy")
    ys = [lax.rem(gy + ny - 1, ny), gy, lax.rem(gy + 1, ny)]
    parity = lax.rem(gx, 2)
    sides = [parity, 1 - parity]
    place = lax.rem(gx, 8)
    early = (place == 0) | (place == 3)
    late = (place == 4) | (place == 7)

    def peer(dx, u):
        return (lax.rem(gx + dx + nx, nx), ys[u + 1])

    def device(d, u):
        return peer(2 * d - 1, u)

    relay, relayed, beyond_relay = 2 * parity - 5, 3 + 2 * parity, 4

    odd, last = lax.rem(gy, 2) == 1, gy == ny - 1
    first = gy == 0
    answers_up = late & odd & jnp.logical_not(last)
    answers_down = late & (odd | first)
    barrier = pltpu.get_barrier_semaphore()

    def greet(when, *devices):
        @pl.when(when)
        def _():
            for other in devices:
                pl.semaphore_signal(barrier, inc=1, device_id=other, device_id_type=MESH)

    greet(jnp.logical_not(late), *[device(sides[0], u) for u in (0, -1, 1)])
    greet(early, peer(beyond_relay, 0), peer(relayed, 0), peer(relayed, -1))
    greet(early & jnp.logical_not(last), peer(relayed, 1))
    greet(jnp.logical_not(late) | answers_down, peer(0, -1))
    greet(jnp.logical_not(late) | answers_up, peer(0, 1))
    greet((place != 5) & (place != 6), *[device(sides[1], u) for u in (0, -1, 1)])
    loads = [
        pltpu.make_async_copy(mass_in, mass.at[0], load_sem.at[0]),
        pltpu.make_async_copy(flags_in, flags, load_sem.at[1]),
        pltpu.make_async_copy(pops_in, pops.at[0], load_sem.at[2]),
        pltpu.make_async_copy(relax_in, relax, load_sem.at[3]),
    ]
    for load in loads:
        load.start()

    fewer = 2 * late.astype(jnp.int32) + answers_up.astype(jnp.int32) + answers_down.astype(jnp.int32)
    greeted = 8 - fewer - (early & first).astype(jnp.int32)

    @pl.when(late)
    def _():
        pl.semaphore_wait(barrier, greeted)
        pl.semaphore_signal(go_sem, inc=1, device_id=peer(-beyond_relay, 0), device_id_type=MESH)

    def x_code(d, at):
        return pltpu.make_async_remote_copy(
            sc.at[d], rc.at[at], sc_sem.at[d], rc_sem.at[at], device_id=device(d, 0), device_id_type=MESH
        )

    def x_chunk(t, d, c, at):
        count = pl.ds(0, 5 + t)
        return pltpu.make_async_remote_copy(
            sx.at[t, d, c, count],
            rx.at[t, at, c, count],
            sx_sem.at[t, d, c],
            rx_sem.at[t, at, c],
            device_id=device(d, 0),
            device_id_type=MESH,
        )

    def x_corner(t, d, u, at):
        return pltpu.make_async_remote_copy(
            sk.at[t, d, u],
            rk.at[t, at[0], at[1]],
            sk_sem.at[t, d, u],
            rk_sem.at[t, at[0], at[1]],
            device_id=device(d, 2 * u - 1),
            device_id_type=MESH,
        )

    def y_tile(t, u, at):
        return pltpu.make_async_remote_copy(
            sy.at[t, u], ry.at[t, at], sy_sem.at[t, u], ry_sem.at[t, at], device_id=(gx, ys[2 * u]), device_id_type=MESH
        )

    def to_relay(src, dst, send, recv, u=0):
        return pltpu.make_async_remote_copy(
            src, dst, send, recv, device_id=peer(relay, u), device_id_type=MESH
        )

    def to_relay_corner(u):
        d = parity
        return to_relay(sk.at[0, d, u], held_k.at[1 - u], sk_sem.at[0, d, u], held_k_sem.at[1 - u], 2 * u - 1)

    def to_relay_code():
        return to_relay(sc.at[parity], held_c, sc_sem.at[parity], held_c_sem.at[0])

    def to_relay_chunk(c):
        d, count = parity, pl.ds(0, 5)
        return to_relay(sx.at[0, d, c, count], held_x.at[c], sx_sem.at[0, d, c], held_x_sem.at[c])

    def arrivals():
        return [to_relay_corner(1), to_relay_corner(0), to_relay_code()] + [to_relay_chunk(c) for c in range(4)]

    def onward(i):
        d, count = parity, pl.ds(0, 5)
        parts = [(held_k.at[u], rk.at[0, d, u], rk_sem.at[0, d, u]) for u in (0, 1)]
        parts.append((held_c, rc.at[d], rc_sem.at[d]))
        parts += [(held_x.at[c], rx.at[0, d, c, count], rx_sem.at[0, d, c]) for c in range(4)]
        src, dst, recv = parts[i]
        return pltpu.make_async_remote_copy(
            src, dst, on_sem.at[i], recv, device_id=peer(beyond_relay, 0), device_id_type=MESH
        )

    def pick(pair, p):
        return pair[0] + p * (pair[1] - pair[0])

    plus, minus = side_dirs(1), side_dirs(-1)
    inward = list(zip(plus, minus))
    outward = list(zip(minus, plus))

    def rim_of(t, q, p, u):
        at = 0 if u == 0 else 2 * LANES - 1
        if q is None:
            return code[t, p, :, at : at + 1]
        return pops[t, q, p, :, at : at + 1]

    def fill_y(t):
        for u in (0, 1):
            sy[t, u] = pack([rim_of(t, q, p, u) for q, p in y_columns(2 * u - 1)])

    def fill_corner(t, p, u):
        q = pick(outward[2 - u], p)
        sk[t, p, u] = pack([rim_of(t, q, p, u), rim_of(t, None, p, u)])

    loads[0].wait()
    loads[1].wait()
    for p in (0, 1):
        code[0, p] = code_of(flags[0, p], mass[0, p])
        sc[p] = code[0, p]
    loads[2].wait()
    for p in (0, 1):
        for u in (0, 1):
            fill_corner(0, p, u)
        for k, (cy, cz) in enumerate(OFFS):
            halves = [pops[0, outward[k][p], p, :, half(h)] for h in (0, 1)]
            if cy:
                halves = shift_y(halves, cy, halves[0])
            if cz:
                halves = shift_z(halves, cz)
            for c, (z, h) in enumerate(CHUNKS):
                sx[0, p, c, k] = halves[h][rows(z)]
    fill_y(0)
    loads[3].wait()

    @pl.when(jnp.logical_not(late))
    def _():
        pl.semaphore_wait(barrier, greeted)

    def open_side(d):
        for u in (0, 1):
            x_corner(0, d, u, (1 - d, 1 - u)).start()
        x_code(d, 1 - d).start()
        for c in range(4):
            x_chunk(0, d, c, 1 - d).start()

    @pl.when(early)
    def _():
        to_relay_corner(1).start()
        to_relay_code().start()
        for c in range(4):
            to_relay_chunk(c).start()

    @pl.when(early & jnp.logical_not(first))
    def _():
        to_relay_corner(0).start()

    @pl.when(jnp.logical_not(early))
    def _():
        open_side(sides[0])

    for u, answers in enumerate((answers_down, answers_up)):

        @pl.when(jnp.logical_not(answers))
        def _(u=u):
            y_tile(0, u, 1 - u).start()

    @pl.when(jnp.logical_not(late))
    def _():
        open_side(sides[1])

    def stream(t):
        place = [{c: k for k, c in enumerate(y_columns(cy))} for cy in (1, -1)]

        def column(q, p, cy):
            u = 0 if cy == 1 else 1
            return spread(ry[t, u], place[u][(q, p)])

        def moved(q, p, cy, cz):
            halves = [pops[t, q, p, :, half(h)] for h in (0, 1)]
            if cy:
                halves = shift_y(halves, cy, column(q, p, cy))
            if cz:
                halves = shift_z(halves, cz)
            return halves

        for p in (0, 1):
            own = [code[t, p, :, half(h)] for h in (0, 1)]
            table = {(0, 0): own}
            for cy in (1, -1):
                table[(cy, 0)] = shift_y(own, cy, column(None, p, cy))
            for cy in (0, 1, -1):
                for cz in (1, -1):
                    table[(cy, cz)] = wall_z(table[(cy, 0)], cz)
            for (cy, cz), halves in table.items():
                for h in (0, 1):
                    near[p, cy + 1, cz + 1, :, half(h)] = halves[h]
            for k, (cy, cz) in enumerate(IN_PLANE):
                halves = moved(INDEX[(0, cy, cz)], p, cy, cz)
                for h in (0, 1):
                    inner[p, k, :, half(h)] = halves[h]
            for k, (cy, cz) in enumerate(OFFS):
                halves = moved(outward[k][p], 1 - p, cy, cz)
                for h in (0, 1):
                    cross[p, k, :, half(h)] = halves[h]

    def plane_code(t, p):
        if t == 0:
            return [rc[p, :, half(h)] for h in (0, 1)]
        return [jnp.concatenate([rx[1, p, 2 * h, 5], rx[1, p, 2 * h + 1, 5]], axis=0) for h in (0, 1)]

    def far_codes(t, p):
        own = plane_code(t, p)
        for k, (cy, cz) in enumerate(OFFS):
            halves = own
            if cy:
                halves = shift_y(own, cy, spread(rk[t, p, 0 if cy == 1 else 1], 1))
            if cz:
                halves = wall_z(own, cz)
            for h in (0, 1):
                far[p, k, :, half(h)] = halves[h]

    def arrive(e, s, r, rebuilt, m):
        g = jnp.where(e == -1.0, r, jnp.where(e == 0.0, rebuilt - r, s))
        a = jnp.where(e == 1.0, 1.0, jnp.where(e > 1.5, 0.5 * (m + (e - 2.0)), 0.0))
        return g, a * (s - r)

    def side_moments(g):
        total = (g[0] + g[1]) + (g[2] + (g[3] + g[4]))
        return [total, g[1] - g[2], g[3] - g[4], g[1] + g[2], g[3] + g[4]]

    def interior(t, p, h, x_far):
        lanes = half(h)
        kind, m = flags[t, p, :, lanes], mass[t, p, :, lanes]
        rest = pops[t, 0, p, :, lanes]
        flat = [pops[t, INDEX[(0, cy, cz)], p, :, lanes] for cy, cz in IN_PLANE]
        fin = [pops[t, pick(inward[k], p), p, :, lanes] for k in range(5)]
        fout = [pops[t, pick(outward[k], p), p, :, lanes] for k in range(5)]
        tin, yin, zin, _, _ = side_moments(fin)
        tout, yout, zout, _, _ = side_moments(fout)
        pp, mm, pm, mp = flat[4:]
        ax = tin - tout
        ay = (yin + yout) + (flat[0] - flat[1]) + (pp - mm) + (pm - mp)
        az = (zin + zout) + (flat[2] - flat[3]) + (pp - mm) - (pm - mp)
        own = jnp.where(kind == 2, 1.0, jnp.where(kind == 1, m, 0.0))
        around = frac_of(x_far) + frac_of(near[1 - p, 1, 1, :, lanes])
        for cy, cz in OFFS[1:]:
            around = around + frac_of(near[p, cy + 1, cz + 1, :, lanes])
        gas = 1.0 - 3.0 * SIGMA * (around - 6.0 * own)
        lift = 2.0 * gas - 3.0 * (ax * ax + ay * ay + az * az)

        dm = jnp.zeros_like(m)
        e0 = near[p, 1, 1, :, lanes]
        g0 = jnp.where(e0 == 0.0, W0 * lift - rest, rest)
        g = []
        for k, (cy, cz) in enumerate(IN_PLANE):
            proj = sum(c * j for c, j in ((cy, ay), (cz, az)) if c)
            w = W2 if cy and cz else W1
            value, moved = arrive(
                near[p, cy + 1, cz + 1, :, lanes],
                inner[p, k, :, lanes],
                flat[k ^ 1],
                w * (lift + 9.0 * (proj * proj)),
                m,
            )
            g.append(value)
            dm = dm + moved
        out = []
        for k, (cy, cz) in enumerate(OFFS):
            proj = -ax + sum(c * j for c, j in ((cy, ay), (cz, az)) if c)
            w = W2 if cy or cz else W1
            value, moved = arrive(
                near[1 - p, cy + 1, cz + 1, :, lanes],
                cross[p, k, :, lanes],
                fin[OPP_OFFS[k]],
                w * (lift + 9.0 * (proj * proj)),
                m,
            )
            out.append(value)
            dm = dm + moved
        total, dy, dz, yy2, zz2 = side_moments(out)
        pp, mm, pm, mp = g[4:]
        diag, anti = pp + mm, pm + mp
        yy, zz = g[0] + g[1], g[2] + g[3]
        rho = total + g0 + yy + zz + (diag + anti)
        jy = dy + (g[0] - g[1]) + (pp - mm) + (pm - mp)
        jz = dz + (g[2] - g[3]) + (pp - mm) - (pm - mp)
        pyy = yy2 + yy + (diag + anti)
        pzz = zz2 + zz + (diag + anti)
        kept = (rho, total, jy, jz, pyy, pzz, dy, dz, diag - anti, dm, lift, ax, ay, az)
        for k, value in enumerate(kept):
            part[p, k, :, lanes] = value

    def finish(t, p, z, lanes, sources):
        kind, m = flags[t, p, z, lanes], mass[t, p, z, lanes]
        rho, tout, jy, jz, pyy, pzz, dyout, dzout, pyz, dm, lift, ax, ay, az = (
            part[p, k, z, lanes] for k in range(14)
        )
        g = []
        for k, (cy, cz) in enumerate(OFFS):
            proj = ax + sum(c * j for c, j in ((cy, ay), (cz, az)) if c)
            w = W2 if cy or cz else W1
            value, moved = arrive(
                far[p, k, z, lanes],
                sources[k],
                pops[t, pick(outward[OPP_OFFS[k]], p), p, z, lanes],
                w * (lift + 9.0 * (proj * proj)),
                m,
            )
            g.append(value)
            dm = dm + moved
        total, dy, dz, yy2, zz2 = side_moments(g)
        rho, jx, pxx = rho + total, total - tout, total + tout
        jy, jz, pyy, pzz = jy + dy, jz + dz, pyy + yy2, pzz + zz2
        pxy, pxz = dy - dyout, dz - dzout
        is_face, is_liquid = kind == 1, kind == 2
        mass_new = jnp.where(is_face, m + dm, jnp.where(is_liquid, rho, 0.0))
        fluid = is_face | is_liquid
        third = rho * (1.0 / 3.0)
        xx, yy, zz = jx * jx, jy * jy, jz * jz
        strength = (1.0 - relax[p, z, lanes]) * 4.5
        qxx, qyy, qzz = pxx - third - xx, pyy - third - yy, pzz - third - zz
        mean = (qxx + qyy + qzz) * (1.0 / 3.0)
        qxx, qyy, qzz, mean = strength * qxx, strength * qyy, strength * qzz, strength * mean
        four = 4.0 * strength
        qxy, qxz, qyz = four * (pxy - jx * jy), four * (pxz - jx * jz), four * (pyz - jy * jz)
        base = rho - 1.5 * (xx + yy + zz) - mean

        def couple(w, proj, stress):
            even = w * (base + 4.5 * (proj * proj) + stress)
            odd = (3.0 * w) * proj
            return jnp.where(fluid, even + odd, w), jnp.where(fluid, even - odd, w)

        new_in, new_out = [None] * 5, [None] * 5
        new_in[0], new_out[0] = couple(W1, jx, qxx)
        new_in[1], new_out[2] = couple(W2, jx + jy, qxx + qyy + qxy)
        new_in[2], new_out[1] = couple(W2, jx - jy, qxx + qyy - qxy)
        new_in[3], new_out[4] = couple(W2, jx + jz, qxx + qzz + qxz)
        new_in[4], new_out[3] = couple(W2, jx - jz, qxx + qzz - qxz)
        flat = [
            *couple(W1, jy, qyy),
            *couple(W1, jz, qzz),
            *couple(W2, jy + jz, qyy + qzz + qyz),
            *couple(W2, jy - jz, qyy + qzz - qyz),
        ]
        new = [(0, jnp.where(fluid, W0 * base, W0))]
        new += [(INDEX[(0, cy, cz)], flat[k]) for k, (cy, cz) in enumerate(IN_PLANE)]
        new += [(pick(inward[k], p), new_in[k]) for k in range(5)]
        new += [(pick(outward[k], p), new_out[k]) for k in range(5)]
        return mass_new, new, new_out

    def close(t, p):
        def corners():
            for u in (0, 1):
                x_corner(t, p, u, (p, u)).wait_recv()

        if t == 0:
            x_code(p, p).wait_recv()
            for h in (0, 1):
                interior(0, p, h, rc[p, :, half(h)])
            corners()

            @pl.when(late & (p == sides[1]))
            def _():
                open_side(p)

            far_codes(0, p)
            for c, (z, h) in enumerate(CHUNKS):
                x_chunk(0, p, c, p).wait_recv()
                sources = [rx[0, p, c, k] for k in range(5)]
                lane = lax.broadcasted_iota(jnp.int32, sources[0].shape, 1)
                k, edge, u = (1, lane == 0, 0) if h == 0 else (2, lane == LANES - 1, 1)
                column = jnp.broadcast_to(rk[0, p, u][:, z : z + 1], lane.shape)
                sources[k] = jnp.where(edge, column, sources[k])
                z, lanes = rows(z), half(h)
                mass_new, new, new_out = finish(0, p, z, lanes, sources)
                code_new = code_of(flags[1, p, z, lanes], mass_new)
                for k in range(5):
                    sx[1, p, c, k] = new_out[k]
                sx[1, p, c, 5] = code_new
                code[1, p, z, lanes] = code_new
                for q, value in new:
                    pops[1, q, p, z, lanes] = value
                if c % 2 == 1:
                    fill_corner(1, p, h)
                    x_corner(1, p, h, (1 - p, 1 - h)).start()
                x_chunk(1, p, c, 1 - p).start()
                mass[1, p, z, lanes] = mass_new
            return
        for h in (0, 1):
            for z in (0, 1):
                x_chunk(1, p, 2 * h + z, p).wait_recv()
            interior(1, p, h, jnp.concatenate([rx[1, p, 2 * h, 5], rx[1, p, 2 * h + 1, 5]], axis=0))
        corners()
        far_codes(1, p)
        beyond = []
        for k, (cy, cz) in enumerate(OFFS):
            halves = [jnp.concatenate([rx[1, p, 2 * h, k], rx[1, p, 2 * h + 1, k]], axis=0) for h in (0, 1)]
            if cy:
                halves = shift_y(halves, cy, spread(rk[1, p, 0 if cy == 1 else 1], 0))
            if cz:
                halves = shift_z(halves, cz)
            beyond.append(halves)
        for h in (0, 1):
            lanes = half(h)
            mass_new, new, _ = finish(1, p, slice(None), lanes, [halves[h] for halves in beyond])
            mass_out[p, :, lanes] = mass_new
            for q, value in new:
                pops_out[q, p, :, lanes] = value

    for t in (0, 1):
        for u in (0, 1):
            y_tile(t, u, u).wait_recv()
        if t == 0:

            for u, answers in enumerate((answers_down, answers_up)):

                @pl.when(answers)
                def _(u=u):
                    y_tile(0, u, 1 - u).start()

        if t == 0:
            @pl.when(early & first)
            def _():
                to_relay_corner(0).start()

        stream(t)

        if t == 0:

            @pl.when(early)
            def _():
                pl.semaphore_wait(go_sem, 1)
                for i, arrival in enumerate(arrivals()):
                    arrival.wait_recv()
                    onward(i).start()

        @pl.loop(0, 2)
        def _(i, t=t):
            close(t, lax.rem(gx + 1 + i, 2))

        if t == 0:
            fill_y(1)
            for u in (0, 1):
                y_tile(1, u, 1 - u).start()

    @pl.when(early)
    def _():
        for i in range(7):
            onward(i).wait_send()

    for d in (0, 1):
        x_code(d, 1 - d).wait_send()
        for t in (0, 1):
            for c in range(4):
                x_chunk(t, d, c, 1 - d).wait_send()
            for u in (0, 1):
                x_corner(t, d, u, (1 - d, 1 - u)).wait_send()
            y_tile(t, d, 1 - d).wait_send()


def write_back(pops, mass, pops_out, mass_out, sem):
    copies = [
        pltpu.make_async_copy(pops, pops_out, sem.at[0]),
        pltpu.make_async_copy(mass, mass_out, sem.at[1]),
    ]
    for copy in copies:
        copy.start()
    for copy in copies:
        copy.wait()


def on_device(populations, mass, flags, relax):
    _, planes, depth, width = populations.shape
    tile, plane = (ROWS, LANES), (depth, width)
    f32 = jnp.float32
    vmem, dma = pltpu.VMEM, pltpu.SemaphoreType.DMA
    state_shape = (
        jax.ShapeDtypeStruct(populations.shape, f32),
        jax.ShapeDtypeStruct(mass.shape, f32),
    )
    hbm = pl.BlockSpec(memory_space=pltpu.HBM)
    here = pl.BlockSpec(memory_space=pltpu.VMEM)
    args = [pltpu.with_memory_space_constraint(a, pltpu.HBM) for a in (populations, mass, flags, relax)]
    state = pl.pallas_call(
        kernel,
        out_shape=state_shape,
        in_specs=[hbm] * 4,
        out_specs=(here, here),
        scratch_shapes=[
            vmem((2, 19, planes, *plane), f32),
            vmem((2, planes, *plane), f32),
            vmem((2, planes, *plane), jnp.int32),
            vmem((planes, *plane), f32),
            vmem((2, planes, *plane), f32),
            vmem((planes, 8, *plane), f32),
            vmem((planes, 5, *plane), f32),
            vmem((planes, 3, 3, *plane), f32),
            vmem((2, 5, *plane), f32),
            vmem((planes, 14, *plane), f32),
            vmem((2, 2, 4, 6, *tile), f32),
            vmem((2, 2, 4, 6, *tile), f32),
            vmem((2, *plane), f32),
            vmem((2, *plane), f32),
            vmem((2, 2, *tile), f32),
            vmem((2, 2, *tile), f32),
            vmem((2, 2, 2, *tile), f32),
            vmem((2, 2, 2, *tile), f32),
            vmem((4, 5, *tile), f32),
            vmem(plane, f32),
            vmem((2, *tile), f32),
            dma((4,)),
            dma((2, 2, 4)),
            dma((2, 2, 4)),
            dma((2,)),
            dma((2,)),
            dma((2, 2)),
            dma((2, 2)),
            dma((2, 2, 2)),
            dma((2, 2, 2)),
            dma((4,)),
            dma((1,)),
            dma((2,)),
            dma((7,)),
            pltpu.SemaphoreType.REGULAR,
        ],
        compiler_params=pltpu.CompilerParams(
            collective_id=0, has_side_effects=True, vmem_limit_bytes=32 * 1024 * 1024
        ),
        name="lattice_steps",
    )(*args)
    anywhere = pl.BlockSpec(memory_space=pl.ANY)
    return pl.pallas_call(
        write_back,
        out_shape=state_shape,
        in_specs=[here] * 2,
        out_specs=(anywhere,) * 2,
        scratch_shapes=[dma((2,))],
        name="write_back",
    )(*(pltpu.with_memory_space_constraint(a, pltpu.VMEM) for a in state))


def solution(mesh):
    return jax.shard_map(
        on_device,
        mesh=mesh,
        in_specs=(
            P(None, "gx", None, "gy"),
            P("gx", None, "gy"),
            P(None, "gx", None, "gy"),
            P("gx", None, "gy"),
        ),
        out_specs=(P(None, "gx", None, "gy"), P("gx", None, "gy")),
        check_vma=False,
    )
```

```python
import jax
import jax.numpy as jnp
from jax import lax
from jax.experimental import pallas as pl
from jax.experimental.pallas import tpu as pltpu
from jax.sharding import PartitionSpec as P

MESH = pl.DeviceIdType.MESH

VEL = [
    (0, 0, 0),
    (1, 0, 0),
    (-1, 0, 0),
    (0, 1, 0),
    (0, -1, 0),
    (0, 0, 1),
    (0, 0, -1),
    (1, 1, 0),
    (-1, -1, 0),
    (1, -1, 0),
    (-1, 1, 0),
    (1, 0, 1),
    (-1, 0, -1),
    (1, 0, -1),
    (-1, 0, 1),
    (0, 1, 1),
    (0, -1, -1),
    (0, 1, -1),
    (0, -1, 1),
]
INDEX = {c: q for q, c in enumerate(VEL)}
OPP = [INDEX[(-a, -b, -c)] for a, b, c in VEL]
W0, W1, W2 = 1.0 / 3.0, 1.0 / 18.0, 1.0 / 36.0
WEIGHT = [W0] + [W1] * 6 + [W2] * 12
SIGMA = 0.02
OFFS = [(0, 0), (1, 0), (-1, 0), (0, 1), (0, -1)]
IN_PLANE = [(1, 0), (-1, 0), (0, 1), (0, -1), (1, 1), (-1, -1), (1, -1), (-1, 1)]
LANES = 128
ROWS = 8


OPP_OFFS = [0, 2, 1, 4, 3]
CHUNKS = [(zh, h) for h in (0, 1) for zh in (0, 1)]
ORDER = (2, 3, 0, 1)


def side_dirs(cx):
    return [INDEX[(cx, b, c)] for b, c in OFFS]


def y_columns(cy):
    cols = []
    for plane in (0, 1):
        for cz in (0, 1, -1):
            cols.append((INDEX[(0, cy, cz)], plane))
        cols.append((INDEX[(1 - 2 * plane, cy, 0)], plane))
        cols.append((None, plane))
    return cols


def frac_of(e):
    return jnp.where(e == 1.0, 1.0, jnp.where(e > 1.5, e - 2.0, 0.0))


def code_of(kind, mass):
    return jnp.where(kind == 3, -1.0, jnp.where(kind == 0, 0.0, jnp.where(kind == 2, 1.0, 2.0 + mass)))


def half(h):
    return slice(h * LANES, (h + 1) * LANES)


def shift_y(halves, cy, column):
    lane = lax.broadcasted_iota(jnp.int32, halves[0].shape, 1)
    if cy == 1:
        moved = [pltpu.roll(a, 1, 1) for a in halves]
        edge = lane == 0
        return [jnp.where(edge, column, moved[0]), jnp.where(edge, moved[0], moved[1])]
    moved = [pltpu.roll(a, LANES - 1, 1) for a in halves]
    edge = lane == LANES - 1
    return [jnp.where(edge, moved[1], moved[0]), jnp.where(edge, column, moved[1])]


def shift_z(halves, cz):
    depth = halves[0].shape[0]
    return [pltpu.roll(a, cz % depth, 0) for a in halves]


def wall_z(halves, cz):
    row = lax.broadcasted_iota(jnp.int32, halves[0].shape, 0)
    outside = row == (0 if cz == 1 else halves[0].shape[0] - 1)
    return [jnp.where(outside, -1.0, a) for a in shift_z(halves, cz)]


def rows(z):
    return slice(z * ROWS, (z + 1) * ROWS)


def spread(tile, k):
    low, high = tile[:, 2 * k : 2 * k + 1], tile[:, 2 * k + 1 : 2 * k + 2]
    return jnp.concatenate([jnp.broadcast_to(low, tile.shape), jnp.broadcast_to(high, tile.shape)], axis=0)


def pack(columns):
    lane = lax.broadcasted_iota(jnp.int32, (ROWS, LANES), 1)
    tile = jnp.zeros(lane.shape, jnp.float32)
    for k, column in enumerate(columns):
        for z in (0, 1):
            tile = jnp.where(lane == 2 * k + z, jnp.broadcast_to(column[rows(z)], lane.shape), tile)
    return tile


def kernel(
    pops_in,
    mass_in,
    flags_in,
    relax_in,
    pops_out,
    mass_out,
    pops,
    mass,
    flags,
    relax,
    code,
    inner,
    cross,
    near,
    far,
    part,
    sx,
    rx,
    sc,
    rc,
    sy,
    ry,
    sk,
    rk,
    held_x,
    held_c,
    held_k,
    load_sem,
    sx_sem,
    rx_sem,
    sc_sem,
    rc_sem,
    sy_sem,
    ry_sem,
    sk_sem,
    rk_sem,
    held_x_sem,
    held_c_sem,
    held_k_sem,
    on_sem,
    go_sem,
):
    nx, ny = lax.axis_size("gx"), lax.axis_size("gy")
    gx, gy = lax.axis_index("gx"), lax.axis_index("gy")
    ys = [lax.rem(gy + ny - 1, ny), gy, lax.rem(gy + 1, ny)]
    parity = lax.rem(gx, 2)
    sides = [parity, 1 - parity]
    place = lax.rem(gx, 8)
    early = (place == 0) | (place == 3)
    late = (place == 4) | (place == 7)

    def peer(dx, u):
        return (lax.rem(gx + dx + nx, nx), ys[u + 1])

    def device(d, u):
        return peer(2 * d - 1, u)

    relay, relayed, beyond_relay = 2 * parity - 5, 3 + 2 * parity, 4

    odd, last = lax.rem(gy, 2) == 1, gy == ny - 1
    first = gy == 0
    answers_up = late & odd & jnp.logical_not(last)
    answers_down = late & (odd | first)
    barrier = pltpu.get_barrier_semaphore()

    def greet(when, *devices):
        @pl.when(when)
        def _():
            for other in devices:
                pl.semaphore_signal(barrier, inc=1, device_id=other, device_id_type=MESH)

    greet(jnp.logical_not(late), *[device(sides[0], u) for u in (0, -1, 1)])
    greet(early, peer(beyond_relay, 0), peer(relayed, 0), peer(relayed, -1))
    greet(early & jnp.logical_not(last), peer(relayed, 1))
    greet(jnp.logical_not(late) | answers_down, peer(0, -1))
    greet(jnp.logical_not(late) | answers_up, peer(0, 1))
    greet((place != 5) & (place != 6), *[device(sides[1], u) for u in (0, -1, 1)])
    loads = [
        pltpu.make_async_copy(mass_in, mass.at[0], load_sem.at[0]),
        pltpu.make_async_copy(flags_in, flags, load_sem.at[1]),
        pltpu.make_async_copy(pops_in, pops.at[0], load_sem.at[2]),
        pltpu.make_async_copy(relax_in, relax, load_sem.at[3]),
    ]
    for load in loads:
        load.start()

    fewer = 2 * late.astype(jnp.int32) + answers_up.astype(jnp.int32) + answers_down.astype(jnp.int32)
    greeted = 8 - fewer - (early & first).astype(jnp.int32)

    @pl.when(late)
    def _():
        pl.semaphore_wait(barrier, greeted)
        pl.semaphore_signal(go_sem, inc=1, device_id=peer(-beyond_relay, 0), device_id_type=MESH)

    def x_code(d, at):
        return pltpu.make_async_remote_copy(
            sc.at[d], rc.at[at], sc_sem.at[d], rc_sem.at[at], device_id=device(d, 0), device_id_type=MESH
        )

    def x_chunk(t, d, c, at):
        count = pl.ds(0, 5 + t)
        return pltpu.make_async_remote_copy(
            sx.at[t, d, c, count],
            rx.at[t, at, c, count],
            sx_sem.at[t, d, c],
            rx_sem.at[t, at, c],
            device_id=device(d, 0),
            device_id_type=MESH,
        )

    def x_corner(t, d, u, at):
        return pltpu.make_async_remote_copy(
            sk.at[t, d, u],
            rk.at[t, at[0], at[1]],
            sk_sem.at[t, d, u],
            rk_sem.at[t, at[0], at[1]],
            device_id=device(d, 2 * u - 1),
            device_id_type=MESH,
        )

    def y_tile(t, u, at):
        return pltpu.make_async_remote_copy(
            sy.at[t, u], ry.at[t, at], sy_sem.at[t, u], ry_sem.at[t, at], device_id=(gx, ys[2 * u]), device_id_type=MESH
        )

    def to_relay(src, dst, send, recv, u=0):
        return pltpu.make_async_remote_copy(
            src, dst, send, recv, device_id=peer(relay, u), device_id_type=MESH
        )

    def to_relay_corner(u):
        d = parity
        return to_relay(sk.at[0, d, u], held_k.at[1 - u], sk_sem.at[0, d, u], held_k_sem.at[1 - u], 2 * u - 1)

    def to_relay_code():
        return to_relay(sc.at[parity], held_c, sc_sem.at[parity], held_c_sem.at[0])

    def to_relay_chunk(c):
        d, count = parity, pl.ds(0, 5)
        return to_relay(sx.at[0, d, c, count], held_x.at[c], sx_sem.at[0, d, c], held_x_sem.at[c])

    def arrivals():
        return [to_relay_corner(1), to_relay_corner(0), to_relay_code()] + [to_relay_chunk(c) for c in ORDER]

    def onward(i):
        d, count = parity, pl.ds(0, 5)
        parts = [(held_k.at[u], rk.at[0, d, u], rk_sem.at[0, d, u]) for u in (0, 1)]
        parts.append((held_c, rc.at[d], rc_sem.at[d]))
        parts += [(held_x.at[c], rx.at[0, d, c, count], rx_sem.at[0, d, c]) for c in ORDER]
        src, dst, recv = parts[i]
        return pltpu.make_async_remote_copy(
            src, dst, on_sem.at[i], recv, device_id=peer(beyond_relay, 0), device_id_type=MESH
        )

    def pick(pair, p):
        return pair[0] + p * (pair[1] - pair[0])

    plus, minus = side_dirs(1), side_dirs(-1)
    inward = list(zip(plus, minus))
    outward = list(zip(minus, plus))

    def rim_of(t, q, p, u):
        at = 0 if u == 0 else 2 * LANES - 1
        if q is None:
            return code[t, p, :, at : at + 1]
        return pops[t, q, p, :, at : at + 1]

    def fill_y(t):
        for u in (0, 1):
            sy[t, u] = pack([rim_of(t, q, p, u) for q, p in y_columns(2 * u - 1)])

    def fill_corner(t, p, u):
        q = pick(outward[2 - u], p)
        sk[t, p, u] = pack([rim_of(t, q, p, u), rim_of(t, None, p, u)])

    loads[0].wait()
    loads[1].wait()
    for p in (0, 1):
        code[0, p] = code_of(flags[0, p], mass[0, p])
        sc[p] = code[0, p]
    loads[2].wait()
    for p in (0, 1):
        for u in (0, 1):
            fill_corner(0, p, u)
        for k, (cy, cz) in enumerate(OFFS):
            halves = [pops[0, outward[k][p], p, :, half(h)] for h in (0, 1)]
            if cy:
                halves = shift_y(halves, cy, halves[0])
            if cz:
                halves = shift_z(halves, cz)
            for c, (z, h) in enumerate(CHUNKS):
                sx[0, p, c, k] = halves[h][rows(z)]
    fill_y(0)
    loads[3].wait()

    @pl.when(jnp.logical_not(late))
    def _():
        pl.semaphore_wait(barrier, greeted)

    def open_side(d):
        for u in (0, 1):
            x_corner(0, d, u, (1 - d, 1 - u)).start()
        x_code(d, 1 - d).start()
        for c in ORDER:
            x_chunk(0, d, c, 1 - d).start()

    @pl.when(early & jnp.logical_not(first))
    def _():
        to_relay_corner(0).start()

    @pl.when(early)
    def _():
        to_relay_corner(1).start()
        to_relay_code().start()
        for c in ORDER:
            to_relay_chunk(c).start()

    @pl.when(jnp.logical_not(early))
    def _():
        open_side(sides[0])

    for u, answers in enumerate((answers_down, answers_up)):

        @pl.when(jnp.logical_not(answers))
        def _(u=u):
            y_tile(0, u, 1 - u).start()

    @pl.when(jnp.logical_not(late))
    def _():
        open_side(sides[1])

    def stream(t):
        place = [{c: k for k, c in enumerate(y_columns(cy))} for cy in (1, -1)]

        def column(q, p, cy):
            u = 0 if cy == 1 else 1
            return spread(ry[t, u], place[u][(q, p)])

        def moved(q, p, cy, cz):
            halves = [pops[t, q, p, :, half(h)] for h in (0, 1)]
            if cy:
                halves = shift_y(halves, cy, column(q, p, cy))
            if cz:
                halves = shift_z(halves, cz)
            return halves

        for p in (0, 1):
            own = [code[t, p, :, half(h)] for h in (0, 1)]
            table = {(0, 0): own}
            for cy in (1, -1):
                table[(cy, 0)] = shift_y(own, cy, column(None, p, cy))
            for cy in (0, 1, -1):
                for cz in (1, -1):
                    table[(cy, cz)] = wall_z(table[(cy, 0)], cz)
            for (cy, cz), halves in table.items():
                for h in (0, 1):
                    near[p, cy + 1, cz + 1, :, half(h)] = halves[h]
            for k, (cy, cz) in enumerate(IN_PLANE):
                halves = moved(INDEX[(0, cy, cz)], p, cy, cz)
                for h in (0, 1):
                    inner[p, k, :, half(h)] = halves[h]
            for k, (cy, cz) in enumerate(OFFS):
                halves = moved(outward[k][p], 1 - p, cy, cz)
                for h in (0, 1):
                    cross[p, k, :, half(h)] = halves[h]

    def plane_code(t, p):
        if t == 0:
            return [rc[p, :, half(h)] for h in (0, 1)]
        return [jnp.concatenate([rx[1, p, 2 * h, 5], rx[1, p, 2 * h + 1, 5]], axis=0) for h in (0, 1)]

    def far_codes(t, p):
        own = plane_code(t, p)
        for k, (cy, cz) in enumerate(OFFS):
            halves = own
            if cy:
                halves = shift_y(own, cy, spread(rk[t, p, 0 if cy == 1 else 1], 1))
            if cz:
                halves = wall_z(own, cz)
            for h in (0, 1):
                far[p, k, :, half(h)] = halves[h]

    def arrive(e, s, r, rebuilt, m):
        g = jnp.where(e == -1.0, r, jnp.where(e == 0.0, rebuilt - r, s))
        a = jnp.where(e == 1.0, 1.0, jnp.where(e > 1.5, 0.5 * (m + (e - 2.0)), 0.0))
        return g, a * (s - r)

    def side_moments(g):
        total = (g[0] + g[1]) + (g[2] + (g[3] + g[4]))
        return [total, g[1] - g[2], g[3] - g[4], g[1] + g[2], g[3] + g[4]]

    def interior(t, p, h, x_far):
        lanes = half(h)
        kind, m = flags[t, p, :, lanes], mass[t, p, :, lanes]
        rest = pops[t, 0, p, :, lanes]
        flat = [pops[t, INDEX[(0, cy, cz)], p, :, lanes] for cy, cz in IN_PLANE]
        fin = [pops[t, pick(inward[k], p), p, :, lanes] for k in range(5)]
        fout = [pops[t, pick(outward[k], p), p, :, lanes] for k in range(5)]
        tin, yin, zin, _, _ = side_moments(fin)
        tout, yout, zout, _, _ = side_moments(fout)
        pp, mm, pm, mp = flat[4:]
        ax = tin - tout
        ay = (yin + yout) + (flat[0] - flat[1]) + (pp - mm) + (pm - mp)
        az = (zin + zout) + (flat[2] - flat[3]) + (pp - mm) - (pm - mp)
        own = jnp.where(kind == 2, 1.0, jnp.where(kind == 1, m, 0.0))
        around = frac_of(x_far) + frac_of(near[1 - p, 1, 1, :, lanes])
        for cy, cz in OFFS[1:]:
            around = around + frac_of(near[p, cy + 1, cz + 1, :, lanes])
        gas = 1.0 - 3.0 * SIGMA * (around - 6.0 * own)
        lift = 2.0 * gas - 3.0 * (ax * ax + ay * ay + az * az)

        dm = jnp.zeros_like(m)
        e0 = near[p, 1, 1, :, lanes]
        g0 = jnp.where(e0 == 0.0, W0 * lift - rest, rest)
        g = []
        for k, (cy, cz) in enumerate(IN_PLANE):
            proj = sum(c * j for c, j in ((cy, ay), (cz, az)) if c)
            w = W2 if cy and cz else W1
            value, moved = arrive(
                near[p, cy + 1, cz + 1, :, lanes],
                inner[p, k, :, lanes],
                flat[k ^ 1],
                w * (lift + 9.0 * (proj * proj)),
                m,
            )
            g.append(value)
            dm = dm + moved
        out = []
        for k, (cy, cz) in enumerate(OFFS):
            proj = -ax + sum(c * j for c, j in ((cy, ay), (cz, az)) if c)
            w = W2 if cy or cz else W1
            value, moved = arrive(
                near[1 - p, cy + 1, cz + 1, :, lanes],
                cross[p, k, :, lanes],
                fin[OPP_OFFS[k]],
                w * (lift + 9.0 * (proj * proj)),
                m,
            )
            out.append(value)
            dm = dm + moved
        total, dy, dz, yy2, zz2 = side_moments(out)
        pp, mm, pm, mp = g[4:]
        diag, anti = pp + mm, pm + mp
        yy, zz = g[0] + g[1], g[2] + g[3]
        rho = total + g0 + yy + zz + (diag + anti)
        jy = dy + (g[0] - g[1]) + (pp - mm) + (pm - mp)
        jz = dz + (g[2] - g[3]) + (pp - mm) - (pm - mp)
        pyy = yy2 + yy + (diag + anti)
        pzz = zz2 + zz + (diag + anti)
        kept = (rho, total, jy, jz, pyy, pzz, dy, dz, diag - anti, dm, lift, ax, ay, az)
        for k, value in enumerate(kept):
            part[p, k, :, lanes] = value

    def finish(t, p, z, lanes, sources):
        kind, m = flags[t, p, z, lanes], mass[t, p, z, lanes]
        rho, tout, jy, jz, pyy, pzz, dyout, dzout, pyz, dm, lift, ax, ay, az = (
            part[p, k, z, lanes] for k in range(14)
        )
        g = []
        for k, (cy, cz) in enumerate(OFFS):
            proj = ax + sum(c * j for c, j in ((cy, ay), (cz, az)) if c)
            w = W2 if cy or cz else W1
            value, moved = arrive(
                far[p, k, z, lanes],
                sources[k],
                pops[t, pick(outward[OPP_OFFS[k]], p), p, z, lanes],
                w * (lift + 9.0 * (proj * proj)),
                m,
            )
            g.append(value)
            dm = dm + moved
        total, dy, dz, yy2, zz2 = side_moments(g)
        rho, jx, pxx = rho + total, total - tout, total + tout
        jy, jz, pyy, pzz = jy + dy, jz + dz, pyy + yy2, pzz + zz2
        pxy, pxz = dy - dyout, dz - dzout
        is_face, is_liquid = kind == 1, kind == 2
        mass_new = jnp.where(is_face, m + dm, jnp.where(is_liquid, rho, 0.0))
        fluid = is_face | is_liquid
        third = rho * (1.0 / 3.0)
        xx, yy, zz = jx * jx, jy * jy, jz * jz
        strength = (1.0 - relax[p, z, lanes]) * 4.5
        qxx, qyy, qzz = pxx - third - xx, pyy - third - yy, pzz - third - zz
        mean = (qxx + qyy + qzz) * (1.0 / 3.0)
        qxx, qyy, qzz, mean = strength * qxx, strength * qyy, strength * qzz, strength * mean
        four = 4.0 * strength
        qxy, qxz, qyz = four * (pxy - jx * jy), four * (pxz - jx * jz), four * (pyz - jy * jz)
        base = rho - 1.5 * (xx + yy + zz) - mean

        def couple(w, proj, stress):
            even = w * (base + 4.5 * (proj * proj) + stress)
            odd = (3.0 * w) * proj
            return jnp.where(fluid, even + odd, w), jnp.where(fluid, even - odd, w)

        new_in, new_out = [None] * 5, [None] * 5
        new_in[0], new_out[0] = couple(W1, jx, qxx)
        new_in[1], new_out[2] = couple(W2, jx + jy, qxx + qyy + qxy)
        new_in[2], new_out[1] = couple(W2, jx - jy, qxx + qyy - qxy)
        new_in[3], new_out[4] = couple(W2, jx + jz, qxx + qzz + qxz)
        new_in[4], new_out[3] = couple(W2, jx - jz, qxx + qzz - qxz)
        flat = [
            *couple(W1, jy, qyy),
            *couple(W1, jz, qzz),
            *couple(W2, jy + jz, qyy + qzz + qyz),
            *couple(W2, jy - jz, qyy + qzz - qyz),
        ]
        new = [(0, jnp.where(fluid, W0 * base, W0))]
        new += [(INDEX[(0, cy, cz)], flat[k]) for k, (cy, cz) in enumerate(IN_PLANE)]
        new += [(pick(inward[k], p), new_in[k]) for k in range(5)]
        new += [(pick(outward[k], p), new_out[k]) for k in range(5)]
        return mass_new, new, new_out

    def close(t, p):
        def corners():
            for u in (0, 1):
                x_corner(t, p, u, (p, u)).wait_recv()

        if t == 0:
            x_code(p, p).wait_recv()
            for h in (0, 1):
                interior(0, p, h, rc[p, :, half(h)])
            corners()

            @pl.when(late & (p == sides[1]))
            def _():
                open_side(p)

            far_codes(0, p)
            for c in ORDER:
                z, h = CHUNKS[c]
                x_chunk(0, p, c, p).wait_recv()
                sources = [rx[0, p, c, k] for k in range(5)]
                lane = lax.broadcasted_iota(jnp.int32, sources[0].shape, 1)
                k, edge, u = (1, lane == 0, 0) if h == 0 else (2, lane == LANES - 1, 1)
                column = jnp.broadcast_to(rk[0, p, u][:, z : z + 1], lane.shape)
                sources[k] = jnp.where(edge, column, sources[k])
                z, lanes = rows(z), half(h)
                mass_new, new, new_out = finish(0, p, z, lanes, sources)
                code_new = code_of(flags[1, p, z, lanes], mass_new)
                for k in range(5):
                    sx[1, p, c, k] = new_out[k]
                sx[1, p, c, 5] = code_new
                code[1, p, z, lanes] = code_new
                for q, value in new:
                    pops[1, q, p, z, lanes] = value
                if c % 2 == 1:
                    fill_corner(1, p, h)
                    x_corner(1, p, h, (1 - p, 1 - h)).start()
                x_chunk(1, p, c, 1 - p).start()
                mass[1, p, z, lanes] = mass_new
            return
        for h in (1, 0):
            for z in (0, 1):
                x_chunk(1, p, 2 * h + z, p).wait_recv()
            interior(1, p, h, jnp.concatenate([rx[1, p, 2 * h, 5], rx[1, p, 2 * h + 1, 5]], axis=0))
        corners()
        far_codes(1, p)
        beyond = []
        for k, (cy, cz) in enumerate(OFFS):
            halves = [jnp.concatenate([rx[1, p, 2 * h, k], rx[1, p, 2 * h + 1, k]], axis=0) for h in (0, 1)]
            if cy:
                halves = shift_y(halves, cy, spread(rk[1, p, 0 if cy == 1 else 1], 0))
            if cz:
                halves = shift_z(halves, cz)
            beyond.append(halves)
        for h in (0, 1):
            lanes = half(h)
            mass_new, new, _ = finish(1, p, slice(None), lanes, [halves[h] for halves in beyond])
            mass_out[p, :, lanes] = mass_new
            for q, value in new:
                pops_out[q, p, :, lanes] = value

    for t in (0, 1):
        for u in (0, 1):
            y_tile(t, u, u).wait_recv()
        if t == 0:

            for u, answers in enumerate((answers_down, answers_up)):

                @pl.when(answers)
                def _(u=u):
                    y_tile(0, u, 1 - u).start()

        if t == 0:
            @pl.when(early & first)
            def _():
                to_relay_corner(0).start()

        stream(t)

        if t == 0:

            @pl.when(early)
            def _():
                pl.semaphore_wait(go_sem, 1)
                for i, arrival in enumerate(arrivals()):
                    arrival.wait_recv()
                    onward(i).start()

        @pl.loop(0, 2)
        def _(i, t=t):
            close(t, lax.rem(gx + 1 + i, 2))

        if t == 0:
            fill_y(1)
            for u in (0, 1):
                y_tile(1, u, 1 - u).start()

    @pl.when(early)
    def _():
        for i in range(7):
            onward(i).wait_send()

    for d in (0, 1):
        x_code(d, 1 - d).wait_send()
        for t in (0, 1):
            for c in range(4):
                x_chunk(t, d, c, 1 - d).wait_send()
            for u in (0, 1):
                x_corner(t, d, u, (1 - d, 1 - u)).wait_send()
            y_tile(t, d, 1 - d).wait_send()


def write_back(pops, mass, pops_out, mass_out, sem):
    copies = [
        pltpu.make_async_copy(pops, pops_out, sem.at[0]),
        pltpu.make_async_copy(mass, mass_out, sem.at[1]),
    ]
    for copy in copies:
        copy.start()
    for copy in copies:
        copy.wait()


def on_device(populations, mass, flags, relax):
    _, planes, depth, width = populations.shape
    tile, plane = (ROWS, LANES), (depth, width)
    f32 = jnp.float32
    vmem, dma = pltpu.VMEM, pltpu.SemaphoreType.DMA
    state_shape = (
        jax.ShapeDtypeStruct(populations.shape, f32),
        jax.ShapeDtypeStruct(mass.shape, f32),
    )
    hbm = pl.BlockSpec(memory_space=pltpu.HBM)
    here = pl.BlockSpec(memory_space=pltpu.VMEM)
    args = [pltpu.with_memory_space_constraint(a, pltpu.HBM) for a in (populations, mass, flags, relax)]
    state = pl.pallas_call(
        kernel,
        out_shape=state_shape,
        in_specs=[hbm] * 4,
        out_specs=(here, here),
        scratch_shapes=[
            vmem((2, 19, planes, *plane), f32),
            vmem((2, planes, *plane), f32),
            vmem((2, planes, *plane), jnp.int32),
            vmem((planes, *plane), f32),
            vmem((2, planes, *plane), f32),
            vmem((planes, 8, *plane), f32),
            vmem((planes, 5, *plane), f32),
            vmem((planes, 3, 3, *plane), f32),
            vmem((2, 5, *plane), f32),
            vmem((planes, 14, *plane), f32),
            vmem((2, 2, 4, 6, *tile), f32),
            vmem((2, 2, 4, 6, *tile), f32),
            vmem((2, *plane), f32),
            vmem((2, *plane), f32),
            vmem((2, 2, *tile), f32),
            vmem((2, 2, *tile), f32),
            vmem((2, 2, 2, *tile), f32),
            vmem((2, 2, 2, *tile), f32),
            vmem((4, 5, *tile), f32),
            vmem(plane, f32),
            vmem((2, *tile), f32),
            dma((4,)),
            dma((2, 2, 4)),
            dma((2, 2, 4)),
            dma((2,)),
            dma((2,)),
            dma((2, 2)),
            dma((2, 2)),
            dma((2, 2, 2)),
            dma((2, 2, 2)),
            dma((4,)),
            dma((1,)),
            dma((2,)),
            dma((7,)),
            pltpu.SemaphoreType.REGULAR,
        ],
        compiler_params=pltpu.CompilerParams(
            collective_id=0, has_side_effects=True, vmem_limit_bytes=32 * 1024 * 1024
        ),
        name="lattice_steps",
    )(*args)
    anywhere = pl.BlockSpec(memory_space=pl.ANY)
    return pl.pallas_call(
        write_back,
        out_shape=state_shape,
        in_specs=[here] * 2,
        out_specs=(anywhere,) * 2,
        scratch_shapes=[dma((2,))],
        name="write_back",
    )(*(pltpu.with_memory_space_constraint(a, pltpu.VMEM) for a in state))


def solution(mesh):
    return jax.shard_map(
        on_device,
        mesh=mesh,
        in_specs=(
            P(None, "gx", None, "gy"),
            P("gx", None, "gy"),
            P(None, "gx", None, "gy"),
            P("gx", None, "gy"),
        ),
        out_specs=(P(None, "gx", None, "gy"), P("gx", None, "gy")),
        check_vma=False,
    )
```

```python
import jax
import jax.numpy as jnp
from jax import lax
from jax.experimental import pallas as pl
from jax.experimental.pallas import tpu as pltpu
from jax.sharding import PartitionSpec as P

MESH = pl.DeviceIdType.MESH

VEL = [
    (0, 0, 0),
    (1, 0, 0),
    (-1, 0, 0),
    (0, 1, 0),
    (0, -1, 0),
    (0, 0, 1),
    (0, 0, -1),
    (1, 1, 0),
    (-1, -1, 0),
    (1, -1, 0),
    (-1, 1, 0),
    (1, 0, 1),
    (-1, 0, -1),
    (1, 0, -1),
    (-1, 0, 1),
    (0, 1, 1),
    (0, -1, -1),
    (0, 1, -1),
    (0, -1, 1),
]
INDEX = {c: q for q, c in enumerate(VEL)}
OPP = [INDEX[(-a, -b, -c)] for a, b, c in VEL]
W0, W1, W2 = 1.0 / 3.0, 1.0 / 18.0, 1.0 / 36.0
WEIGHT = [W0] + [W1] * 6 + [W2] * 12
SIGMA = 0.02
OFFS = [(0, 0), (1, 0), (-1, 0), (0, 1), (0, -1)]
IN_PLANE = [(1, 0), (-1, 0), (0, 1), (0, -1), (1, 1), (-1, -1), (1, -1), (-1, 1)]
LANES = 128
ROWS = 8


OPP_OFFS = [0, 2, 1, 4, 3]
CHUNKS = [(zh, h) for h in (0, 1) for zh in (0, 1)]
ORDER = (2, 3, 0, 1)


def side_dirs(cx):
    return [INDEX[(cx, b, c)] for b, c in OFFS]


def y_columns(cy):
    cols = []
    for plane in (0, 1):
        for cz in (0, 1, -1):
            cols.append((INDEX[(0, cy, cz)], plane))
        cols.append((INDEX[(1 - 2 * plane, cy, 0)], plane))
        cols.append((None, plane))
    return cols


def frac_of(e):
    return jnp.where(e == 1.0, 1.0, jnp.where(e > 1.5, e - 2.0, 0.0))


def code_of(kind, mass):
    return jnp.where(kind == 3, -1.0, jnp.where(kind == 0, 0.0, jnp.where(kind == 2, 1.0, 2.0 + mass)))


def half(h):
    return slice(h * LANES, (h + 1) * LANES)


def shift_y(halves, cy, column):
    lane = lax.broadcasted_iota(jnp.int32, halves[0].shape, 1)
    if cy == 1:
        moved = [pltpu.roll(a, 1, 1) for a in halves]
        edge = lane == 0
        return [jnp.where(edge, column, moved[0]), jnp.where(edge, moved[0], moved[1])]
    moved = [pltpu.roll(a, LANES - 1, 1) for a in halves]
    edge = lane == LANES - 1
    return [jnp.where(edge, moved[1], moved[0]), jnp.where(edge, column, moved[1])]


def shift_z(halves, cz):
    depth = halves[0].shape[0]
    return [pltpu.roll(a, cz % depth, 0) for a in halves]


def wall_z(halves, cz):
    row = lax.broadcasted_iota(jnp.int32, halves[0].shape, 0)
    outside = row == (0 if cz == 1 else halves[0].shape[0] - 1)
    return [jnp.where(outside, -1.0, a) for a in shift_z(halves, cz)]


def rows(z):
    return slice(z * ROWS, (z + 1) * ROWS)


def spread(tile, k):
    low, high = tile[:, 2 * k : 2 * k + 1], tile[:, 2 * k + 1 : 2 * k + 2]
    return jnp.concatenate([jnp.broadcast_to(low, tile.shape), jnp.broadcast_to(high, tile.shape)], axis=0)


def pack(columns):
    lane = lax.broadcasted_iota(jnp.int32, (ROWS, LANES), 1)
    tile = jnp.zeros(lane.shape, jnp.float32)
    for k, column in enumerate(columns):
        for z in (0, 1):
            tile = jnp.where(lane == 2 * k + z, jnp.broadcast_to(column[rows(z)], lane.shape), tile)
    return tile


def kernel(
    pops_in,
    mass_in,
    flags_in,
    relax_in,
    pops_out,
    mass_out,
    pops,
    mass,
    flags,
    relax,
    code,
    inner,
    cross,
    near,
    far,
    part,
    sx,
    rx,
    sc,
    rc,
    sy,
    ry,
    sk,
    rk,
    held_x,
    held_c,
    held_k,
    load_sem,
    sx_sem,
    rx_sem,
    sc_sem,
    rc_sem,
    sy_sem,
    ry_sem,
    sk_sem,
    rk_sem,
    held_x_sem,
    held_c_sem,
    held_k_sem,
    on_sem,
    go_sem,
):
    nx, ny = lax.axis_size("gx"), lax.axis_size("gy")
    gx, gy = lax.axis_index("gx"), lax.axis_index("gy")
    ys = [lax.rem(gy + ny - 1, ny), gy, lax.rem(gy + 1, ny)]
    parity = lax.rem(gx, 2)
    sides = [parity, 1 - parity]
    place = lax.rem(gx, 8)
    early = (place == 0) | (place == 3)
    late = (place == 4) | (place == 7)

    def peer(dx, u):
        return (lax.rem(gx + dx + nx, nx), ys[u + 1])

    def device(d, u):
        return peer(2 * d - 1, u)

    relay, relayed, beyond_relay = 2 * parity - 5, 3 + 2 * parity, 4

    odd, last = lax.rem(gy, 2) == 1, gy == ny - 1
    first = gy == 0
    answers_up = late & odd & jnp.logical_not(last)
    answers_down = late & (odd | first)
    barrier = pltpu.get_barrier_semaphore()

    def greet(when, *devices):
        @pl.when(when)
        def _():
            for other in devices:
                pl.semaphore_signal(barrier, inc=1, device_id=other, device_id_type=MESH)

    greet(jnp.logical_not(late), *[device(sides[0], u) for u in (0, -1, 1)])
    greet(early, peer(beyond_relay, 0), peer(relayed, 0), peer(relayed, -1))
    greet(early & jnp.logical_not(last), peer(relayed, 1))
    greet(jnp.logical_not(late) | answers_down, peer(0, -1))
    greet(jnp.logical_not(late) | answers_up, peer(0, 1))
    greet((place != 5) & (place != 6), *[device(sides[1], u) for u in (0, -1, 1)])
    loads = [
        pltpu.make_async_copy(mass_in, mass.at[0], load_sem.at[0]),
        pltpu.make_async_copy(flags_in, flags, load_sem.at[1]),
        pltpu.make_async_copy(pops_in, pops.at[0], load_sem.at[2]),
        pltpu.make_async_copy(relax_in, relax, load_sem.at[3]),
    ]
    for load in loads:
        load.start()

    fewer = 2 * late.astype(jnp.int32) + answers_up.astype(jnp.int32) + answers_down.astype(jnp.int32)
    greeted = 8 - fewer - (early & first).astype(jnp.int32)

    @pl.when(late)
    def _():
        pl.semaphore_wait(barrier, greeted)
        pl.semaphore_signal(go_sem, inc=1, device_id=peer(-beyond_relay, 0), device_id_type=MESH)

    def x_code(d, at):
        return pltpu.make_async_remote_copy(
            sc.at[d], rc.at[at], sc_sem.at[d], rc_sem.at[at], device_id=device(d, 0), device_id_type=MESH
        )

    def x_chunk(t, d, c, at):
        count = pl.ds(0, 5 + t)
        return pltpu.make_async_remote_copy(
            sx.at[t, d, c, count],
            rx.at[t, at, c, count],
            sx_sem.at[t, d, c],
            rx_sem.at[t, at, c],
            device_id=device(d, 0),
            device_id_type=MESH,
        )

    def x_corner(t, d, u, at):
        return pltpu.make_async_remote_copy(
            sk.at[t, d, u],
            rk.at[t, at[0], at[1]],
            sk_sem.at[t, d, u],
            rk_sem.at[t, at[0], at[1]],
            device_id=device(d, 2 * u - 1),
            device_id_type=MESH,
        )

    def y_tile(t, u, at):
        return pltpu.make_async_remote_copy(
            sy.at[t, u], ry.at[t, at], sy_sem.at[t, u], ry_sem.at[t, at], device_id=(gx, ys[2 * u]), device_id_type=MESH
        )

    def to_relay(src, dst, send, recv, u=0):
        return pltpu.make_async_remote_copy(
            src, dst, send, recv, device_id=peer(relay, u), device_id_type=MESH
        )

    def to_relay_corner(u):
        d = parity
        return to_relay(sk.at[0, d, u], held_k.at[1 - u], sk_sem.at[0, d, u], held_k_sem.at[1 - u], 2 * u - 1)

    def to_relay_code():
        return to_relay(sc.at[parity], held_c, sc_sem.at[parity], held_c_sem.at[0])

    def to_relay_chunk(c):
        d, count = parity, pl.ds(0, 5)
        return to_relay(sx.at[0, d, c, count], held_x.at[c], sx_sem.at[0, d, c], held_x_sem.at[c])

    def arrivals():
        return [to_relay_corner(1), to_relay_corner(0), to_relay_code()] + [to_relay_chunk(c) for c in ORDER]

    def onward(i):
        d, count = parity, pl.ds(0, 5)
        parts = [(held_k.at[u], rk.at[0, d, u], rk_sem.at[0, d, u]) for u in (0, 1)]
        parts.append((held_c, rc.at[d], rc_sem.at[d]))
        parts += [(held_x.at[c], rx.at[0, d, c, count], rx_sem.at[0, d, c]) for c in ORDER]
        src, dst, recv = parts[i]
        return pltpu.make_async_remote_copy(
            src, dst, on_sem.at[i], recv, device_id=peer(beyond_relay, 0), device_id_type=MESH
        )

    def pick(pair, p):
        return pair[0] + p * (pair[1] - pair[0])

    plus, minus = side_dirs(1), side_dirs(-1)
    inward = list(zip(plus, minus))
    outward = list(zip(minus, plus))

    def rim_of(t, q, p, u):
        at = 0 if u == 0 else 2 * LANES - 1
        if q is None:
            return code[t, p, :, at : at + 1]
        return pops[t, q, p, :, at : at + 1]

    def fill_y(t):
        for u in (0, 1):
            sy[t, u] = pack([rim_of(t, q, p, u) for q, p in y_columns(2 * u - 1)])

    def fill_corner(t, p, u):
        q = pick(outward[2 - u], p)
        sk[t, p, u] = pack([rim_of(t, q, p, u), rim_of(t, None, p, u)])

    loads[0].wait()
    loads[1].wait()
    for p in (0, 1):
        code[0, p] = code_of(flags[0, p], mass[0, p])
        sc[p] = code[0, p]
    loads[2].wait()
    for p in (0, 1):
        for u in (0, 1):
            fill_corner(0, p, u)
        for k, (cy, cz) in enumerate(OFFS):
            halves = [pops[0, outward[k][p], p, :, half(h)] for h in (0, 1)]
            if cy:
                halves = shift_y(halves, cy, halves[0])
            if cz:
                halves = shift_z(halves, cz)
            for c, (z, h) in enumerate(CHUNKS):
                sx[0, p, c, k] = halves[h][rows(z)]
    fill_y(0)
    loads[3].wait()

    @pl.when(jnp.logical_not(late))
    def _():
        pl.semaphore_wait(barrier, greeted)

    def open_side(d):
        for u in (0, 1):
            x_corner(0, d, u, (1 - d, 1 - u)).start()
        x_code(d, 1 - d).start()
        for c in ORDER:
            x_chunk(0, d, c, 1 - d).start()

    @pl.when(early & jnp.logical_not(first))
    def _():
        to_relay_corner(0).start()

    @pl.when(early)
    def _():
        to_relay_corner(1).start()
        to_relay_code().start()
        for c in ORDER:
            to_relay_chunk(c).start()

    @pl.when(jnp.logical_not(early))
    def _():
        open_side(sides[0])

    for u, answers in enumerate((answers_down, answers_up)):

        @pl.when(jnp.logical_not(answers))
        def _(u=u):
            y_tile(0, u, 1 - u).start()

    @pl.when(jnp.logical_not(late))
    def _():
        open_side(sides[1])

    def stream(t):
        place = [{c: k for k, c in enumerate(y_columns(cy))} for cy in (1, -1)]

        def column(q, p, cy):
            u = 0 if cy == 1 else 1
            return spread(ry[t, u], place[u][(q, p)])

        def moved(q, p, cy, cz):
            halves = [pops[t, q, p, :, half(h)] for h in (0, 1)]
            if cy:
                halves = shift_y(halves, cy, column(q, p, cy))
            if cz:
                halves = shift_z(halves, cz)
            return halves

        for p in (0, 1):
            own = [code[t, p, :, half(h)] for h in (0, 1)]
            table = {(0, 0): own}
            for cy in (1, -1):
                table[(cy, 0)] = shift_y(own, cy, column(None, p, cy))
            for cy in (0, 1, -1):
                for cz in (1, -1):
                    table[(cy, cz)] = wall_z(table[(cy, 0)], cz)
            for (cy, cz), halves in table.items():
                for h in (0, 1):
                    near[p, cy + 1, cz + 1, :, half(h)] = halves[h]
            for k, (cy, cz) in enumerate(IN_PLANE):
                halves = moved(INDEX[(0, cy, cz)], p, cy, cz)
                for h in (0, 1):
                    inner[p, k, :, half(h)] = halves[h]
            for k, (cy, cz) in enumerate(OFFS):
                halves = moved(outward[k][p], 1 - p, cy, cz)
                for h in (0, 1):
                    cross[p, k, :, half(h)] = halves[h]

    def plane_code(t, p):
        if t == 0:
            return [rc[p, :, half(h)] for h in (0, 1)]
        return [jnp.concatenate([rx[1, p, 2 * h, 5], rx[1, p, 2 * h + 1, 5]], axis=0) for h in (0, 1)]

    def far_codes(t, p):
        own = plane_code(t, p)
        for k, (cy, cz) in enumerate(OFFS):
            halves = own
            if cy:
                halves = shift_y(own, cy, spread(rk[t, p, 0 if cy == 1 else 1], 1))
            if cz:
                halves = wall_z(own, cz)
            for h in (0, 1):
                far[p, k, :, half(h)] = halves[h]

    def arrive(e, s, r, rebuilt, m):
        g = jnp.where(e == -1.0, r, jnp.where(e == 0.0, rebuilt - r, s))
        a = jnp.where(e == 1.0, 1.0, jnp.where(e > 1.5, 0.5 * (m + (e - 2.0)), 0.0))
        return g, a * (s - r)

    def side_moments(g):
        total = (g[0] + g[1]) + (g[2] + (g[3] + g[4]))
        return [total, g[1] - g[2], g[3] - g[4], g[1] + g[2], g[3] + g[4]]

    def interior(t, p, h, x_far):
        lanes = half(h)
        kind, m = flags[t, p, :, lanes], mass[t, p, :, lanes]
        rest = pops[t, 0, p, :, lanes]
        flat = [pops[t, INDEX[(0, cy, cz)], p, :, lanes] for cy, cz in IN_PLANE]
        fin = [pops[t, pick(inward[k], p), p, :, lanes] for k in range(5)]
        fout = [pops[t, pick(outward[k], p), p, :, lanes] for k in range(5)]
        tin, yin, zin, _, _ = side_moments(fin)
        tout, yout, zout, _, _ = side_moments(fout)
        pp, mm, pm, mp = flat[4:]
        ax = tin - tout
        ay = (yin + yout) + (flat[0] - flat[1]) + (pp - mm) + (pm - mp)
        az = (zin + zout) + (flat[2] - flat[3]) + (pp - mm) - (pm - mp)
        own = jnp.where(kind == 2, 1.0, jnp.where(kind == 1, m, 0.0))
        around = frac_of(x_far) + frac_of(near[1 - p, 1, 1, :, lanes])
        for cy, cz in OFFS[1:]:
            around = around + frac_of(near[p, cy + 1, cz + 1, :, lanes])
        gas = 1.0 - 3.0 * SIGMA * (around - 6.0 * own)
        lift = 2.0 * gas - 3.0 * (ax * ax + ay * ay + az * az)

        dm = jnp.zeros_like(m)
        e0 = near[p, 1, 1, :, lanes]
        g0 = jnp.where(e0 == 0.0, W0 * lift - rest, rest)
        g = []
        for k, (cy, cz) in enumerate(IN_PLANE):
            proj = sum(c * j for c, j in ((cy, ay), (cz, az)) if c)
            w = W2 if cy and cz else W1
            value, moved = arrive(
                near[p, cy + 1, cz + 1, :, lanes],
                inner[p, k, :, lanes],
                flat[k ^ 1],
                w * (lift + 9.0 * (proj * proj)),
                m,
            )
            g.append(value)
            dm = dm + moved
        out = []
        for k, (cy, cz) in enumerate(OFFS):
            proj = -ax + sum(c * j for c, j in ((cy, ay), (cz, az)) if c)
            w = W2 if cy or cz else W1
            value, moved = arrive(
                near[1 - p, cy + 1, cz + 1, :, lanes],
                cross[p, k, :, lanes],
                fin[OPP_OFFS[k]],
                w * (lift + 9.0 * (proj * proj)),
                m,
            )
            out.append(value)
            dm = dm + moved
        total, dy, dz, yy2, zz2 = side_moments(out)
        pp, mm, pm, mp = g[4:]
        diag, anti = pp + mm, pm + mp
        yy, zz = g[0] + g[1], g[2] + g[3]
        rho = total + g0 + yy + zz + (diag + anti)
        jy = dy + (g[0] - g[1]) + (pp - mm) + (pm - mp)
        jz = dz + (g[2] - g[3]) + (pp - mm) - (pm - mp)
        pyy = yy2 + yy + (diag + anti)
        pzz = zz2 + zz + (diag + anti)
        kept = (rho, total, jy, jz, pyy, pzz, dy, dz, diag - anti, dm, lift, ax, ay, az)
        for k, value in enumerate(kept):
            part[p, k, :, lanes] = value

    def finish(t, p, z, lanes, sources):
        kind, m = flags[t, p, z, lanes], mass[t, p, z, lanes]
        rho, tout, jy, jz, pyy, pzz, dyout, dzout, pyz, dm, lift, ax, ay, az = (
            part[p, k, z, lanes] for k in range(14)
        )
        g = []
        for k, (cy, cz) in enumerate(OFFS):
            proj = ax + sum(c * j for c, j in ((cy, ay), (cz, az)) if c)
            w = W2 if cy or cz else W1
            value, moved = arrive(
                far[p, k, z, lanes],
                sources[k],
                pops[t, pick(outward[OPP_OFFS[k]], p), p, z, lanes],
                w * (lift + 9.0 * (proj * proj)),
                m,
            )
            g.append(value)
            dm = dm + moved
        total, dy, dz, yy2, zz2 = side_moments(g)
        rho, jx, pxx = rho + total, total - tout, total + tout
        jy, jz, pyy, pzz = jy + dy, jz + dz, pyy + yy2, pzz + zz2
        pxy, pxz = dy - dyout, dz - dzout
        is_face, is_liquid = kind == 1, kind == 2
        mass_new = jnp.where(is_face, m + dm, jnp.where(is_liquid, rho, 0.0))
        fluid = is_face | is_liquid
        third = rho * (1.0 / 3.0)
        xx, yy, zz = jx * jx, jy * jy, jz * jz
        strength = (1.0 - relax[p, z, lanes]) * 4.5
        qxx, qyy, qzz = pxx - third - xx, pyy - third - yy, pzz - third - zz
        mean = (qxx + qyy + qzz) * (1.0 / 3.0)
        qxx, qyy, qzz, mean = strength * qxx, strength * qyy, strength * qzz, strength * mean
        four = 4.0 * strength
        qxy, qxz, qyz = four * (pxy - jx * jy), four * (pxz - jx * jz), four * (pyz - jy * jz)
        base = rho - 1.5 * (xx + yy + zz) - mean

        def couple(w, proj, stress):
            even = w * (base + 4.5 * (proj * proj) + stress)
            odd = (3.0 * w) * proj
            return jnp.where(fluid, even + odd, w), jnp.where(fluid, even - odd, w)

        new_in, new_out = [None] * 5, [None] * 5
        new_in[0], new_out[0] = couple(W1, jx, qxx)
        new_in[1], new_out[2] = couple(W2, jx + jy, qxx + qyy + qxy)
        new_in[2], new_out[1] = couple(W2, jx - jy, qxx + qyy - qxy)
        new_in[3], new_out[4] = couple(W2, jx + jz, qxx + qzz + qxz)
        new_in[4], new_out[3] = couple(W2, jx - jz, qxx + qzz - qxz)
        flat = [
            *couple(W1, jy, qyy),
            *couple(W1, jz, qzz),
            *couple(W2, jy + jz, qyy + qzz + qyz),
            *couple(W2, jy - jz, qyy + qzz - qyz),
        ]
        new = [(0, jnp.where(fluid, W0 * base, W0))]
        new += [(INDEX[(0, cy, cz)], flat[k]) for k, (cy, cz) in enumerate(IN_PLANE)]
        new += [(pick(inward[k], p), new_in[k]) for k in range(5)]
        new += [(pick(outward[k], p), new_out[k]) for k in range(5)]
        return mass_new, new, new_out

    def close(t, p):
        def corners():
            for u in (0, 1):
                x_corner(t, p, u, (p, u)).wait_recv()

        if t == 0:
            x_code(p, p).wait_recv()
            for h in (0, 1):
                interior(0, p, h, rc[p, :, half(h)])
            corners()

            @pl.when(late & (p == sides[1]))
            def _():
                open_side(p)

            far_codes(0, p)
            for c in ORDER:
                z, h = CHUNKS[c]
                x_chunk(0, p, c, p).wait_recv()
                sources = [rx[0, p, c, k] for k in range(5)]
                lane = lax.broadcasted_iota(jnp.int32, sources[0].shape, 1)
                k, edge, u = (1, lane == 0, 0) if h == 0 else (2, lane == LANES - 1, 1)
                column = jnp.broadcast_to(rk[0, p, u][:, z : z + 1], lane.shape)
                sources[k] = jnp.where(edge, column, sources[k])
                z, lanes = rows(z), half(h)
                mass_new, new, new_out = finish(0, p, z, lanes, sources)
                code_new = code_of(flags[1, p, z, lanes], mass_new)
                for k in range(5):
                    sx[1, p, c, k] = new_out[k]
                sx[1, p, c, 5] = code_new
                code[1, p, z, lanes] = code_new
                for q, value in new:
                    pops[1, q, p, z, lanes] = value
                if c % 2 == 1:
                    fill_corner(1, p, h)
                    x_corner(1, p, h, (1 - p, 1 - h)).start()
                mass[1, p, z, lanes] = mass_new
            for c in ORDER:
                x_chunk(1, p, c, 1 - p).start()
            return
        for h in (1, 0):
            for z in (0, 1):
                x_chunk(1, p, 2 * h + z, p).wait_recv()
            interior(1, p, h, jnp.concatenate([rx[1, p, 2 * h, 5], rx[1, p, 2 * h + 1, 5]], axis=0))
        corners()
        far_codes(1, p)
        beyond = []
        for k, (cy, cz) in enumerate(OFFS):
            halves = [jnp.concatenate([rx[1, p, 2 * h, k], rx[1, p, 2 * h + 1, k]], axis=0) for h in (0, 1)]
            if cy:
                halves = shift_y(halves, cy, spread(rk[1, p, 0 if cy == 1 else 1], 0))
            if cz:
                halves = shift_z(halves, cz)
            beyond.append(halves)
        for h in (0, 1):
            lanes = half(h)
            mass_new, new, _ = finish(1, p, slice(None), lanes, [halves[h] for halves in beyond])
            mass_out[p, :, lanes] = mass_new
            for q, value in new:
                pops_out[q, p, :, lanes] = value

    for t in (0, 1):
        for u in (0, 1):
            y_tile(t, u, u).wait_recv()
        if t == 0:

            for u, answers in enumerate((answers_down, answers_up)):

                @pl.when(answers)
                def _(u=u):
                    y_tile(0, u, 1 - u).start()

        if t == 0:
            @pl.when(early & first)
            def _():
                to_relay_corner(0).start()

        stream(t)

        if t == 0:

            @pl.when(early)
            def _():
                pl.semaphore_wait(go_sem, 1)
                for i, arrival in enumerate(arrivals()):
                    arrival.wait_recv()
                    onward(i).start()

        @pl.loop(0, 2)
        def _(i, t=t):
            close(t, lax.rem(gx + 1 + i, 2))

        if t == 0:
            fill_y(1)
            for u in (0, 1):
                y_tile(1, u, 1 - u).start()

    @pl.when(early)
    def _():
        for i in range(7):
            onward(i).wait_send()

    for d in (0, 1):
        x_code(d, 1 - d).wait_send()
        for t in (0, 1):
            for c in range(4):
                x_chunk(t, d, c, 1 - d).wait_send()
            for u in (0, 1):
                x_corner(t, d, u, (1 - d, 1 - u)).wait_send()
            y_tile(t, d, 1 - d).wait_send()


def write_back(pops, mass, pops_out, mass_out, sem):
    copies = [
        pltpu.make_async_copy(pops, pops_out, sem.at[0]),
        pltpu.make_async_copy(mass, mass_out, sem.at[1]),
    ]
    for copy in copies:
        copy.start()
    for copy in copies:
        copy.wait()


def on_device(populations, mass, flags, relax):
    _, planes, depth, width = populations.shape
    tile, plane = (ROWS, LANES), (depth, width)
    f32 = jnp.float32
    vmem, dma = pltpu.VMEM, pltpu.SemaphoreType.DMA
    state_shape = (
        jax.ShapeDtypeStruct(populations.shape, f32),
        jax.ShapeDtypeStruct(mass.shape, f32),
    )
    hbm = pl.BlockSpec(memory_space=pltpu.HBM)
    here = pl.BlockSpec(memory_space=pltpu.VMEM)
    args = [pltpu.with_memory_space_constraint(a, pltpu.HBM) for a in (populations, mass, flags, relax)]
    state = pl.pallas_call(
        kernel,
        out_shape=state_shape,
        in_specs=[hbm] * 4,
        out_specs=(here, here),
        scratch_shapes=[
            vmem((2, 19, planes, *plane), f32),
            vmem((2, planes, *plane), f32),
            vmem((2, planes, *plane), jnp.int32),
            vmem((planes, *plane), f32),
            vmem((2, planes, *plane), f32),
            vmem((planes, 8, *plane), f32),
            vmem((planes, 5, *plane), f32),
            vmem((planes, 3, 3, *plane), f32),
            vmem((2, 5, *plane), f32),
            vmem((planes, 14, *plane), f32),
            vmem((2, 2, 4, 6, *tile), f32),
            vmem((2, 2, 4, 6, *tile), f32),
            vmem((2, *plane), f32),
            vmem((2, *plane), f32),
            vmem((2, 2, *tile), f32),
            vmem((2, 2, *tile), f32),
            vmem((2, 2, 2, *tile), f32),
            vmem((2, 2, 2, *tile), f32),
            vmem((4, 5, *tile), f32),
            vmem(plane, f32),
            vmem((2, *tile), f32),
            dma((4,)),
            dma((2, 2, 4)),
            dma((2, 2, 4)),
            dma((2,)),
            dma((2,)),
            dma((2, 2)),
            dma((2, 2)),
            dma((2, 2, 2)),
            dma((2, 2, 2)),
            dma((4,)),
            dma((1,)),
            dma((2,)),
            dma((7,)),
            pltpu.SemaphoreType.REGULAR,
        ],
        compiler_params=pltpu.CompilerParams(
            collective_id=0, has_side_effects=True, vmem_limit_bytes=32 * 1024 * 1024
        ),
        name="lattice_steps",
    )(*args)
    anywhere = pl.BlockSpec(memory_space=pl.ANY)
    return pl.pallas_call(
        write_back,
        out_shape=state_shape,
        in_specs=[here] * 2,
        out_specs=(anywhere,) * 2,
        scratch_shapes=[dma((2,))],
        name="write_back",
    )(*(pltpu.with_memory_space_constraint(a, pltpu.VMEM) for a in state))


def solution(mesh):
    return jax.shard_map(
        on_device,
        mesh=mesh,
        in_specs=(
            P(None, "gx", None, "gy"),
            P("gx", None, "gy"),
            P(None, "gx", None, "gy"),
            P("gx", None, "gy"),
        ),
        out_specs=(P(None, "gx", None, "gy"), P("gx", None, "gy")),
        check_vma=False,
    )
```
